32 devices in a mesh: replica: 4 (over x, core), shard: 8 (over z, y).
Axes of the slice: x: 2, y: 2, z: 4, core: 2. Of those that a mesh axis runs over, the one named last changes fastest.
Arguments:
- tokens: bfloat16 [8192, 1088], P(('replica', 'shard')), may hold values from -6 to 6
- slot: int32 [8192], P(('replica', 'shard')), may hold values from 0 to 2047, as said below
- lengths: int32 [4, 6], P('replica'), may hold values from 1 to 1024, 2048 in all within a row
- attn_in_weight: bfloat16 [1088, 3264], P('shard'), may hold values from -0.1875 to 0.1875
- attn_out_weight: bfloat16 [1088, 1088], P('shard'), may hold values from -2.5 to 2.5
- up_weight: bfloat16 [1088, 4352], P('shard'), may hold values from -0.1875 to 0.1875
- down_weight: bfloat16 [4352, 1088], P('shard'), may hold values from -0.09375 to 0.09375
- norm_gains: float32 [2, 1088], replicated, may hold values from 0.1 to 1.9
- layer_biases: float32 [6, 1088], replicated, may hold values from -0.6 to 0.6
- up_bias: float32 [4352], replicated, may hold values from -3 to 3
- cotangent: bfloat16 [8192, 1088], P(('replica', 'shard')), may hold values from -6 to 6
Outputs:
- mixed: bfloat16 [8192, 1088], P(('replica', 'shard'))
- tokens_grad: float32 [8192, 1088], P(('replica', 'shard'))
- attn_in_grad: float32 [1088, 3264], P('shard')
- attn_out_grad: float32 [1088, 1088], P('shard')
- up_grad: float32 [1088, 4352], P('shard')
- down_grad: float32 [4352, 1088], P('shard')
- gains_grad: float32 [2, 1088], P(None, 'shard')
- biases_grad: float32 [6, 1088], P(None, 'shard')
- up_bias_grad: float32 [4352], P('shard')
The draws below stay inside these ranges and needn't reach their ends.
Inputs may be any that keep to these rules, and one draw needn't show every extreme that they name: `slot`: within each group's rows (blocks of 2048 rows in order), every place 0 to 2047 occurs exactly once. Each row of lengths sums to 2048; its largest entry is 1024.
All inputs are finite; a program needn't handle non-finite values.
Results may differ from the reference program's by a relative error of at most 0.02.
Values may be sent and summed in bfloat16 or wider, within the bound.
No kernel may reach another device: no remote copies, remote signals or barrier semaphores. Data moves between devices by JAX's collectives and lax.ppermute only.
A program may use at most 256 MiB of HBM per device.

```python
import math
import jax
import jax.numpy as jnp
import numpy as np
from jax import lax

D = 1088
HEADS = 17
HEAD = 64
FF = 4352
TOK_DEV = 256
GROUP_TOK = 2048
GROUPS = 4
TOKENS = 8192
LONGEST = 1024
SEQS = 6
N_SHARD = 8


def draw_slot(key, part):
    key = jax.random.fold_in(key, 11)
    group_keys = jax.random.split(key, GROUPS)
    orders = jax.vmap(lambda one_key: jax.random.permutation(one_key, GROUP_TOK))(group_keys)
    return orders.reshape(-1).astype(jnp.int32)


def level_of(key, shape, cuts, low, largest):
    def one(dim, parts):
        heights = jax.random.uniform(jax.random.fold_in(jax.random.fold_in(key, 6), dim), (parts,), jnp.float32, low / len(cuts), largest / len(cuts))
        return jnp.repeat(jnp.exp(heights), shape[dim] // parts).reshape((-1,) + (1,) * (len(shape) - dim - 1))

    level = one(*cuts[0])
    for cut in cuts[1:]:
        level = level * one(*cut)
    return level


def length_profile(number_of, total, most, skew):
    portions = [(1 << 20) // math.isqrt(grade ** skew) + 1 for grade in range(2, number_of + 1)]
    surplus, given = total - most - (number_of - 1), [1] * (number_of - 1)
    while surplus > 0:
        movable = [i for i in range(number_of - 1) if given[i] < most]
        whole, left = sum([portions[i] for i in movable]), surplus
        for i in movable:
            more = min(most - given[i], max(1, left * portions[i] // whole), surplus)
            given[i] = given[i] + more
            surplus = surplus - more
    return np.array([most] + given)


def uneven(stream_key, number_of, total, reach, slope):
    if number_of == 2:
        one = jax.random.randint(stream_key, (), max(1, total - reach), min(reach, total - 1) + 1)
        return jnp.stack([one, total - one])
    sizes = jnp.asarray(length_profile(number_of, total, reach, slope), jnp.int32)
    twos = (number_of - 1) // 2
    source_of, sink = sizes[1:1 + 2 * twos:2], sizes[2:2 + 2 * twos:2]
    slack = jnp.minimum(source_of - 1, reach - sink)
    moved = jax.random.randint(jax.random.fold_in(stream_key, 1), (twos,), 0, 1 << 20) % (slack + 1)
    sizes = sizes.at[1:1 + 2 * twos:2].set(source_of - moved).at[2:2 + 2 * twos:2].set(sink + moved)
    return sizes[jax.random.permutation(jax.random.fold_in(stream_key, 2), number_of)]


def gaussian(key, extent, width, limit, shards=(), kind=jnp.bfloat16):
    entries = jax.random.normal(key, extent, jnp.float32) * width
    if len(shards) > 0:
        entries = level_of(key, extent, shards, -0.22, 0.18) * entries
    return jnp.clip(entries, min=-limit, max=limit).astype(kind)


def setup_inputs(seed: int = 0) -> dict:
    seeds = jax.random.split(jax.random.key(seed), 12)
    tokens = gaussian(seeds[0], (TOKENS, D), 1.0, 6.0, ((0, 32),))
    slot = draw_slot(jax.random.fold_in(seeds[11], 71), 0)
    lengths = jax.vmap(lambda own: uneven(own, SEQS, GROUP_TOK, LONGEST, 2))(jax.random.split(seeds[2], GROUPS)).reshape((GROUPS, SEQS)).astype(jnp.int32)
    attn_in_weight = gaussian(seeds[3], (D, 3 * D), D ** -0.5, 0.1875, ((0, 8),))
    attn_out_weight = gaussian(seeds[4], (D, D), (D // 256 + 1) ** -0.5, 2.5, ((0, 8),))
    up_weight = gaussian(seeds[5], (D, FF), D ** -0.5, 0.1875, ((0, 8),))
    down_weight = gaussian(seeds[6], (FF, D), FF ** -0.5, 0.09375, ((0, 8),))
    norm_gains = jnp.clip(1.0 + 0.18 * jax.random.normal(seeds[7], (2, D), jnp.float32), 0.1, 1.9)
    layer_biases = gaussian(seeds[8], (6, D), 0.1, 0.6, (), jnp.float32)
    up_bias = gaussian(seeds[9], (FF,), 0.5, 3.0, (), jnp.float32)
    cotangent = gaussian(seeds[10], (TOKENS, D), 1.0, 6.0, ((0, 32),))
    return dict(tokens=tokens, slot=slot, lengths=lengths, attn_in_weight=attn_in_weight, attn_out_weight=attn_out_weight, up_weight=up_weight, down_weight=down_weight, norm_gains=norm_gains, layer_biases=layer_biases, up_bias=up_bias, cotangent=cotangent)


@jax.custom_vjp
def low(v):
    return lax.optimization_barrier(v.astype(jnp.bfloat16)).astype(jnp.float32)

@jax.custom_vjp
def low_back(v):
    return v

def low_keep(v):
    return (low(v), None)

def low_pass(kept, grad):
    return (grad,)

def back_keep(v):
    return (v, None)

def back_low(kept, grad):
    return (low(grad),)
low.defvjp(low_keep, low_pass)
low_back.defvjp(back_keep, back_low)

def matmul_high(left, right):
    return jnp.dot(left, right, precision=lax.Precision.HIGHEST, preferred_element_type=jnp.float32)

def norm_apply(values, gain_row, bias_row):
    centre = values - lax.optimization_barrier(jnp.mean(values, axis=-1, keepdims=True))
    spread = lax.optimization_barrier(jnp.mean(centre * centre, axis=-1, keepdims=True))
    return centre * lax.rsqrt(spread + 1e-05) * gain_row + bias_row

def attend(query, keys, values, slot_row, doc_row):
    query_blocks = query.reshape(N_SHARD, TOK_DEV, HEADS, HEAD)
    slot_blocks = slot_row.reshape(N_SHARD, TOK_DEV)
    doc_blocks = doc_row.reshape(N_SHARD, TOK_DEV)

    def one_block(inputs_now):
        query_part, slot_part, doc_part = inputs_now
        scores = jnp.einsum('thd,shd->hts', query_part, keys, precision=lax.Precision.HIGHEST) * 0.125
        scores = low_back(scores)
        allowed = (doc_row[None, :] == doc_part[:, None]) & (slot_row[None, :] <= slot_part[:, None])
        scores = jnp.where(allowed[None], scores, -1e+30)
        row_max = lax.optimization_barrier(jnp.max(scores, axis=-1, keepdims=True))
        expo = jnp.exp(scores - row_max)
        prob = expo / lax.optimization_barrier(jnp.sum(expo, axis=-1, keepdims=True))
        return jnp.einsum('hts,shd->thd', low(prob), values, precision=lax.Precision.HIGHEST)
    outputs = lax.map(jax.checkpoint(one_block), (query_blocks, slot_blocks, doc_blocks))
    return outputs.reshape(GROUP_TOK, D)

def reference(tokens, slot, lengths, attn_in_weight, attn_out_weight, up_weight, down_weight, norm_gains, layer_biases, up_bias, cotangent):
    slot_groups = slot.reshape(GROUPS, GROUP_TOK)
    ends = jnp.cumsum(lengths, axis=1)
    doc_groups = lax.optimization_barrier(jnp.sum((slot_groups[:, :, None] >= ends[:, None, :]).astype(jnp.int32), axis=-1)).astype(jnp.int32)

    def forward(inputs, w_in, w_out, w_up, w_down, gains, biases, ubias):

        def group_fn(inputs_now):
            rows_in, slot_row, doc_row = inputs_now
            h_first = low(norm_apply(rows_in, gains[0], biases[0]))
            projected = matmul_high(h_first, w_in)
            query = low_back(low(projected[:, :D] + biases[1]))
            keys = low_back(low(projected[:, D:2 * D]))
            values = low_back(low(projected[:, 2 * D:] + biases[2]))
            attended = attend(query.reshape(GROUP_TOK, HEADS, HEAD), keys.reshape(GROUP_TOK, HEADS, HEAD), values.reshape(GROUP_TOK, HEADS, HEAD), slot_row, doc_row)
            attended = low_back(low(attended))
            branch = low_back(matmul_high(attended, w_out) + biases[3])
            middle = rows_in + branch
            h_second = low(norm_apply(middle, gains[1], biases[4]))
            pre = low_back(matmul_high(h_second, w_up) + ubias)
            act = low(jax.nn.gelu(pre, approximate=True))
            branch_two = low_back(matmul_high(act, w_down) + biases[5])
            return middle + branch_two
        grouped = inputs.reshape(GROUPS, GROUP_TOK, D)
        outputs = lax.map(jax.checkpoint(group_fn), (grouped, slot_groups, doc_groups))
        return outputs.reshape(TOKENS, D)
    primals = (tokens.astype(jnp.float32), attn_in_weight.astype(jnp.float32), attn_out_weight.astype(jnp.float32), up_weight.astype(jnp.float32), down_weight.astype(jnp.float32), norm_gains.astype(jnp.float32), layer_biases.astype(jnp.float32), up_bias.astype(jnp.float32))
    output, back_fn = jax.vjp(forward, *primals)
    grads = back_fn(cotangent.astype(jnp.float32))
    return (output.astype(jnp.bfloat16), grads[0], grads[1], grads[2], grads[3], grads[4], grads[5], grads[6], grads[7])
```

```python
import functools

import jax
import jax.numpy as jnp
from jax import lax
from jax.experimental import pallas as pl
from jax.experimental.pallas import tpu as pltpu
from jax.sharding import Mesh, PartitionSpec as P

HEAD = 64
BF = jnp.bfloat16
F32 = jnp.float32
REP = ("x", "core")
SHARD = ("z", "y")
NEG = -1e30


def dot(left, right):
    return jnp.dot(left, right, preferred_element_type=F32)


def dot_nt(left, right):
    return lax.dot_general(left, right, (((1,), (1,)), ((), ())), preferred_element_type=F32)


def dot_tn(left, right):
    return lax.dot_general(left, right, (((0,), (0,)), ((), ())), preferred_element_type=F32)


def iota(shape, dim):
    return lax.broadcasted_iota(jnp.int32, shape, dim)


def doc_starts(places, ends_ref):
    starts = jnp.zeros_like(places)
    for n in range(ends_ref.shape[0]):
        starts = jnp.where(places >= ends_ref[n], ends_ref[n], starts)
    return starts


def first_block(block, tile, ends_ref):
    row = block * tile
    start = jnp.int32(0)
    for n in range(ends_ref.shape[0]):
        start = jnp.where(row >= ends_ref[n], ends_ref[n], start)
    return lax.div(start, jnp.int32(tile))


def rows(block, tile):
    return pl.ds(pl.multiple_of(block * tile, tile), tile)


def only_head(values, head):
    lanes = iota(values.shape, 1)
    keep = (lanes < HEAD) if head == 0 else (lanes >= HEAD)
    return jnp.where(keep, values, jnp.zeros_like(values))


def forward_kernel(
    ends_ref, me_ref, h_ref, w_ref, b_ref, srow_ref, scol_ref, own_ref,
    sp_ref, kt_ref, o_ref, of_ref, lse_ref, q16_ref, o16_ref, lse16_ref,
    p_scr, vt_scr, ob_scr,
):
    total = h_ref.shape[0]
    tile = own_ref.shape[1]
    blocks = total // tile

    @pl.loop(0, blocks)
    def _(b):
        r = rows(b, tile)
        p_scr[r, :] = (dot(h_ref[r, :], w_ref[...]) + b_ref[...]).astype(BF)

    @pl.loop(0, blocks)
    def _(b):
        r = rows(b, tile)
        place = iota((tile, total), 0) + b * tile
        pick = jnp.where(srow_ref[...] == place, 1.0, 0.0).astype(BF)
        sorted_f = dot(pick, p_scr[:, :512])
        sp_ref[r, :] = sorted_f.astype(BF)
        kt_ref[b] = sorted_f[:, 128:256].T.astype(BF)
        vt_scr[b, :128, :] = sorted_f[:, 256:384].T.astype(BF)
        vt_scr[b, 128:, :] = sorted_f[:, 384:512].T.astype(BF)

    q16 = p_scr[rows(me_ref[0], tile), 512:640]
    q16_ref[...] = q16

    @pl.loop(0, blocks)
    def _(qb):
        q = sp_ref[rows(qb, tile), 0:128]
        qs = [only_head(q, 0), only_head(q, 1)]
        qpos = iota((1, tile), 1) + qb * tile
        qstart = doc_starts(qpos, ends_ref)
        low = first_block(qb, tile, ends_ref)

        def step(n, state):
            kb = qb - n
            k = sp_ref[rows(kb, tile), 128:256]
            kpos = iota((tile, tile), 0) + kb * tile
            ok = (kpos <= qpos) & (kpos >= qstart)
            new = []
            for head in range(2):
                m, l, acc = state[head]
                s = jnp.where(ok, dot_nt(k, qs[head]) * 0.125, NEG)
                mn = jnp.maximum(m, jnp.max(s, axis=0, keepdims=True))
                p = jnp.exp(s - mn)
                a = jnp.exp(m - mn)
                l = l * a + jnp.sum(p, axis=0, keepdims=True)
                vt = vt_scr[kb, head * HEAD:(head + 1) * HEAD, :]
                acc = acc * a + dot(vt, p.astype(BF))
                new.append((mn, l, acc))
            return tuple(new)

        start = (jnp.full((1, tile), NEG, F32), jnp.zeros((1, tile), F32), jnp.zeros((HEAD, tile), F32))
        state = lax.fori_loop(0, qb - low + 1, step, (start, start))
        out = jnp.concatenate([state[0][2] / state[0][1], state[1][2] / state[1][1]], axis=0).T
        of_ref[rows(qb, tile), :] = out
        ob_scr[rows(qb, tile), :] = out.astype(BF)
        lse_ref[qb] = jnp.concatenate([s[0] + jnp.log(s[1]) for s in state], axis=0)

    own = own_ref[...]
    own_start = doc_starts(own, ends_ref)

    def step16(kb, state):
        m, l, acc = state
        kv = sp_ref[rows(kb, tile), 384:512]
        kpos = iota((tile, tile), 0) + kb * tile
        ok = (kpos <= own) & (kpos >= own_start)
        s = jnp.where(ok, dot_nt(kv, q16) * 0.125, NEG)
        mn = jnp.maximum(m, jnp.max(s, axis=0, keepdims=True))
        p = jnp.where(ok, jnp.exp(s - mn), 0.0)
        a = jnp.exp(m - mn)
        l = l * a + jnp.sum(p, axis=0, keepdims=True)
        acc = acc * a + dot(vt_scr[kb, 192:256, :], p.astype(BF))
        return mn, l, acc

    start = (jnp.full((1, tile), NEG, F32), jnp.zeros((1, tile), F32), jnp.zeros((HEAD, tile), F32))
    m, l, acc = lax.fori_loop(0, blocks, step16, start)
    o16_ref[...] = jnp.concatenate([jnp.zeros_like(acc), acc / l], axis=0).T
    lse16_ref[...] = m + jnp.log(l)

    @pl.loop(0, blocks)
    def _(b):
        r = rows(b, tile)
        pick = jnp.where(scol_ref[r, :] == iota((tile, total), 1), 1.0, 0.0).astype(BF)
        o_ref[r, :] = dot(pick, ob_scr[...]).astype(BF)


def backward_kernel(
    ends_ref, srow_ref, scol_ref, own_ref, sp_ref, kt_ref, of_ref, lse_ref,
    do_ref, q16_ref, do16_ref, o16_ref, lse16_ref,
    dp_ref, dq16_ref,
    dos_scr, acc_scr, acc16_scr, dps_scr,
):
    total = sp_ref.shape[0]
    tile = own_ref.shape[1]
    blocks = total // tile

    @pl.loop(0, blocks)
    def _(b):
        r = rows(b, tile)
        place = iota((tile, total), 0) + b * tile
        pick = jnp.where(srow_ref[...] == place, 1.0, 0.0).astype(BF)
        dos_scr[r, :] = dot(pick, do_ref[...]).astype(BF)
        acc_scr[r, :] = jnp.zeros((tile, 256), F32)

    @pl.loop(0, blocks)
    def _(qb):
        qr = rows(qb, tile)
        q = sp_ref[qr, 0:128]
        do = dos_scr[qr, :]
        qs = [only_head(q, 0), only_head(q, 1)]
        ds_ = [only_head(do, 0), only_head(do, 1)]
        q_two = jnp.concatenate(qs, axis=0)
        do_two = jnp.concatenate(ds_, axis=0)
        prod = (do.astype(F32) * of_ref[qr, :]).T
        delta = [jnp.sum(prod[:HEAD], axis=0, keepdims=True), jnp.sum(prod[HEAD:], axis=0, keepdims=True)]
        lse = lse_ref[qb]
        qpos = iota((1, tile), 1) + qb * tile
        qstart = doc_starts(qpos, ends_ref)
        low = first_block(qb, tile, ends_ref)

        def step(kb, dqt):
            kr = rows(kb, tile)
            k = sp_ref[kr, 128:256]
            v = sp_ref[kr, 256:384]
            kpos = iota((tile, tile), 0) + kb * tile
            ok = (kpos <= qpos) & (kpos >= qstart)
            ps, dss, new = [], [], []
            for head in range(2):
                s = dot_nt(k, qs[head]) * 0.125 - lse[head:head + 1]
                p = jnp.where(ok, jnp.exp(s), 0.0)
                dprob = dot_nt(v, ds_[head])
                ds = (p * (dprob - delta[head])).astype(BF)
                ps.append(p.astype(BF))
                dss.append(ds)
                new.append(dqt[head] + dot(kt_ref[kb, head * HEAD:(head + 1) * HEAD, :], ds))
            acc_scr[kr, 0:128] += dot(jnp.concatenate(dss, axis=1), q_two)
            acc_scr[kr, 128:256] += dot(jnp.concatenate(ps, axis=1), do_two)
            return tuple(new)

        zero = jnp.zeros((HEAD, tile), F32)
        dqt = lax.fori_loop(low, qb + 1, step, (zero, zero))
        dps_scr[qr, 0:128] = (jnp.concatenate(dqt, axis=0).T * 0.125).astype(BF)

    own = own_ref[...]
    own_start = doc_starts(own, ends_ref)
    q16 = q16_ref[...]
    do16 = do16_ref[...]
    both = jnp.concatenate([q16, do16], axis=0)
    delta16 = jnp.sum((do16.astype(F32) * o16_ref[...]).T, axis=0, keepdims=True)
    lse16 = lse16_ref[...]

    def step16(kb, dq):
        kr = rows(kb, tile)
        kv = sp_ref[kr, 384:512]
        kpos = iota((tile, tile), 0) + kb * tile
        ok = (kpos <= own) & (kpos >= own_start)
        p = jnp.where(ok, jnp.exp(dot_nt(kv, q16) * 0.125 - lse16), 0.0)
        ds = (p * (dot_nt(kv, do16) - delta16)).astype(BF)
        acc16_scr[kr, :] = dot(jnp.concatenate([ds, p.astype(BF)], axis=1), both)
        return dq + dot_tn(ds, kv)

    dq16 = lax.fori_loop(0, blocks, step16, jnp.zeros((tile, 128), F32))
    dq16_ref[...] = (dq16 * 0.125).astype(BF)

    @pl.loop(0, blocks)
    def _(b):
        r = rows(b, tile)
        dps_scr[r, 128:256] = (acc_scr[r, 0:128] * 0.125).astype(BF)
        dps_scr[r, 256:384] = acc_scr[r, 128:256].astype(BF)
        part = acc16_scr[r, :]
        dps_scr[r, 384:512] = jnp.where(iota(part.shape, 1) < HEAD, part * 0.125, part).astype(BF)

    @pl.loop(0, blocks)
    def _(b):
        r = rows(b, tile)
        pick = jnp.where(scol_ref[r, :] == iota((tile, total), 1), 1.0, 0.0).astype(BF)
        dp_ref[r, :] = dot(pick, dps_scr[...]).astype(BF)


VM = pl.BlockSpec(memory_space=pltpu.VMEM)
SM = pl.BlockSpec(memory_space=pltpu.SMEM)


def attention_forward(ends, me, h_all, w_own, b_own, slots_all, slot):
    total, tile = h_all.shape[0], slot.shape[0]
    blocks = total // tile
    shapes = (
        jax.ShapeDtypeStruct((total, 512), BF),
        jax.ShapeDtypeStruct((blocks, 128, tile), BF),
        jax.ShapeDtypeStruct((total, 128), BF),
        jax.ShapeDtypeStruct((total, 128), F32),
        jax.ShapeDtypeStruct((blocks, 2, tile), F32),
        jax.ShapeDtypeStruct((tile, 128), BF),
        jax.ShapeDtypeStruct((tile, 128), F32),
        jax.ShapeDtypeStruct((1, tile), F32),
    )
    return pl.pallas_call(
        forward_kernel,
        out_shape=shapes,
        in_specs=[SM, SM] + [VM] * 6,
        out_specs=[VM] * len(shapes),
        scratch_shapes=[
            pltpu.VMEM((total, 640), BF),
            pltpu.VMEM((blocks, 256, tile), BF),
            pltpu.VMEM((total, 128), BF),
        ],
        compiler_params=pltpu.CompilerParams(vmem_limit_bytes=40 * 2**20),
        cost_estimate=pl.CostEstimate(flops=14_000_000_000, bytes_accessed=12_000_000, transcendentals=6_000_000),
    )(ends, me, h_all, w_own, b_own, slots_all.reshape(1, total), slots_all.reshape(total, 1), slot.reshape(1, tile))


def attention_backward(ends, slots_all, slot, saved, do, do16):
    sp, kt, of, lse, q16, o16, lse16 = saved
    total, tile = sp.shape[0], slot.shape[0]
    shapes = (jax.ShapeDtypeStruct((total, 512), BF), jax.ShapeDtypeStruct((tile, 128), BF))
    return pl.pallas_call(
        backward_kernel,
        out_shape=shapes,
        in_specs=[SM] + [VM] * 12,
        out_specs=[VM] * len(shapes),
        scratch_shapes=[
            pltpu.VMEM((total, 128), BF),
            pltpu.VMEM((total, 256), F32),
            pltpu.VMEM((total, 128), F32),
            pltpu.VMEM((total, 512), BF),
        ],
        compiler_params=pltpu.CompilerParams(vmem_limit_bytes=40 * 2**20),
        cost_estimate=pl.CostEstimate(flops=20_000_000_000, bytes_accessed=12_000_000, transcendentals=6_000_000),
    )(
        ends, slots_all.reshape(1, total), slots_all.reshape(total, 1), slot.reshape(1, tile),
        sp, kt, of, lse, do, q16, do16, o16, lse16,
    )


def swap(values, axis):
    return lax.ppermute(values, axis, [(0, 1), (1, 0)])


def gather_rep(values):
    other = swap(values, "x")
    pair = jnp.concatenate([values, other], axis=0)
    return jnp.concatenate([pair, swap(pair, "core")], axis=0)


def scatter_rep(parts):
    half = parts.shape[0] // 2
    pair = parts[:half] + swap(parts[half:].astype(BF), "core").astype(F32)
    quarter = half // 2
    return pair[:quarter] + swap(pair[quarter:].astype(BF), "x").astype(F32)


def in_order(mine, other, axis):
    first = lax.axis_index(axis) == 0
    return jnp.where(first, mine, other), jnp.where(first, other, mine)


def ordered_rep(values):
    pair = jnp.stack(in_order(values, swap(values, "x"), "x"))
    first, second = in_order(pair, swap(pair, "core"), "core")
    return jnp.stack([first, second])


def split_rep(values):
    half = values.shape[1] // 2
    keep, send = in_order(values[:, :half], values[:, half:], "core")
    kept = keep + swap(send.astype(BF), "core").astype(F32)
    half = half // 2
    keep, send = in_order(kept[:, :half], kept[:, half:], "x")
    return keep + swap(send.astype(BF), "x").astype(F32)


def sum_rep(values):
    for axis in ("core", "x"):
        low = values.astype(BF)
        values = low.astype(F32) + swap(low, axis).astype(F32)
    return values


def sum_all(values):
    z_size = lax.axis_size("z")
    for axis in ("core", "x", "y"):
        values = values + swap(values, axis)
    step = 1
    while step < z_size:
        values = values + lax.ppermute(values, "z", [(n, n ^ step) for n in range(z_size)])
        step = step * 2
    return sum_dp(values)


def sum_dp(values):
    if lax.axis_size("dp") > 1:
        return lax.psum(values, "dp")
    return values


def gather_shard(values):
    return lax.all_gather(values, SHARD, axis=0, tiled=True)


def scatter_shard(values):
    return lax.psum_scatter(values.astype(BF), SHARD, scatter_dimension=0, tiled=True)


def exchange_shard(values):
    return lax.all_to_all(values, SHARD, 0, 0, tiled=True)


def norm_stats(values):
    centre = values - jnp.mean(values, axis=-1, keepdims=True)
    spread = jnp.mean(centre * centre, axis=-1, keepdims=True)
    rate = lax.rsqrt(spread + 1e-05)
    return centre * rate, rate


def norm_back(grad, normed, rate, gain):
    scaled = grad * gain
    inner = jnp.mean(scaled * normed, axis=-1, keepdims=True)
    back = rate * (scaled - jnp.mean(scaled, axis=-1, keepdims=True) - normed * inner)
    return back, jnp.sum(grad * normed, axis=0), jnp.sum(grad, axis=0)


def gelu_tanh(values):
    return jax.nn.gelu(values, approximate=True)


def shards(
    tokens, slot, lengths, attn_in_weight, attn_out_weight, up_weight, down_weight,
    norm_gains, layer_biases, up_bias, cotangent,
):
    tile, feats = tokens.shape
    n_shard = lax.axis_size("z") * lax.axis_size("y")
    heads = feats // HEAD
    per = heads // n_shard
    mine = per * HEAD
    spare = n_shard * mine
    me = lax.axis_index("z") * lax.axis_size("y") + lax.axis_index("y")
    rep = lax.axis_index("x") * 2 + lax.axis_index("core")
    row_part = attn_in_weight.shape[0]
    ff_part = down_weight.shape[0]
    n_rep = 4
    quarter = ff_part // n_rep

    in_parts = attn_in_weight.reshape(row_part, 3, feats)
    main = in_parts[:, :, :spare].reshape(row_part, 3, n_shard, mine).transpose(2, 0, 1, 3)
    main = main.reshape(n_shard, row_part, 3 * mine)
    extra = jnp.concatenate([in_parts[:, 1, spare:], in_parts[:, 2, spare:], in_parts[:, 0, spare:]], axis=1)
    extra = jnp.broadcast_to(extra[None], (n_shard,) + extra.shape)
    w_own = exchange_shard(jnp.concatenate([main, extra], axis=2)).reshape(feats, -1)
    w_pad = jnp.pad(w_own, ((0, 0), (0, 640 - w_own.shape[1])))

    ends = jnp.cumsum(lengths[0]).astype(jnp.int32)
    slots_all = gather_shard(slot)

    tokens_f = tokens.astype(F32)
    normed1, rate1 = norm_stats(tokens_f)
    h_first = (normed1 * norm_gains[0] + layer_biases[0]).astype(BF)
    h_all = gather_shard(h_first)

    up_mine = lax.dynamic_index_in_dim(
        up_weight.reshape(row_part, n_shard, n_rep, quarter), rep, 2, keepdims=False
    ).reshape(row_part, n_shard * quarter)
    down_mine = lax.dynamic_slice_in_dim(down_weight, rep * quarter, quarter, 0)
    w_out = gather_shard(attn_out_weight)
    w_ff = gather_shard(jnp.concatenate([up_mine, down_mine], axis=1))
    w_up, w_down = w_ff[:, : n_shard * quarter], w_ff[:, n_shard * quarter :]
    up_bias_mine = lax.dynamic_index_in_dim(
        up_bias.reshape(n_shard, n_rep, quarter), rep, 1, keepdims=False
    ).reshape(-1)

    query_bias = lax.dynamic_slice_in_dim(layer_biases[1], me * mine, mine)
    value_bias = lax.dynamic_slice_in_dim(layer_biases[2], me * mine, mine)
    zeros = functools.partial(jnp.zeros, dtype=F32)
    b_own = jnp.concatenate(
        [query_bias, zeros(mine), value_bias, zeros(HEAD), layer_biases[2, spare:], layer_biases[1, spare:], zeros(HEAD)]
    )[None]

    sp, kt, o_own, of, lse, q16, o16, lse16 = attention_forward(
        ends, me.reshape(1).astype(jnp.int32), h_all, w_pad, b_own, slots_all, slot
    )
    o_back = exchange_shard(o_own.reshape(n_shard, tile, mine))
    attended = jnp.concatenate(
        [o_back.transpose(1, 0, 2).reshape(tile, spare), o16[:, HEAD:].astype(BF)], axis=1
    )
    middle = tokens_f + dot(attended, w_out) + layer_biases[3]
    normed2, rate2 = norm_stats(middle)
    h_second = (normed2 * norm_gains[1] + layer_biases[4]).astype(BF)

    dout_rep = gather_rep(cotangent)
    h_rep = gather_rep(h_second)
    pre = dot(h_rep, w_up) + up_bias_mine
    act_f, gelu_back = jax.vjp(gelu_tanh, pre)
    act = act_f.astype(BF)
    mixed = (middle + scatter_rep(dot(act, w_down)) + layer_biases[5]).astype(BF)

    dpre = gelu_back(dot_nt(dout_rep, w_down))[0].astype(BF)
    dh_second = scatter_rep(dot_nt(dpre, w_up))
    down_grad = dot_tn(act, dout_rep)
    up_grad = dot_tn(h_rep, dpre)
    up_bias_grad = jnp.sum(dpre.astype(F32), axis=0)

    dout = cotangent.astype(F32)
    norm_grad, gain_two, bias_two = norm_back(dh_second, normed2, rate2, norm_gains[1])
    dmiddle = dout + norm_grad
    dbranch = dmiddle.astype(BF)
    dattended = dot_nt(dbranch, w_out).astype(BF)
    out_grad = split_rep(dot_tn(attended, dbranch))
    owned = scatter_shard(jnp.concatenate([up_grad, down_grad, out_grad], axis=1))

    do_own = exchange_shard(dattended[:, :spare].reshape(tile, n_shard, mine).transpose(1, 0, 2))
    do16 = jnp.pad(dattended[:, spare:], ((0, 0), (HEAD, 0)))
    dp, dq16 = attention_backward(
        ends, slots_all, slot, (sp, kt, of, lse, q16, o16, lse16), do_own.reshape(-1, mine), do16
    )
    dq16 = dq16[:, :HEAD]
    dh_first = scatter_shard(dot_nt(dp, w_own[:, :512])).astype(F32) + dot_nt(dq16, w_own[:, 512:])
    in_grad = jnp.concatenate([dot_tn(h_all, dp), dot_tn(h_first, dq16)], axis=1).astype(BF)
    in_back = exchange_shard(in_grad.reshape(n_shard, row_part, -1))
    norm_grad, gain_one, bias_one = norm_back(dh_first, normed1, rate1, norm_gains[0])
    tokens_grad = dmiddle + norm_grad

    in_main = in_back[:, :, : 3 * mine].reshape(n_shard, row_part, 3, mine).transpose(1, 2, 0, 3)
    in_main = in_main.reshape(row_part, 3, spare)
    in_extra = jnp.sum(in_back[:, :, 3 * mine :].astype(F32), axis=0).astype(BF)
    key16, value16, query16 = jnp.split(in_extra, 3, axis=1)
    in_rows = jnp.concatenate([in_main, jnp.stack([query16, key16, value16], axis=1)], axis=2)
    in_out = sum_dp(sum_rep(in_rows.reshape(row_part, 3 * feats)))

    owned = sum_dp(owned)
    whole = ordered_rep(owned)
    wide = n_shard * quarter
    up_out = whole[..., :wide].reshape(2, 2, row_part, n_shard, quarter).transpose(2, 3, 1, 0, 4)
    up_out = up_out.reshape(row_part, -1).astype(F32)
    down_out = whole[..., wide : 2 * wide].transpose(1, 0, 2, 3).reshape(ff_part, feats).astype(F32)
    out_out = whole[..., 2 * wide :].transpose(2, 0, 1, 3).reshape(row_part, feats).astype(F32)

    dp_sums = jnp.sum(dp.astype(F32), axis=0)
    query_sums = lax.dynamic_update_slice(zeros(feats), dp_sums[:mine], (me * mine,))
    query_sums = query_sums + jnp.pad(jnp.sum(dq16.astype(F32), axis=0), (spare, 0))
    value_sums = lax.dynamic_update_slice(zeros(feats), dp_sums[2 * mine : 3 * mine], (me * mine,))
    value_sums = value_sums + jnp.pad(dp_sums[3 * mine + HEAD : 3 * mine + 2 * HEAD], (spare, 0))
    place = (jnp.arange(n_rep) == rep)[:, None]
    vectors = jnp.concatenate(
        [
            jnp.stack(
                [
                    bias_one, query_sums, value_sums, jnp.sum(dbranch.astype(F32), axis=0),
                    bias_two, jnp.sum(dout, axis=0), gain_one, gain_two,
                ]
            ),
            jnp.where(place, up_bias_grad[None], 0.0),
        ]
    )
    vectors = lax.dynamic_slice_in_dim(sum_all(vectors), me * row_part, row_part, 1)
    return (
        mixed, tokens_grad, in_out, out_out, up_out, down_out,
        vectors[6:8], vectors[0:6], vectors[8:].reshape(-1),
    )


def solution(mesh):
    replicas, n_shard = mesh.shape["replica"], mesh.shape["shard"]
    fine = Mesh(
        mesh.devices.reshape(replicas // 4, 2, 2, n_shard // 2, 2), ("dp", "x", "core", "z", "y")
    )
    rep = ("dp", "x", "core")
    both = rep + SHARD
    in_specs = (
        P(both, None), P(both), P(rep, None), P(SHARD, None), P(SHARD, None), P(SHARD, None), P(SHARD, None),
        P(), P(), P(), P(both, None),
    )
    out_specs = (
        P(both, None), P(both, None), P(SHARD, None), P(SHARD, None), P(SHARD, None), P(SHARD, None),
        P(None, SHARD), P(None, SHARD), P(SHARD),
    )
    return jax.shard_map(shards, mesh=fine, in_specs=in_specs, out_specs=out_specs, check_vma=False)
```

```python
import functools
import math

import jax
import jax.numpy as jnp
from jax import lax
from jax.experimental import pallas as pl
from jax.experimental.pallas import tpu as pltpu
from jax.sharding import Mesh, PartitionSpec as P

HEAD = 64
BF = jnp.bfloat16
F32 = jnp.float32
REP = ("x", "core")
SHARD = ("z", "y")
NEG = -1e30
GATHER_ROUND = 2


def dot(left, right):
    return jnp.dot(left, right, preferred_element_type=F32)


def dot_nt(left, right):
    return lax.dot_general(left, right, (((1,), (1,)), ((), ())), preferred_element_type=F32)


def dot_tn(left, right):
    return lax.dot_general(left, right, (((0,), (0,)), ((), ())), preferred_element_type=F32)


def iota(shape, dim):
    return lax.broadcasted_iota(jnp.int32, shape, dim)


def doc_starts(places, ends_ref):
    starts = jnp.zeros_like(places)
    for n in range(ends_ref.shape[0]):
        starts = jnp.where(places >= ends_ref[n], ends_ref[n], starts)
    return starts


def first_block(block, tile, ends_ref):
    row = block * tile
    start = jnp.int32(0)
    for n in range(ends_ref.shape[0]):
        start = jnp.where(row >= ends_ref[n], ends_ref[n], start)
    return lax.div(start, jnp.int32(tile))


def rows(block, tile):
    return pl.ds(pl.multiple_of(block * tile, tile), tile)


def only_head(values, head):
    lanes = iota(values.shape, 1)
    keep = (lanes < HEAD) if head == 0 else (lanes >= HEAD)
    return jnp.where(keep, values, jnp.zeros_like(values))


def tail_slots(tail):
    lanes = iota(tail.shape, 1)
    spare = tail.shape[1] // 2
    weight = jnp.where(lanes == spare, 64.0, jnp.where(lanes == spare + 1, 1.0, 0.0))
    return tail.astype(F32) * weight


def forward_kernel(blocks, ends_ref, spot_ref, *refs):
    h_refs, refs = refs[:blocks], refs[blocks:]
    (
        wa_ref, wb_ref, bias_ref, own_ref,
        sp_ref, kt_ref, o_ref, of_ref, lse_ref, q16_ref, o16_ref, lse16_ref, w_ref, srow_ref, scol_ref,
        p_scr, vt_scr, ob_scr, row_scr,
    ) = refs
    tile = own_ref.shape[1]
    total = blocks * tile
    feats = wa_ref.shape[1]
    wide = in_width(feats, blocks)
    z, y, corner = spot_ref[0], spot_ref[1], spot_ref[2]
    zs = blocks // 2

    w_ref[...] = jnp.zeros_like(w_ref)
    for c in range(4):
        @pl.when(corner == c)
        def _(c=c):
            for n, (ref, at) in enumerate(((wa_ref, 0), (wa_ref, 1), (wb_ref, 0), (wb_ref, 1))):
                place = c ^ n
                w_ref[:feats, place * wide:(place + 1) * wide] = ref[at, :, :wide]

    me = z * 2 + y
    lanes = pl.ds(pl.multiple_of(me * 128, 128), 128)
    blank = jnp.zeros((1, 128), F32)
    last = bias_ref.shape[1] - HEAD
    bias = jnp.concatenate(
        [
            bias_ref[1:2, lanes], blank, bias_ref[2:3, lanes],
            blank[:, :HEAD], bias_ref[2:3, last:], bias_ref[1:2, last:], blank[:, :HEAD],
        ],
        axis=1,
    )
    for b in range(blocks):
        r = slice(b * tile, (b + 1) * tile)
        p_scr[r, :] = (dot(h_refs[b][...], w_ref[...]) + bias).astype(BF)
        tail = tail_slots(h_refs[b][:, h_refs[b].shape[1] - 128:])
        scol_ref[r, :] = jnp.sum(tail, axis=1, keepdims=True).astype(jnp.int32)
        row = jnp.sum(tail.T, axis=0, keepdims=True).astype(jnp.int32)
        row_scr[:, r] = row
        shard = lax.rem(z + zs - b // 2, zs) * 2 + lax.rem(y + b % 2, 2)
        srow_ref[shard] = row

    @pl.loop(0, blocks)
    def _(b):
        r = rows(b, tile)
        place = iota((tile, total), 0) + b * tile
        pick = jnp.where(row_scr[...] == place, 1.0, 0.0).astype(BF)
        sorted_f = dot(pick, p_scr[:, :512])
        sp_ref[r, :] = sorted_f.astype(BF)
        kt_ref[b] = sorted_f[:, 128:256].T.astype(BF)
        vt_scr[b, :128, :] = sorted_f[:, 256:384].T.astype(BF)
        vt_scr[b, 128:, :] = sorted_f[:, 384:512].T.astype(BF)

    q16 = p_scr[0:tile, 512:640]
    q16_ref[...] = q16

    @pl.loop(0, blocks)
    def _(qb):
        q = sp_ref[rows(qb, tile), 0:128]
        qs = [only_head(q, 0), only_head(q, 1)]
        qpos = iota((1, tile), 1) + qb * tile
        qstart = doc_starts(qpos, ends_ref)
        low = first_block(qb, tile, ends_ref)

        def step(n, state):
            kb = qb - n
            k = sp_ref[rows(kb, tile), 128:256]
            kpos = iota((tile, tile), 0) + kb * tile
            ok = (kpos <= qpos) & (kpos >= qstart)
            new = []
            for head in range(2):
                m, l, acc = state[head]
                s = jnp.where(ok, dot_nt(k, qs[head]) * 0.125, NEG)
                mn = jnp.maximum(m, jnp.max(s, axis=0, keepdims=True))
                p = jnp.exp(s - mn)
                a = jnp.exp(m - mn)
                l = l * a + jnp.sum(p, axis=0, keepdims=True)
                vt = vt_scr[kb, head * HEAD:(head + 1) * HEAD, :]
                acc = acc * a + dot(vt, p.astype(BF))
                new.append((mn, l, acc))
            return tuple(new)

        start = (jnp.full((1, tile), NEG, F32), jnp.zeros((1, tile), F32), jnp.zeros((HEAD, tile), F32))
        state = lax.fori_loop(0, qb - low + 1, step, (start, start))
        out = jnp.concatenate([state[0][2] / state[0][1], state[1][2] / state[1][1]], axis=0).T
        of_ref[rows(qb, tile), :] = out
        ob_scr[rows(qb, tile), :] = out.astype(BF)
        lse_ref[qb] = jnp.concatenate([s[0] + jnp.log(s[1]) for s in state], axis=0)

    own = own_ref[...]
    own_start = doc_starts(own, ends_ref)

    def step16(kb, state):
        m, l, acc = state
        kv = sp_ref[rows(kb, tile), 384:512]
        kpos = iota((tile, tile), 0) + kb * tile
        ok = (kpos <= own) & (kpos >= own_start)
        s = jnp.where(ok, dot_nt(kv, q16) * 0.125, NEG)
        mn = jnp.maximum(m, jnp.max(s, axis=0, keepdims=True))
        p = jnp.where(ok, jnp.exp(s - mn), 0.0)
        a = jnp.exp(m - mn)
        l = l * a + jnp.sum(p, axis=0, keepdims=True)
        acc = acc * a + dot(vt_scr[kb, 192:256, :], p.astype(BF))
        return mn, l, acc

    start = (jnp.full((1, tile), NEG, F32), jnp.zeros((1, tile), F32), jnp.zeros((HEAD, tile), F32))
    m, l, acc = lax.fori_loop(0, blocks, step16, start)
    o16_ref[...] = jnp.concatenate([jnp.zeros_like(acc), acc / l], axis=0).T
    lse16_ref[...] = m + jnp.log(l)

    for b in range(blocks):
        pick = jnp.where(scol_ref[b * tile:(b + 1) * tile, :] == iota((tile, total), 1), 1.0, 0.0).astype(BF)
        shard = lax.rem(z + zs - b // 2, zs) * 2 + lax.rem(y + b % 2, 2)
        o_ref[shard] = dot(pick, ob_scr[...]).astype(BF)


def backward_kernel(
    ends_ref, w_ref, srow_ref, scol_ref, own_ref, sp_ref, kt_ref, of_ref, lse_ref,
    do_ref, q16_ref, do16_ref, o16_ref, lse16_ref,
    dp_ref, dq16_ref, *refs,
):
    total = sp_ref.shape[0]
    tile = own_ref.shape[1]
    blocks = total // tile
    dh_refs, (dos_scr, acc_scr, acc16_scr, dps_scr) = refs[:blocks], refs[blocks:]

    places = jnp.concatenate([srow_ref[b] for b in range(blocks)], axis=1)

    @pl.loop(0, blocks)
    def _(b):
        r = rows(b, tile)
        pick = jnp.where(places == iota((tile, total), 0) + b * tile, 1.0, 0.0).astype(BF)
        dos_scr[r, :] = dot(pick, do_ref[...]).astype(BF)
        acc_scr[r, :] = jnp.zeros((tile, 256), F32)

    @pl.loop(0, blocks)
    def _(qb):
        qr = rows(qb, tile)
        q = sp_ref[qr, 0:128]
        do = dos_scr[qr, :]
        qs = [only_head(q, 0), only_head(q, 1)]
        ds_ = [only_head(do, 0), only_head(do, 1)]
        q_two = jnp.concatenate(qs, axis=0)
        do_two = jnp.concatenate(ds_, axis=0)
        prod = (do.astype(F32) * of_ref[qr, :]).T
        delta = [jnp.sum(prod[:HEAD], axis=0, keepdims=True), jnp.sum(prod[HEAD:], axis=0, keepdims=True)]
        lse = lse_ref[qb]
        qpos = iota((1, tile), 1) + qb * tile
        qstart = doc_starts(qpos, ends_ref)
        low = first_block(qb, tile, ends_ref)

        def step(kb, dqt):
            kr = rows(kb, tile)
            k = sp_ref[kr, 128:256]
            v = sp_ref[kr, 256:384]
            kpos = iota((tile, tile), 0) + kb * tile
            ok = (kpos <= qpos) & (kpos >= qstart)
            ps, dss, new = [], [], []
            for head in range(2):
                s = dot_nt(k, qs[head]) * 0.125 - lse[head:head + 1]
                p = jnp.where(ok, jnp.exp(s), 0.0)
                dprob = dot_nt(v, ds_[head])
                ds = (p * (dprob - delta[head])).astype(BF)
                ps.append(p.astype(BF))
                dss.append(ds)
                new.append(dqt[head] + dot(kt_ref[kb, head * HEAD:(head + 1) * HEAD, :], ds))
            acc_scr[kr, 0:128] += dot(jnp.concatenate(dss, axis=1), q_two)
            acc_scr[kr, 128:256] += dot(jnp.concatenate(ps, axis=1), do_two)
            return tuple(new)

        zero = jnp.zeros((HEAD, tile), F32)
        dqt = lax.fori_loop(low, qb + 1, step, (zero, zero))
        dps_scr[qr, 0:128] = (jnp.concatenate(dqt, axis=0).T * 0.125).astype(BF)

    own = own_ref[...]
    own_start = doc_starts(own, ends_ref)
    q16 = q16_ref[...]
    do16 = do16_ref[...]
    both = jnp.concatenate([q16, do16], axis=0)
    delta16 = jnp.sum((do16.astype(F32) * o16_ref[...]).T, axis=0, keepdims=True)
    lse16 = lse16_ref[...]

    def step16(kb, dq):
        kr = rows(kb, tile)
        kv = sp_ref[kr, 384:512]
        kpos = iota((tile, tile), 0) + kb * tile
        ok = (kpos <= own) & (kpos >= own_start)
        p = jnp.where(ok, jnp.exp(dot_nt(kv, q16) * 0.125 - lse16), 0.0)
        ds = (p * (dot_nt(kv, do16) - delta16)).astype(BF)
        acc16_scr[kr, :] = dot(jnp.concatenate([ds, p.astype(BF)], axis=1), both)
        return dq + dot_tn(ds, kv)

    dq16 = lax.fori_loop(0, blocks, step16, jnp.zeros((tile, 128), F32))
    dq16 = (dq16 * 0.125).astype(BF)
    dq16_ref[...] = dq16

    @pl.loop(0, blocks)
    def _(b):
        r = rows(b, tile)
        dps_scr[r, 128:256] = (acc_scr[r, 0:128] * 0.125).astype(BF)
        dps_scr[r, 256:384] = acc_scr[r, 128:256].astype(BF)
        part = acc16_scr[r, :]
        dps_scr[r, 384:512] = jnp.where(iota(part.shape, 1) < HEAD, part * 0.125, part).astype(BF)

    for b in range(blocks):
        r = slice(b * tile, (b + 1) * tile)
        pick = jnp.where(scol_ref[r, :] == iota((tile, total), 1), 1.0, 0.0).astype(BF)
        dp = dot(pick, dps_scr[...]).astype(BF)
        dp_ref[r, :] = dp
        dh = dot_nt(dp, w_ref[:, :512])
        if b == 0:
            dh = dh + dot_nt(only_head(dq16, 0), w_ref[:, 512:640])
        dh_refs[b][...] = dh[:, :dh_refs[b].shape[1]].astype(BF)


def norm_stats(values):
    centre = values - jnp.mean(values, axis=-1, keepdims=True)
    spread = jnp.mean(centre * centre, axis=-1, keepdims=True)
    rate = lax.rsqrt(spread + 1e-05)
    return centre * rate, rate


def norm_back(grad, normed, rate, gain):
    scaled = grad * gain
    inner = jnp.mean(scaled * normed, axis=-1, keepdims=True)
    back = rate * (scaled - jnp.mean(scaled, axis=-1, keepdims=True) - normed * inner)
    return back, jnp.sum(grad * normed, axis=0, keepdims=True), jnp.sum(grad, axis=0, keepdims=True)


def put(ref, values):
    width = values.shape[1]
    ref[:, :width] = values
    ref[:, width:] = jnp.zeros((ref.shape[0], ref.shape[1] - width), ref.dtype)


def first_norm_kernel(tok_ref, slot_ref, gain_ref, bias_ref, h_ref):
    tile, feats = tok_ref.shape
    normed, _ = norm_stats(tok_ref[...].astype(F32))
    h_ref[:, :feats] = (normed * gain_ref[0:1] + bias_ref[0:1]).astype(BF)
    width = h_ref.shape[1] - feats
    slot = slot_ref[...]
    high = lax.shift_right_logical(slot, 6)
    lanes = iota((tile, width), 1)
    pair = jnp.where(lanes == 0, high, jnp.where(lanes == 1, slot - high * 64, 0))
    h_ref[:, feats:] = pair.astype(F32).astype(BF)


def slab(feats, n_shard, shard):
    mine = feats // HEAD // n_shard * HEAD
    spare = n_shard * mine
    left = feats - spare
    return [
        (shard * mine, mine), (feats + shard * mine, mine), (2 * feats + shard * mine, mine),
        (feats + spare, left), (2 * feats + spare, left), (spare, left),
    ]


def slab_part(feats, n_shard, shard, low, high):
    found, at = [], 0
    for start, width in slab(feats, n_shard, shard):
        first, end = max(at, low), min(at + width, high)
        if first < end:
            found.append((start + first - at, end - first, first - low))
        at = at + width
    return found


def in_width(feats, n_shard):
    return sum(width for _, width in slab(feats, n_shard, 0)) // 4


def pack_in_kernel(spot_ref, w_ref, out_w_ref, out_ref):
    feats = w_ref.shape[1] // 3
    n_shard = out_ref.shape[0]
    wide, out_wide = in_width(feats, n_shard), feats // 4
    for c in range(4):
        @pl.when(spot_ref[2] == c)
        def _(c=c):
            for s in range(n_shard):
                for column, width, place in slab_part(feats, n_shard, s, c * wide, (c + 1) * wide):
                    out_ref[s, :, place:place + width] = w_ref[:, column:column + width]
                out_ref[s, :, wide:wide + out_wide] = out_w_ref[:, c * out_wide:(c + 1) * out_wide]
                out_ref[s, :, wide + out_wide:] = jnp.zeros_like(out_ref[s, :, wide + out_wide:])


def pack_ff_kernel(n_shard, spot_ref, up_ref, down_ref, bias_ref, out_ref, own_bias_ref):
    feats = down_ref.shape[1]
    quarter = down_ref.shape[0] // 4
    aligned = -(-feats // 128) * 128
    out_ref[...] = jnp.zeros_like(out_ref)
    for c in range(4):
        r = (c % 2) * 2 + c // 2

        @pl.when(spot_ref[2] == c)
        def _(c=c, r=r):
            for s in range(n_shard):
                at = (s * 4 + r) * quarter
                out_ref[:, s * quarter:(s + 1) * quarter] = up_ref[:, at:at + quarter]
                own_bias_ref[:, s * quarter:(s + 1) * quarter] = bias_ref[:, at:at + quarter]
            out_ref[:, aligned:aligned + feats] = down_ref[r * quarter:(r + 1) * quarter, :]


def middle_kernel(
    spot_ref, o_ref, o16_ref, wa_ref, wb_ref, tok_ref, gain_ref, bias_ref,
    h_ref, middle_ref, attended_ref, w_ref,
):
    n_shard, tile, mine = o_ref.shape
    feats = tok_ref.shape[1]
    wide, first = feats // 4, in_width(feats, n_shard)
    for s in range(n_shard):
        attended_ref[:, s * mine:(s + 1) * mine] = o_ref[s]
    attended_ref[:, n_shard * mine:] = o16_ref[:, HEAD:].astype(BF)
    for c in range(4):
        @pl.when(spot_ref[2] == c)
        def _(c=c):
            for n, (ref, at) in enumerate(((wa_ref, 0), (wa_ref, 1), (wb_ref, 0), (wb_ref, 1))):
                place = c ^ n
                w_ref[:, place * wide:(place + 1) * wide] = ref[at, :, first:first + wide]
    middle = tok_ref[...].astype(F32) + (dot(attended_ref[...], w_ref[...]) + bias_ref[3:4])
    middle_ref[...] = middle
    normed, _ = norm_stats(middle)
    put(h_ref, (normed * gain_ref[1:2] + bias_ref[4:5]).astype(BF))


def by_corner(spot_ref, full_ref, wide, keep_a, keep_b, send_ref):
    for c in range(4):
        @pl.when(spot_ref[2] == c)
        def _(c=c):
            for n in range(4):
                p = c ^ n
                part = full_ref[:, p * wide:(p + 1) * wide]
                if n < 2:
                    put((keep_a, keep_b)[n], part)
                else:
                    put(send_ref.at[n - 2], part.astype(BF))


def middle_back_kernel(
    spot_ref, kept_ref, core_ref, far_ref, middle_ref, w_ref, cot_ref, attended_ref, gain_ref,
    dmiddle_ref, do_ref, do16_ref, keep_a, keep_b, send_ref, sums_ref, full_scr,
):
    n_shard, tile, mine = do_ref.shape
    feats = middle_ref.shape[1]
    dh = (kept_ref[...] + core_ref[...].astype(F32) + far_ref[...].astype(F32))[:, :feats]
    normed, rate = norm_stats(middle_ref[...])
    dout = cot_ref[:, :feats].astype(F32)
    back, gain_sum, bias_sum = norm_back(dh, normed, rate, gain_ref[1:2])
    dmiddle = dout + back
    dmiddle_ref[...] = dmiddle
    dbranch = dmiddle.astype(BF)
    dattended = dot_nt(dbranch, w_ref[...]).astype(BF)
    for s in range(n_shard):
        do_ref[s] = dattended[:, s * mine:(s + 1) * mine]
    last = dattended[:, n_shard * mine:]
    do16_ref[...] = jnp.concatenate([jnp.zeros_like(last), last], axis=1)
    full_scr[...] = dot_tn(attended_ref[...], dbranch)
    by_corner(spot_ref, full_scr, feats // 4, keep_a, keep_b, send_ref)
    sums_ref[0:1] = jnp.sum(dbranch.astype(F32), axis=0, keepdims=True)
    sums_ref[1:2] = bias_sum
    sums_ref[2:3] = jnp.sum(dout, axis=0, keepdims=True)
    sums_ref[3:4] = gain_sum


def last_kernel(kept_ref, y_ref, a_ref, b_ref, dmiddle_ref, tok_ref, gain_ref, out_ref, sums_ref):
    dh = kept_ref[...].astype(F32) + y_ref[...].astype(F32) + a_ref[...].astype(F32) + b_ref[...].astype(F32)
    dh = dh[:, :tok_ref.shape[1]]
    normed, rate = norm_stats(tok_ref[...].astype(F32))
    back, gain_sum, bias_sum = norm_back(dh, normed, rate, gain_ref[0:1])
    out_ref[...] = dmiddle_ref[...] + back
    sums_ref[0:1] = bias_sum
    sums_ref[1:2] = gain_sum


def feed_forward_kernel(
    h_a, h_b, h_c, g_a, g_b, g_c, w_ref, bias_ref,
    act_ref, dpre_ref, keep_a, keep_b, send_ref, sum_ref,
):
    tile, aligned = h_a.shape
    units, feats = act_ref.shape[1], w_ref.shape[0]
    total = jnp.zeros((1, units), F32)
    sources = ((h_a, g_a, None), (h_b, g_b, None), (h_c, g_c, 0), (h_c, g_c, 1))
    for n, (h_ref, g_ref, at) in enumerate(sources):
        h = h_ref[:, :feats] if at is None else h_ref[at, :, :feats]
        g = g_ref[:, :feats] if at is None else g_ref[at, :, :feats]
        r = slice(n * tile, (n + 1) * tile)
        pre = dot(h, w_ref[:, :units]) + bias_ref[...]
        dact = dot_nt(g, w_ref[:, aligned:aligned + feats])
        square = pre * pre
        root = 0.7978845608028654
        flat = jnp.tanh(root * pre * (1.0 + 0.044715 * square))
        half = 0.5 * (1.0 + flat)
        act_ref[r, :] = (pre * half).astype(BF)
        slope = half + 0.5 * pre * (1.0 - flat * flat) * root * (1.0 + 0.134145 * square)
        dpre = (dact * slope).astype(BF)
        dpre_ref[r, :] = dpre
        total = total + jnp.sum(dpre.astype(F32), axis=0, keepdims=True)
        dh = dot_nt(dpre, w_ref[:, :units])
        if n < 2:
            put((keep_a, keep_b)[n], dh)
        else:
            put(send_ref.at[n - 2], dh.astype(BF))
    sum_ref[...] = total


def feed_grads_kernel(
    h_a, h_b, h_c, g_a, g_b, g_c, w_ref, act_ref, dpre_ref,
    keep_a, keep_b, send_ref, grad_ref, h_scr, g_scr,
):
    tile, aligned = h_a.shape
    units, feats = act_ref.shape[1], w_ref.shape[0]
    down = w_ref[:, aligned:aligned + feats]
    sources = ((h_a, g_a, None), (h_b, g_b, None), (h_c, g_c, 0), (h_c, g_c, 1))
    for n, (h_ref, g_ref, at) in enumerate(sources):
        r = slice(n * tile, (n + 1) * tile)
        h_scr[r, :] = h_ref[:, :feats] if at is None else h_ref[at, :, :feats]
        g_scr[r, :] = g_ref[:, :feats] if at is None else g_ref[at, :, :feats]
    step = 256
    for at in range(0, units, step):
        c = slice(at, min(at + step, units))
        grad_ref[:, c] = dot_tn(h_scr[...], dpre_ref[:, c]).astype(BF)
    for at in range(0, feats, step):
        end = min(at + step, feats)
        part = dot_tn(act_ref[...], g_scr[:, at:end])
        grad_ref[:, aligned + at:aligned + end] = part.astype(BF)
    blank = jnp.zeros((grad_ref.shape[0], aligned - feats), BF)
    grad_ref[:, units:aligned] = blank
    grad_ref[:, aligned + feats:2 * aligned] = blank
    for n in range(4):
        mixed = dot(act_ref[n * tile:(n + 1) * tile, :], down)
        if n < 2:
            put((keep_a, keep_b)[n], mixed)
        else:
            put(send_ref.at[n - 2], mixed.astype(BF))


def in_grad_kernel(blocks, spot_ref, *refs):
    h_refs, (dp_ref, dq16_ref, keep_a, keep_b, send_ref, full_scr) = refs[:blocks], refs[blocks:]
    tile = dq16_ref.shape[0]
    feats = keep_a.shape[0]
    for at in range(0, 512, 256):
        acc = dot_tn(h_refs[0][:, :feats], dp_ref[:tile, at:at + 256])
        for b in range(1, blocks):
            acc = acc + dot_tn(h_refs[b][:, :feats], dp_ref[b * tile:(b + 1) * tile, at:at + 256])
        full_scr[:, at:at + 256] = acc
    full_scr[:, 512:576] = dot_tn(h_refs[0][:, :feats], dq16_ref[...])[:, :HEAD]
    by_corner(spot_ref, full_scr, in_width(feats, blocks), keep_a, keep_b, send_ref)


def fold_kernel(wide, in_ref, out_ref):
    for s in range(in_ref.shape[0]):
        out_ref[:, s * wide:(s + 1) * wide] = in_ref[s, :, :wide]


def fill_kernel(all_ref, a_ref, b_ref, c_ref, out_ref):
    out_ref[...] = (a_ref[...] + b_ref[...].astype(F32) + c_ref[...].astype(F32)).astype(BF)


def filled(values, terms):
    count, wide = terms[0].shape
    last = values.shape[1] // wide - 1
    part = pl.BlockSpec((count, wide), lambda n: (0, 0))
    return pl.pallas_call(
        fill_kernel,
        grid=(1,),
        out_shape=jax.ShapeDtypeStruct(values.shape, values.dtype),
        in_specs=[pl.BlockSpec(memory_space=pl.ANY)] + [part] * 3,
        out_specs=pl.BlockSpec((count, wide), lambda n: (0, last)),
        input_output_aliases={0: 0},
        compiler_params=pltpu.CompilerParams(vmem_limit_bytes=32 * 2**20),
    )(values, *terms)


def owned_kernel(n_shard, spot_ref, a_ref, b_ref, c_ref, up_ref, down_ref, out_w_ref):
    quarter, feats = a_ref.shape[0], down_ref.shape[1]
    aligned = -(-feats // 128) * 128
    out_wide = feats // 4
    for c in range(4):
        @pl.when(spot_ref[2] == c)
        def _(c=c):
            for n, (ref, at) in enumerate(((a_ref, None), (b_ref, None), (c_ref, 0), (c_ref, 1))):
                place = c ^ n
                r = (place % 2) * 2 + place // 2
                part = ref[...] if at is None else ref[at]
                for s in range(n_shard):
                    to = (s * 4 + r) * quarter
                    up_ref[:, to:to + quarter] = part[:, s * quarter:(s + 1) * quarter].astype(F32)
                down_ref[r * quarter:(r + 1) * quarter, :] = part[:, aligned:aligned + feats].astype(F32)
                out_part = part[:, 2 * aligned:2 * aligned + out_wide].astype(F32)
                out_w_ref[:, place * out_wide:(place + 1) * out_wide] = out_part


def owned_in_kernel(n_shard, spot_ref, a_ref, b_ref, c_ref, out_ref):
    feats = out_ref.shape[1] // 3
    wide = in_width(feats, n_shard)
    shared = 3 * (feats // HEAD // n_shard * HEAD)
    for c in range(4):
        @pl.when(spot_ref[2] == c)
        def _(c=c):
            for n, (ref, at) in enumerate(((a_ref, None), (b_ref, None), (c_ref, 0), (c_ref, 1))):
                place = c ^ n
                low = place * wide

                def block(s):
                    lanes = slice(s * wide, (s + 1) * wide)
                    return (ref[:, lanes] if at is None else ref[at, :, lanes]).astype(F32)

                for s in range(n_shard):
                    for column, width, to in slab_part(feats, n_shard, s, low, min(low + wide, shared)):
                        out_ref[:, column:column + width] = block(s)[:, to:to + width]
                if low + wide > shared:
                    total = block(0)
                    for s in range(1, n_shard):
                        total = total + block(s)
                    first = max(low, shared)
                    for column, width, to in slab_part(feats, n_shard, 0, first, low + wide):
                        to = to + first - low
                        out_ref[:, column:column + width] = total[:, to:to + width]


VM = pl.BlockSpec(memory_space=pltpu.VMEM)
SM = pl.BlockSpec(memory_space=pltpu.SMEM)


def run(kernel, outs, operands, scalars=0, scratch=(), size=58, flops=0.0):
    moved = sum(v.size * v.dtype.itemsize for v in operands)
    moved = moved + sum(math.prod(shape) * jnp.dtype(kind).itemsize for shape, kind in outs)
    return pl.pallas_call(
        kernel,
        out_shape=tuple(jax.ShapeDtypeStruct(shape, kind) for shape, kind in outs),
        in_specs=[SM] * scalars + [VM] * (len(operands) - scalars),
        out_specs=tuple([VM] * len(outs)),
        scratch_shapes=[pltpu.VMEM(shape, kind) for shape, kind in scratch],
        compiler_params=pltpu.CompilerParams(vmem_limit_bytes=size * 2**20),
        cost_estimate=pl.CostEstimate(flops=int(flops), bytes_accessed=int(moved), transcendentals=0),
    )(*operands)


def swap(values, axis):
    return lax.ppermute(values, axis, [(0, 1), (1, 0)])


def gather_rep(values):
    other = swap(values, "x")
    return values, other, swap(jnp.stack([values, other]), "core")


def scatter_rep(keep_a, keep_b, send):
    across = swap(send, "core")
    return keep_a, across[0], swap((keep_b + across[1].astype(F32)).astype(BF), "x")


def shift(values, step):
    size = lax.axis_size("z")
    return lax.ppermute(values, "z", [(n, (n + step) % size) for n in range(size)])


def together(*values):
    return lax.optimization_barrier(values)


def ring_gather(values, beside):
    size = lax.axis_size("z")
    column = [values] + [None] * (size - 1)
    other = [None] * size
    arrived, last = [(0, values)], {1: values, -1: values}
    for n in range(1, size // 2 + 2):
        places, moving = [], []
        for place, block in arrived:
            places.append((other, place))
            moving.append(swap(block, "y"))
        arrived = []
        if n <= size // 2:
            steps = (1, -1) if size - n > n else (1,)
            for step in steps:
                places.append((column, n if step == 1 else size - n))
                moving.append(shift(last[step], step))
        moving = beside(n, moving)
        for (target, place), block in zip(places, moving):
            target[place] = block
            if target is column:
                arrived.append((place, block))
                last[1 if place == n else -1] = block
    return [block for pair in zip(column, other) for block in pair]


def ring_scatter(parts, beside):
    size = lax.axis_size("z")
    kept, sent = parts[0::2], parts[1::2]
    half = size // 2
    joined, running = {}, {1: None, -1: None}
    wanted = [[half] + ([size - half + 1] if size - half + 1 < size else [])]
    wanted += [[n] + ([size - n + 1] if size - n + 1 < size else []) for n in range(half - 1, 0, -1)]
    wanted += [[0]]
    for index, now in enumerate(wanted + [[]]):
        moving = [swap(sent[n], "y") for n in now]
        steps = []
        if index > 0:
            n = half + 1 - index
            for step, place in ((-1, n), (1, size - n)):
                if n >= 1 and (step == -1 or size - n > n):
                    total = joined[place]
                    if running[step] is not None:
                        total = total + running[step].astype(F32)
                    steps.append(step)
                    moving.append(shift(total.astype(BF), step))
        if not moving:
            continue
        moving = beside(index + 1, moving)
        for n, block in zip(now, moving):
            joined[n] = block if n == 0 else kept[n].astype(F32) + block.astype(F32)
        for step, block in zip(steps, moving[len(now):]):
            running[step] = block
    return kept[0], joined[0], running[-1], running[1]


def sum_dp(values):
    if lax.axis_size("dp") > 1:
        return lax.psum(values, "dp")
    return values


def sum_all(values):
    z_size = lax.axis_size("z")
    for axis in ("core", "x", "y"):
        values = values + swap(values, axis)
    step = 1
    while step < z_size:
        values = values + lax.ppermute(values, "z", [(n, n ^ step) for n in range(z_size)])
        step = step * 2
    return sum_dp(values)


def gather_shard(values):
    return lax.all_gather(values, SHARD, axis=0, tiled=True)


def scatter_shard(values):
    return lax.psum_scatter(values.astype(BF), SHARD, scatter_dimension=0, tiled=True)


def exchange_shard(values):
    return lax.all_to_all(values, SHARD, 0, 0, tiled=True)


def shards(
    tokens, slot, lengths, attn_in_weight, attn_out_weight, up_weight, down_weight,
    norm_gains, layer_biases, up_bias, cotangent,
):
    tile, feats = tokens.shape
    zs = lax.axis_size("z")
    n_shard = zs * 2
    total = n_shard * tile
    mine = feats // HEAD // n_shard * HEAD
    spare = n_shard * mine
    z, y = lax.axis_index("z"), lax.axis_index("y")
    me = z * 2 + y
    rep = lax.axis_index("x") * 2 + lax.axis_index("core")
    corner = lax.axis_index("core") * 2 + lax.axis_index("x")
    spot = jnp.stack([z, y, corner]).astype(jnp.int32)
    row_part = attn_in_weight.shape[0]
    ff_part = down_weight.shape[0]
    n_rep = 4
    quarter = ff_part // n_rep
    units = n_shard * quarter
    aligned = -(-feats // 128) * 128
    in_wide = in_width(feats, n_shard)
    out_wide = feats // n_rep
    both_wide = -(-(in_wide + out_wide) // 128) * 128
    in_full = -(-in_wide // 128) * 128
    out_full = -(-out_wide // 128) * 128
    fold_wide = -(-(n_shard * in_wide) // 128) * 128

    ends = jnp.cumsum(lengths[0]).astype(jnp.int32)
    (h_first,) = run(
        first_norm_kernel, [((tile, aligned), BF)], (tokens, slot.reshape(tile, 1), norm_gains, layer_biases)
    )

    (in_pack,) = run(
        pack_in_kernel, [((n_shard, row_part, both_wide), BF)], (spot, attn_in_weight, attn_out_weight), 1
    )
    ff_pack, up_bias_mine = run(
        functools.partial(pack_ff_kernel, n_shard),
        [((row_part, 2 * aligned), BF), ((1, units), F32)],
        (spot, up_weight, down_weight, up_bias.reshape(1, -1)), 1,
    )
    held = dict(
        in_own=exchange_shard(in_pack).reshape(feats, both_wide),
        dout=jnp.pad(cotangent, ((0, 0), (0, aligned - feats))),
        ff_pack=ff_pack,
    )

    def beside_gather(n, moving):
        names = []
        if n == 1:
            names = ["in_own", "dout", "ff_pack"]
        elif n == 2:
            held["in_far"], held["dout_far"] = swap(held["in_own"], "x"), swap(held["dout"], "x")
            names = ["in_own", "in_far", "dout", "dout_far", "ff_pack"]
        elif n == 3:
            held["in_a"] = jnp.stack([held["in_own"], held["in_far"]])
            held["in_b"] = swap(held["in_a"], "core")
            held["g_core"] = swap(jnp.stack([held["dout"], held["dout_far"]]), "core")
            names = ["in_a", "in_b", "dout", "dout_far", "g_core"]
        *moving, = together(*moving, *[held[name] for name in names])
        for name in reversed(names):
            held[name] = moving.pop()
        if n == GATHER_ROUND:
            held["w_all"] = gather_shard(held["ff_pack"])
        return moving

    h_parts = ring_gather(h_first, beside_gather)
    w_all, in_a, in_b = held["w_all"], held["in_a"], held["in_b"]
    dout, g_rep = held["dout"], (held["dout"], held["dout_far"], held["g_core"])
    (sp, kt, o_own, of, lse, q16, o16, lse16, w_own, slot_rows, slot_columns) = run(
        functools.partial(forward_kernel, n_shard),
        [
            ((total, 512), BF), ((n_shard, 128, tile), BF), ((n_shard, tile, 128), BF), ((total, 128), F32),
            ((n_shard, 2, tile), F32), ((tile, 128), BF), ((tile, 128), F32), ((1, tile), F32),
            ((aligned, 640), BF), ((n_shard, 1, tile), jnp.int32), ((total, 1), jnp.int32),
        ],
        (ends, spot, *h_parts, in_a, in_b, layer_biases, slot.reshape(1, tile)), 2,
        scratch=[((total, 640), BF), ((n_shard, 256, tile), BF), ((total, 128), BF), ((1, total), jnp.int32)],
        size=58, flops=30e9,
    )
    o_back = exchange_shard(o_own)
    h_second, middle, attended, w_out = run(
        middle_kernel,
        [((tile, aligned), BF), ((tile, feats), F32), ((tile, feats), BF), ((feats, feats), BF)],
        (spot, o_back, o16, in_a, in_b, tokens, norm_gains, layer_biases), 1, flops=2e9,
    )

    h_rep = gather_rep(h_second)
    whole, one, pair = (n_rep * tile, units), (tile, aligned), (2, tile, aligned)
    act, dpre, *dh_terms, up_bias_grad = run(
        feed_forward_kernel,
        [(whole, BF), (whole, BF), (one, F32), (one, F32), (pair, BF), ((1, units), F32)],
        (*h_rep, *g_rep, w_all, up_bias_mine), flops=10e9,
    )
    kept, joined, send = dh_terms
    across = swap(send, "core")
    joined, act, dpre = together((joined + across[1].astype(F32)).astype(BF), act, dpre)
    *mixed_terms, ff_grads = run(
        feed_grads_kernel,
        [(one, F32), (one, F32), (pair, BF), ((feats, 2 * aligned + out_full), BF)],
        (*h_rep, *g_rep, w_all, act, dpre),
        scratch=[((n_rep * tile, feats), BF)] * 2, size=58, flops=10e9,
    )
    far, ff_grads = together(swap(joined, "x"), ff_grads)
    dh_terms = (kept, across[0], far)
    mixed_terms = scatter_rep(*mixed_terms)
    mixed = (
        middle
        + (mixed_terms[0] + mixed_terms[1].astype(F32) + mixed_terms[2].astype(F32))[:, :feats]
        + layer_biases[5]
    ).astype(BF)

    dmiddle, do_all, do16, *out_terms, sums = run(
        middle_back_kernel,
        [
            ((tile, feats), F32), ((n_shard, tile, mine), BF), ((tile, 128), BF),
            ((feats, out_full), F32), ((feats, out_full), F32), ((2, feats, out_full), BF), ((4, feats), F32),
        ],
        (spot, *dh_terms, middle, w_out, dout, attended, norm_gains), 1,
        scratch=[((feats, feats), F32)], flops=3e9,
    )

    ff_grads = filled(ff_grads, scatter_rep(*out_terms))
    do_own, ff_grads = together(exchange_shard(do_all).reshape(total, mine), ff_grads)
    ff_owned = sum_dp(scatter_shard(ff_grads))
    dp, dq16, *dh_parts = run(
        backward_kernel,
        [((total, 512), BF), ((tile, 128), BF)] + [((tile, aligned), BF)] * n_shard,
        (
            ends, w_own, slot_rows, slot_columns, slot.reshape(1, tile),
            sp, kt, of, lse, do_own, q16, do16, o16, lse16,
        ),
        1,
        scratch=[((total, 128), BF), ((total, 256), F32), ((total, 128), F32), ((total, 512), BF)],
        size=58, flops=30e9,
    )
    in_kept, in_joined, in_send = run(
        functools.partial(in_grad_kernel, n_shard),
        [((feats, in_full), F32), ((feats, in_full), F32), ((2, feats, in_full), BF)],
        (spot, *h_parts, dp, dq16), 1, scratch=[((feats, 576), F32)], flops=3e9,
    )

    def beside_scatter(n, moving):
        if n == 3:
            across = swap(in_send, "core")
            far = swap((in_joined + across[1].astype(F32)).astype(BF), "x")
            *moving, across, far, held["ff"] = together(*moving, across, far, ff_owned)
            grad = (in_kept + across[0].astype(F32) + far.astype(F32)).astype(BF)
            held["in_back"] = exchange_shard(grad.reshape(n_shard, row_part, in_full))
        return moving

    dh_first = ring_scatter(dh_parts, beside_scatter)
    (in_back,) = run(functools.partial(fold_kernel, in_wide), [((row_part, fold_wide), BF)], (held["in_back"],))
    in_back = gather_rep(sum_dp(in_back))

    tokens_grad, first_sums = run(
        last_kernel, [((tile, feats), F32), ((2, feats), F32)], (*dh_first, dmiddle, tokens, norm_gains)
    )

    up_out, down_out, out_out = run(
        functools.partial(owned_kernel, n_shard),
        [((row_part, up_weight.shape[1]), F32), ((ff_part, feats), F32), ((row_part, feats), F32)],
        (spot, *gather_rep(held["ff"])), 1,
    )
    (in_out,) = run(
        functools.partial(owned_in_kernel, n_shard), [((row_part, 3 * feats), F32)], (spot, *in_back), 1
    )
    zeros = functools.partial(jnp.zeros, dtype=F32)
    dp_sums = jnp.sum(dp.astype(F32), axis=0)
    query_sums = lax.dynamic_update_slice(zeros(feats), dp_sums[:mine], (me * mine,))
    query_sums = query_sums + jnp.pad(jnp.sum(dq16[:, :HEAD].astype(F32), axis=0), (spare, 0))
    value_sums = lax.dynamic_update_slice(zeros(feats), dp_sums[2 * mine : 3 * mine], (me * mine,))
    value_sums = value_sums + jnp.pad(dp_sums[3 * mine + HEAD : 3 * mine + 2 * HEAD], (spare, 0))
    place = (jnp.arange(n_rep) == rep)[:, None]
    vectors = jnp.concatenate(
        [
            first_sums[0:1], jnp.stack([query_sums, value_sums]), sums[0:3], first_sums[1:2], sums[3:4],
            jnp.where(place, up_bias_grad, 0.0),
        ]
    )
    vectors = lax.dynamic_slice_in_dim(sum_all(vectors), me * row_part, row_part, 1)
    return (
        mixed, tokens_grad, in_out, out_out, up_out, down_out,
        vectors[6:8], vectors[0:6], vectors[8:].reshape(-1),
    )


def solution(mesh):
    replicas, n_shard = mesh.shape["replica"], mesh.shape["shard"]
    fine = Mesh(
        mesh.devices.reshape(replicas // 4, 2, 2, n_shard // 2, 2), ("dp", "x", "core", "z", "y")
    )
    rep = ("dp", "x", "core")
    both = rep + SHARD
    in_specs = (
        P(both, None), P(both), P(rep, None), P(SHARD, None), P(SHARD, None), P(SHARD, None), P(SHARD, None),
        P(), P(), P(), P(both, None),
    )
    out_specs = (
        P(both, None), P(both, None), P(SHARD, None), P(SHARD, None), P(SHARD, None), P(SHARD, None),
        P(None, SHARD), P(None, SHARD), P(SHARD),
    )
    return jax.shard_map(shards, mesh=fine, in_specs=in_specs, out_specs=out_specs, check_vma=False)
```

```python
import functools
import math

import jax
import jax.numpy as jnp
from jax import lax
from jax.experimental import pallas as pl
from jax.experimental.pallas import tpu as pltpu
from jax.sharding import Mesh, PartitionSpec as P

HEAD = 64
BF = jnp.bfloat16
F32 = jnp.float32
REP = ("x", "core")
SHARD = ("z", "y")
NEG = -1e30


def dot(left, right):
    return jnp.dot(left, right, preferred_element_type=F32)


def dot_nt(left, right):
    return lax.dot_general(left, right, (((1,), (1,)), ((), ())), preferred_element_type=F32)


def dot_tn(left, right):
    return lax.dot_general(left, right, (((0,), (0,)), ((), ())), preferred_element_type=F32)


def iota(shape, dim):
    return lax.broadcasted_iota(jnp.int32, shape, dim)


def doc_starts(places, ends_ref):
    starts = jnp.zeros_like(places)
    for n in range(ends_ref.shape[0]):
        starts = jnp.where(places >= ends_ref[n], ends_ref[n], starts)
    return starts


def first_block(block, tile, ends_ref):
    row = block * tile
    start = jnp.int32(0)
    for n in range(ends_ref.shape[0]):
        start = jnp.where(row >= ends_ref[n], ends_ref[n], start)
    return lax.div(start, jnp.int32(tile))


def rows(block, tile):
    return pl.ds(pl.multiple_of(block * tile, tile), tile)


def only_head(values, head):
    lanes = iota(values.shape, 1)
    keep = (lanes < HEAD) if head == 0 else (lanes >= HEAD)
    return jnp.where(keep, values, jnp.zeros_like(values))


def tail_slots(tail):
    lanes = iota(tail.shape, 1)
    spare = tail.shape[1] // 2
    weight = jnp.where(lanes == spare, 64.0, jnp.where(lanes == spare + 1, 1.0, 0.0))
    return tail.astype(F32) * weight


def forward_kernel(blocks, ends_ref, spot_ref, *refs):
    h_refs, refs = refs[:blocks], refs[blocks:]
    (
        wa_ref, wb_ref, bias_ref, own_ref,
        sp_ref, kt_ref, o_ref, of_ref, lse_ref, q16_ref, o16_ref, lse16_ref, w_ref, srow_ref, scol_ref,
        p_scr, vt_scr, ob_scr, row_scr,
    ) = refs
    tile = own_ref.shape[1]
    total = blocks * tile
    feats = wa_ref.shape[1]
    wide = in_width(feats, blocks)
    z, y, corner = spot_ref[0], spot_ref[1], spot_ref[2]
    zs = blocks // 2

    w_ref[...] = jnp.zeros_like(w_ref)
    for c in range(4):
        @pl.when(corner == c)
        def _(c=c):
            for n, (ref, at) in enumerate(((wa_ref, 0), (wa_ref, 1), (wb_ref, 0), (wb_ref, 1))):
                place = c ^ n
                w_ref[:feats, place * wide:(place + 1) * wide] = ref[at, :, :wide]

    me = z * 2 + y
    lanes = pl.ds(pl.multiple_of(me * 128, 128), 128)
    blank = jnp.zeros((1, 128), F32)
    last = bias_ref.shape[1] - HEAD
    bias = jnp.concatenate(
        [
            bias_ref[1:2, lanes], blank, bias_ref[2:3, lanes],
            blank[:, :HEAD], bias_ref[2:3, last:], bias_ref[1:2, last:], blank[:, :HEAD],
        ],
        axis=1,
    )
    for b in range(blocks):
        r = slice(b * tile, (b + 1) * tile)
        p_scr[r, :] = (dot(h_refs[b][...], w_ref[...]) + bias).astype(BF)
        tail = tail_slots(h_refs[b][:, h_refs[b].shape[1] - 128:])
        scol_ref[r, :] = jnp.sum(tail, axis=1, keepdims=True).astype(jnp.int32)
        row = jnp.sum(tail.T, axis=0, keepdims=True).astype(jnp.int32)
        row_scr[:, r] = row
        shard = lax.rem(z + zs - b // 2, zs) * 2 + lax.rem(y + b % 2, 2)
        srow_ref[shard] = row

    @pl.loop(0, blocks)
    def _(b):
        r = rows(b, tile)
        place = iota((tile, total), 0) + b * tile
        pick = jnp.where(row_scr[...] == place, 1.0, 0.0).astype(BF)
        sorted_f = dot(pick, p_scr[:, :512])
        sp_ref[r, :] = sorted_f.astype(BF)
        kt_ref[b] = sorted_f[:, 128:256].T.astype(BF)
        vt_scr[b, :128, :] = sorted_f[:, 256:384].T.astype(BF)
        vt_scr[b, 128:, :] = sorted_f[:, 384:512].T.astype(BF)

    q16 = p_scr[0:tile, 512:640]
    q16_ref[...] = q16

    own = own_ref[...]
    own_start = doc_starts(own, ends_ref)

    def step16(kb, state):
        m, l, acc = state
        kv = sp_ref[rows(kb, tile), 384:512]
        kpos = iota((tile, tile), 0) + kb * tile
        ok = (kpos <= own) & (kpos >= own_start)
        s = jnp.where(ok, dot_nt(kv, q16) * 0.125, NEG)
        mn = jnp.maximum(m, jnp.max(s, axis=0, keepdims=True))
        p = jnp.where(ok, jnp.exp(s - mn), 0.0)
        a = jnp.exp(m - mn)
        l = l * a + jnp.sum(p, axis=0, keepdims=True)
        acc = acc * a + dot(vt_scr[kb, 192:256, :], p.astype(BF))
        return mn, l, acc

    def query_block(qb, state16):
        state16 = step16(qb, state16)
        q = sp_ref[rows(qb, tile), 0:128]
        qs = [only_head(q, 0), only_head(q, 1)]
        qpos = iota((1, tile), 1) + qb * tile
        qstart = doc_starts(qpos, ends_ref)
        low = first_block(qb, tile, ends_ref)

        def step(n, state):
            kb = qb - n
            k = sp_ref[rows(kb, tile), 128:256]
            kpos = iota((tile, tile), 0) + kb * tile
            ok = (kpos <= qpos) & (kpos >= qstart)
            new = []
            for head in range(2):
                m, l, acc = state[head]
                s = jnp.where(ok, dot_nt(k, qs[head]) * 0.125, NEG)
                mn = jnp.maximum(m, jnp.max(s, axis=0, keepdims=True))
                p = jnp.exp(s - mn)
                a = jnp.exp(m - mn)
                l = l * a + jnp.sum(p, axis=0, keepdims=True)
                vt = vt_scr[kb, head * HEAD:(head + 1) * HEAD, :]
                acc = acc * a + dot(vt, p.astype(BF))
                new.append((mn, l, acc))
            return tuple(new)

        state = step(0, (start, start))
        state = lax.fori_loop(1, qb - low + 1, step, state)
        out = jnp.concatenate([state[0][2] / state[0][1], state[1][2] / state[1][1]], axis=0).T
        of_ref[rows(qb, tile), :] = out
        ob_scr[rows(qb, tile), :] = out.astype(BF)
        lse_ref[qb] = jnp.concatenate([s[0] + jnp.log(s[1]) for s in state], axis=0)
        return state16

    start = (jnp.full((1, tile), NEG, F32), jnp.zeros((1, tile), F32), jnp.zeros((HEAD, tile), F32))
    m, l, acc = lax.fori_loop(0, blocks, query_block, start)
    o16_ref[...] = jnp.concatenate([jnp.zeros_like(acc), acc / l], axis=0).T
    lse16_ref[...] = m + jnp.log(l)

    for b in range(blocks):
        pick = jnp.where(scol_ref[b * tile:(b + 1) * tile, :] == iota((tile, total), 1), 1.0, 0.0).astype(BF)
        shard = lax.rem(z + zs - b // 2, zs) * 2 + lax.rem(y + b % 2, 2)
        o_ref[shard] = dot(pick, ob_scr[...]).astype(BF)


def backward_kernel(
    ends_ref, w_ref, srow_ref, scol_ref, own_ref, sp_ref, kt_ref, of_ref, lse_ref,
    do_ref, q16_ref, do16_ref, o16_ref, lse16_ref,
    dp_ref, dq16_ref, *refs,
):
    total = sp_ref.shape[0]
    tile = own_ref.shape[1]
    blocks = total // tile
    dh_refs, (dos_scr, acc_scr, acc16_scr, dps_scr) = refs[:blocks], refs[blocks:]

    places = jnp.concatenate([srow_ref[b] for b in range(blocks)], axis=1)

    @pl.loop(0, blocks)
    def _(b):
        r = rows(b, tile)
        pick = jnp.where(places == iota((tile, total), 0) + b * tile, 1.0, 0.0).astype(BF)
        dos_scr[r, :] = dot(pick, do_ref[...]).astype(BF)
        acc_scr[r, :] = jnp.zeros((tile, 256), F32)

    own = own_ref[...]
    own_start = doc_starts(own, ends_ref)
    q16 = q16_ref[...]
    do16 = do16_ref[...]
    both = jnp.concatenate([q16, do16], axis=0)
    delta16 = jnp.sum((do16.astype(F32) * o16_ref[...]).T, axis=0, keepdims=True)
    lse16 = lse16_ref[...]

    def step16(kb, dq):
        kr = rows(kb, tile)
        kv = sp_ref[kr, 384:512]
        kpos = iota((tile, tile), 0) + kb * tile
        ok = (kpos <= own) & (kpos >= own_start)
        p = jnp.where(ok, jnp.exp(dot_nt(kv, q16) * 0.125 - lse16), 0.0)
        ds = (p * (dot_nt(kv, do16) - delta16)).astype(BF)
        acc16_scr[kr, :] = dot(jnp.concatenate([ds, p.astype(BF)], axis=1), both)
        return dq + dot_tn(ds, kv)

    def query_block(qb, dq16):
        dq16 = step16(qb, dq16)
        qr = rows(qb, tile)
        q = sp_ref[qr, 0:128]
        do = dos_scr[qr, :]
        qs = [only_head(q, 0), only_head(q, 1)]
        ds_ = [only_head(do, 0), only_head(do, 1)]
        q_two = jnp.concatenate(qs, axis=0)
        do_two = jnp.concatenate(ds_, axis=0)
        prod = (do.astype(F32) * of_ref[qr, :]).T
        delta = [jnp.sum(prod[:HEAD], axis=0, keepdims=True), jnp.sum(prod[HEAD:], axis=0, keepdims=True)]
        lse = lse_ref[qb]
        qpos = iota((1, tile), 1) + qb * tile
        qstart = doc_starts(qpos, ends_ref)
        low = first_block(qb, tile, ends_ref)

        def step(kb, dqt):
            kr = rows(kb, tile)
            k = sp_ref[kr, 128:256]
            v = sp_ref[kr, 256:384]
            kpos = iota((tile, tile), 0) + kb * tile
            ok = (kpos <= qpos) & (kpos >= qstart)
            ps, dss, new = [], [], []
            for head in range(2):
                s = dot_nt(k, qs[head]) * 0.125 - lse[head:head + 1]
                p = jnp.where(ok, jnp.exp(s), 0.0)
                dprob = dot_nt(v, ds_[head])
                ds = (p * (dprob - delta[head])).astype(BF)
                ps.append(p.astype(BF))
                dss.append(ds)
                new.append(dqt[head] + dot(kt_ref[kb, head * HEAD:(head + 1) * HEAD, :], ds))
            acc_scr[kr, 0:128] += dot(jnp.concatenate(dss, axis=1), q_two)
            acc_scr[kr, 128:256] += dot(jnp.concatenate(ps, axis=1), do_two)
            return tuple(new)

        zero = jnp.zeros((HEAD, tile), F32)
        dqt = lax.fori_loop(low, qb, step, step(qb, (zero, zero)))
        dps_scr[qr, 0:128] = (jnp.concatenate(dqt, axis=0).T * 0.125).astype(BF)
        return dq16

    dq16 = lax.fori_loop(0, blocks, query_block, jnp.zeros((tile, 128), F32))
    dq16 = (dq16 * 0.125).astype(BF)
    dq16_ref[...] = dq16

    @pl.loop(0, blocks)
    def _(b):
        r = rows(b, tile)
        dps_scr[r, 128:256] = (acc_scr[r, 0:128] * 0.125).astype(BF)
        dps_scr[r, 256:384] = acc_scr[r, 128:256].astype(BF)
        part = acc16_scr[r, :]
        dps_scr[r, 384:512] = jnp.where(iota(part.shape, 1) < HEAD, part * 0.125, part).astype(BF)

    for b in range(blocks):
        r = slice(b * tile, (b + 1) * tile)
        pick = jnp.where(scol_ref[r, :] == iota((tile, total), 1), 1.0, 0.0).astype(BF)
        dp = dot(pick, dps_scr[...]).astype(BF)
        dp_ref[r, :] = dp
        dh = dot_nt(dp, w_ref[:, :512])
        if b == 0:
            dh = dh + dot_nt(only_head(dq16, 0), w_ref[:, 512:640])
        dh_refs[b][...] = dh[:, :dh_refs[b].shape[1]].astype(BF)


def norm_stats(values):
    centre = values - jnp.mean(values, axis=-1, keepdims=True)
    spread = jnp.mean(centre * centre, axis=-1, keepdims=True)
    rate = lax.rsqrt(spread + 1e-05)
    return centre * rate, rate


def norm_back(grad, normed, rate, gain):
    scaled = grad * gain
    inner = jnp.mean(scaled * normed, axis=-1, keepdims=True)
    back = rate * (scaled - jnp.mean(scaled, axis=-1, keepdims=True) - normed * inner)
    return back, jnp.sum(grad * normed, axis=0, keepdims=True), jnp.sum(grad, axis=0, keepdims=True)


def put(ref, values):
    width = values.shape[1]
    ref[:, :width] = values
    ref[:, width:] = jnp.zeros((ref.shape[0], ref.shape[1] - width), ref.dtype)


def first_norm_kernel(tok_ref, slot_ref, gain_ref, bias_ref, h_ref):
    tile, feats = tok_ref.shape
    normed, _ = norm_stats(tok_ref[...].astype(F32))
    h_ref[:, :feats] = (normed * gain_ref[0:1] + bias_ref[0:1]).astype(BF)
    width = h_ref.shape[1] - feats
    slot = slot_ref[...]
    high = lax.shift_right_logical(slot, 6)
    lanes = iota((tile, width), 1)
    pair = jnp.where(lanes == 0, high, jnp.where(lanes == 1, slot - high * 64, 0))
    h_ref[:, feats:] = pair.astype(F32).astype(BF)


def slab(feats, n_shard, shard):
    mine = feats // HEAD // n_shard * HEAD
    spare = n_shard * mine
    left = feats - spare
    return [
        (shard * mine, mine), (feats + shard * mine, mine), (2 * feats + shard * mine, mine),
        (feats + spare, left), (2 * feats + spare, left), (spare, left),
    ]


def slab_part(feats, n_shard, shard, low, high):
    found, at = [], 0
    for start, width in slab(feats, n_shard, shard):
        first, end = max(at, low), min(at + width, high)
        if first < end:
            found.append((start + first - at, end - first, first - low))
        at = at + width
    return found


def in_width(feats, n_shard):
    return sum(width for _, width in slab(feats, n_shard, 0)) // 4


def pack_in_kernel(spot_ref, w_ref, out_w_ref, out_ref):
    feats = w_ref.shape[1] // 3
    n_shard = out_ref.shape[0]
    wide, out_wide = in_width(feats, n_shard), feats // 4
    for c in range(4):
        @pl.when(spot_ref[2] == c)
        def _(c=c):
            for s in range(n_shard):
                for column, width, place in slab_part(feats, n_shard, s, c * wide, (c + 1) * wide):
                    out_ref[s, :, place:place + width] = w_ref[:, column:column + width]
                out_ref[s, :, wide:wide + out_wide] = out_w_ref[:, c * out_wide:(c + 1) * out_wide]
                out_ref[s, :, wide + out_wide:] = jnp.zeros_like(out_ref[s, :, wide + out_wide:])


def pack_ff_kernel(n_shard, spot_ref, up_ref, down_ref, bias_ref, out_ref, own_bias_ref):
    feats = down_ref.shape[1]
    quarter = down_ref.shape[0] // 4
    aligned = -(-feats // 128) * 128
    out_ref[...] = jnp.zeros_like(out_ref)
    for c in range(4):
        r = (c % 2) * 2 + c // 2

        @pl.when(spot_ref[2] == c)
        def _(c=c, r=r):
            for s in range(n_shard):
                at = (s * 4 + r) * quarter
                out_ref[:, s * quarter:(s + 1) * quarter] = up_ref[:, at:at + quarter]
                own_bias_ref[:, s * quarter:(s + 1) * quarter] = bias_ref[:, at:at + quarter]
            out_ref[:, aligned:aligned + feats] = down_ref[r * quarter:(r + 1) * quarter, :]


def middle_kernel(
    spot_ref, o_ref, o16_ref, wa_ref, wb_ref, tok_ref, gain_ref, bias_ref,
    h_ref, middle_ref, attended_ref, w_ref,
):
    n_shard, tile, mine = o_ref.shape
    feats = tok_ref.shape[1]
    wide, first = feats // 4, in_width(feats, n_shard)
    for s in range(n_shard):
        attended_ref[:, s * mine:(s + 1) * mine] = o_ref[s]
    attended_ref[:, n_shard * mine:] = o16_ref[:, HEAD:].astype(BF)
    for c in range(4):
        @pl.when(spot_ref[2] == c)
        def _(c=c):
            for n, (ref, at) in enumerate(((wa_ref, 0), (wa_ref, 1), (wb_ref, 0), (wb_ref, 1))):
                place = c ^ n
                w_ref[:, place * wide:(place + 1) * wide] = ref[at, :, first:first + wide]
    middle = tok_ref[...].astype(F32) + (dot(attended_ref[...], w_ref[...]) + bias_ref[3:4])
    middle_ref[...] = middle
    normed, _ = norm_stats(middle)
    put(h_ref, (normed * gain_ref[1:2] + bias_ref[4:5]).astype(BF))


def by_corner(spot_ref, full_ref, wide, keep_a, keep_b, send_ref):
    for c in range(4):
        @pl.when(spot_ref[2] == c)
        def _(c=c):
            for n in range(4):
                p = c ^ n
                part = full_ref[:, p * wide:(p + 1) * wide]
                if n < 2:
                    put((keep_a, keep_b)[n], part)
                else:
                    put(send_ref.at[n - 2], part.astype(BF))


def middle_back_kernel(
    spot_ref, kept_ref, core_ref, far_ref, middle_ref, w_ref, cot_ref, attended_ref, gain_ref,
    dmiddle_ref, do_ref, do16_ref, keep_a, keep_b, send_ref, sums_ref, full_scr,
):
    n_shard, tile, mine = do_ref.shape
    feats = middle_ref.shape[1]
    dh = (kept_ref[...] + core_ref[...].astype(F32) + far_ref[...].astype(F32))[:, :feats]
    normed, rate = norm_stats(middle_ref[...])
    dout = cot_ref[:, :feats].astype(F32)
    back, gain_sum, bias_sum = norm_back(dh, normed, rate, gain_ref[1:2])
    dmiddle = dout + back
    dmiddle_ref[...] = dmiddle
    dbranch = dmiddle.astype(BF)
    dattended = dot_nt(dbranch, w_ref[...]).astype(BF)
    for s in range(n_shard):
        do_ref[s] = dattended[:, s * mine:(s + 1) * mine]
    last = dattended[:, n_shard * mine:]
    do16_ref[...] = jnp.concatenate([jnp.zeros_like(last), last], axis=1)
    full_scr[...] = dot_tn(attended_ref[...], dbranch)
    by_corner(spot_ref, full_scr, feats // 4, keep_a, keep_b, send_ref)
    sums_ref[0:1] = jnp.sum(dbranch.astype(F32), axis=0, keepdims=True)
    sums_ref[1:2] = bias_sum
    sums_ref[2:3] = jnp.sum(dout, axis=0, keepdims=True)
    sums_ref[3:4] = gain_sum


def last_kernel(kept_ref, y_ref, a_ref, b_ref, dmiddle_ref, tok_ref, gain_ref, out_ref, sums_ref):
    dh = kept_ref[...].astype(F32) + y_ref[...].astype(F32) + a_ref[...].astype(F32) + b_ref[...].astype(F32)
    dh = dh[:, :tok_ref.shape[1]]
    normed, rate = norm_stats(tok_ref[...].astype(F32))
    back, gain_sum, bias_sum = norm_back(dh, normed, rate, gain_ref[0:1])
    out_ref[...] = dmiddle_ref[...] + back
    sums_ref[0:1] = bias_sum
    sums_ref[1:2] = gain_sum


def feed_forward_kernel(
    h_a, h_b, h_c, g_a, g_b, g_c, w_ref, bias_ref,
    act_ref, dpre_ref, keep_a, keep_b, send_ref, sum_ref,
):
    tile, aligned = h_a.shape
    units, feats = act_ref.shape[1], w_ref.shape[0]
    total = jnp.zeros((1, units), F32)
    sources = ((h_a, g_a, None), (h_b, g_b, None), (h_c, g_c, 0), (h_c, g_c, 1))
    for n, (h_ref, g_ref, at) in enumerate(sources):
        h = h_ref[:, :feats] if at is None else h_ref[at, :, :feats]
        g = g_ref[:, :feats] if at is None else g_ref[at, :, :feats]
        r = slice(n * tile, (n + 1) * tile)
        pre = dot(h, w_ref[:, :units]) + bias_ref[...]
        dact = dot_nt(g, w_ref[:, aligned:aligned + feats])
        square = pre * pre
        root = 0.7978845608028654
        flat = jnp.tanh(root * pre * (1.0 + 0.044715 * square))
        half = 0.5 * (1.0 + flat)
        act_ref[r, :] = (pre * half).astype(BF)
        slope = half + 0.5 * pre * (1.0 - flat * flat) * root * (1.0 + 0.134145 * square)
        dpre = (dact * slope).astype(BF)
        dpre_ref[r, :] = dpre
        total = total + jnp.sum(dpre.astype(F32), axis=0, keepdims=True)
        dh = dot_nt(dpre, w_ref[:, :units])
        if n < 2:
            put((keep_a, keep_b)[n], dh)
        else:
            put(send_ref.at[n - 2], dh.astype(BF))
    sum_ref[...] = total


def feed_grads_kernel(
    h_a, h_b, h_c, g_a, g_b, g_c, w_ref, act_ref, dpre_ref,
    keep_a, keep_b, send_ref, grad_ref, h_scr, g_scr,
):
    tile, aligned = h_a.shape
    units, feats = act_ref.shape[1], w_ref.shape[0]
    down = w_ref[:, aligned:aligned + feats]
    sources = ((h_a, g_a, None), (h_b, g_b, None), (h_c, g_c, 0), (h_c, g_c, 1))
    for n, (h_ref, g_ref, at) in enumerate(sources):
        r = slice(n * tile, (n + 1) * tile)
        h_scr[r, :] = h_ref[:, :feats] if at is None else h_ref[at, :, :feats]
        g_scr[r, :] = g_ref[:, :feats] if at is None else g_ref[at, :, :feats]
    step = 256
    for at in range(0, units, step):
        c = slice(at, min(at + step, units))
        grad_ref[:, c] = dot_tn(h_scr[...], dpre_ref[:, c]).astype(BF)
    for at in range(0, feats, step):
        end = min(at + step, feats)
        part = dot_tn(act_ref[...], g_scr[:, at:end])
        grad_ref[:, aligned + at:aligned + end] = part.astype(BF)
    blank = jnp.zeros((grad_ref.shape[0], aligned - feats), BF)
    grad_ref[:, units:aligned] = blank
    grad_ref[:, aligned + feats:] = blank
    for n in range(4):
        mixed = dot(act_ref[n * tile:(n + 1) * tile, :], down)
        if n < 2:
            put((keep_a, keep_b)[n], mixed)
        else:
            put(send_ref.at[n - 2], mixed.astype(BF))


def in_grad_kernel(blocks, spot_ref, *refs):
    h_refs, (dp_ref, dq16_ref, keep_a, keep_b, send_ref, full_scr) = refs[:blocks], refs[blocks:]
    tile = dq16_ref.shape[0]
    feats = keep_a.shape[0]
    for at in range(0, 512, 256):
        acc = dot_tn(h_refs[0][:, :feats], dp_ref[:tile, at:at + 256])
        for b in range(1, blocks):
            acc = acc + dot_tn(h_refs[b][:, :feats], dp_ref[b * tile:(b + 1) * tile, at:at + 256])
        full_scr[:, at:at + 256] = acc
    full_scr[:, 512:576] = dot_tn(h_refs[0][:, :feats], dq16_ref[...])[:, :HEAD]
    by_corner(spot_ref, full_scr, in_width(feats, blocks), keep_a, keep_b, send_ref)


def join_kernel(wide, out_wide, a_ref, b_ref, c_ref, out_a_ref, out_b_ref, out_c_ref, to_ref):
    to_ref[...] = jnp.zeros_like(to_ref)
    part = a_ref[...] + b_ref[...].astype(F32) + c_ref[...].astype(F32)
    to_ref[:, :wide] = part[:, :wide].astype(BF)
    part = out_a_ref[...] + out_b_ref[...].astype(F32) + out_c_ref[...].astype(F32)
    to_ref[:, wide:wide + out_wide] = part[:, :out_wide].astype(BF)


def fold_kernel(wide, out_wide, in_ref, out_ref):
    n_shard = in_ref.shape[0]
    for s in range(n_shard):
        out_ref[:, s * wide:(s + 1) * wide] = in_ref[s, :, :wide]
    total = in_ref[0, :, wide:wide + out_wide].astype(F32)
    for s in range(1, n_shard):
        total = total + in_ref[s, :, wide:wide + out_wide].astype(F32)
    out_ref[:, n_shard * wide:n_shard * wide + out_wide] = total.astype(BF)
    out_ref[:, n_shard * wide + out_wide:] = jnp.zeros_like(out_ref[:, n_shard * wide + out_wide:])


def owned_kernel(n_shard, spot_ref, a_ref, b_ref, c_ref, up_ref, down_ref):
    quarter, feats = a_ref.shape[0], down_ref.shape[1]
    aligned = -(-feats // 128) * 128
    for c in range(4):
        @pl.when(spot_ref[2] == c)
        def _(c=c):
            for n, (ref, at) in enumerate(((a_ref, None), (b_ref, None), (c_ref, 0), (c_ref, 1))):
                place = c ^ n
                r = (place % 2) * 2 + place // 2
                part = ref[...] if at is None else ref[at]
                for s in range(n_shard):
                    to = (s * 4 + r) * quarter
                    up_ref[:, to:to + quarter] = part[:, s * quarter:(s + 1) * quarter].astype(F32)
                down_ref[r * quarter:(r + 1) * quarter, :] = part[:, aligned:aligned + feats].astype(F32)


def owned_in_kernel(n_shard, spot_ref, a_ref, b_ref, c_ref, out_ref, out_w_ref):
    feats = out_ref.shape[1] // 3
    wide, out_wide = in_width(feats, n_shard), feats // 4
    shared = 3 * (feats // HEAD // n_shard * HEAD)
    for c in range(4):
        @pl.when(spot_ref[2] == c)
        def _(c=c):
            for n, (ref, at) in enumerate(((a_ref, None), (b_ref, None), (c_ref, 0), (c_ref, 1))):
                place = c ^ n
                low = place * wide

                def block(s):
                    lanes = slice(s * wide, (s + 1) * wide)
                    return (ref[:, lanes] if at is None else ref[at, :, lanes]).astype(F32)

                lanes = slice(n_shard * wide, n_shard * wide + out_wide)
                part = ref[:, lanes] if at is None else ref[at, :, lanes]
                out_w_ref[:, place * out_wide:(place + 1) * out_wide] = part.astype(F32)
                for s in range(n_shard):
                    for column, width, to in slab_part(feats, n_shard, s, low, min(low + wide, shared)):
                        out_ref[:, column:column + width] = block(s)[:, to:to + width]
                if low + wide > shared:
                    total = block(0)
                    for s in range(1, n_shard):
                        total = total + block(s)
                    first = max(low, shared)
                    for column, width, to in slab_part(feats, n_shard, 0, first, low + wide):
                        to = to + first - low
                        out_ref[:, column:column + width] = total[:, to:to + width]


VM = pl.BlockSpec(memory_space=pltpu.VMEM)
SM = pl.BlockSpec(memory_space=pltpu.SMEM)


def run(kernel, outs, operands, scalars=0, scratch=(), size=58, flops=0.0):
    moved = sum(v.size * v.dtype.itemsize for v in operands)
    moved = moved + sum(math.prod(shape) * jnp.dtype(kind).itemsize for shape, kind in outs)
    return pl.pallas_call(
        kernel,
        out_shape=tuple(jax.ShapeDtypeStruct(shape, kind) for shape, kind in outs),
        in_specs=[SM] * scalars + [VM] * (len(operands) - scalars),
        out_specs=tuple([VM] * len(outs)),
        scratch_shapes=[pltpu.VMEM(shape, kind) for shape, kind in scratch],
        compiler_params=pltpu.CompilerParams(vmem_limit_bytes=size * 2**20),
        cost_estimate=pl.CostEstimate(flops=int(flops), bytes_accessed=int(moved), transcendentals=0),
    )(*operands)


def swap(values, axis):
    return lax.ppermute(values, axis, [(0, 1), (1, 0)])


def gather_rep(values):
    other = swap(values, "x")
    return values, other, swap(jnp.stack([values, other]), "core")


def scatter_rep(keep_a, keep_b, send):
    across = swap(send, "core")
    return keep_a, across[0], swap((keep_b + across[1].astype(F32)).astype(BF), "x")


def shift(values, step):
    size = lax.axis_size("z")
    return lax.ppermute(values, "z", [(n, (n + step) % size) for n in range(size)])


def together(*values):
    return lax.optimization_barrier(values)


def ring_gather(values, beside):
    size = lax.axis_size("z")
    column = [values] + [None] * (size - 1)
    other = [None] * size
    arrived, last = [(0, values)], {1: values, -1: values}
    for n in range(1, size // 2 + 2):
        places, moving = [], []
        for place, block in arrived:
            places.append((other, place))
            moving.append(swap(block, "y"))
        arrived = []
        if n <= size // 2:
            steps = (1, -1) if size - n > n else (1,)
            for step in steps:
                places.append((column, n if step == 1 else size - n))
                moving.append(shift(last[step], step))
        moving = beside(n, moving)
        for (target, place), block in zip(places, moving):
            target[place] = block
            if target is column:
                arrived.append((place, block))
                last[1 if place == n else -1] = block
    return [block for pair in zip(column, other) for block in pair]


def ring_scatter(parts, beside):
    size = lax.axis_size("z")
    kept, sent = parts[0::2], parts[1::2]
    half = size // 2
    joined, running = {}, {1: None, -1: None}
    wanted = [[half] + ([size - half + 1] if size - half + 1 < size else [])]
    wanted += [[n] + ([size - n + 1] if size - n + 1 < size else []) for n in range(half - 1, 0, -1)]
    wanted += [[0]]
    for index, now in enumerate(wanted + [[]]):
        moving = [swap(sent[n], "y") for n in now]
        steps = []
        if index > 0:
            n = half + 1 - index
            for step, place in ((-1, n), (1, size - n)):
                if n >= 1 and (step == -1 or size - n > n):
                    total = joined[place]
                    if running[step] is not None:
                        total = total + running[step].astype(F32)
                    steps.append(step)
                    moving.append(shift(total.astype(BF), step))
        if not moving:
            continue
        moving = beside(index + 1, moving)
        for n, block in zip(now, moving):
            joined[n] = block if n == 0 else kept[n].astype(F32) + block.astype(F32)
        for step, block in zip(steps, moving[len(now):]):
            running[step] = block
    return kept[0], joined[0], running[-1], running[1]


def sum_dp(values):
    if lax.axis_size("dp") > 1:
        return lax.psum(values, "dp")
    return values


def sum_all(values):
    others = [shift(values, n) for n in range(1, lax.axis_size("z"))]
    for other in others:
        values = values + other
    for axis in ("y", "core", "x"):
        values = values + swap(values, axis)
    return sum_dp(values)


def gather_shard(values):
    return lax.all_gather(values, SHARD, axis=0, tiled=True)


def scatter_shard(values):
    return lax.psum_scatter(values.astype(BF), SHARD, scatter_dimension=0, tiled=True)


def exchange_shard(values):
    return lax.all_to_all(values, SHARD, 0, 0, tiled=True)


def shards(
    tokens, slot, lengths, attn_in_weight, attn_out_weight, up_weight, down_weight,
    norm_gains, layer_biases, up_bias, cotangent,
):
    tile, feats = tokens.shape
    zs = lax.axis_size("z")
    n_shard = zs * 2
    total = n_shard * tile
    mine = feats // HEAD // n_shard * HEAD
    spare = n_shard * mine
    z, y = lax.axis_index("z"), lax.axis_index("y")
    me = z * 2 + y
    rep = lax.axis_index("x") * 2 + lax.axis_index("core")
    corner = lax.axis_index("core") * 2 + lax.axis_index("x")
    spot = jnp.stack([z, y, corner]).astype(jnp.int32)
    row_part = attn_in_weight.shape[0]
    ff_part = down_weight.shape[0]
    n_rep = 4
    quarter = ff_part // n_rep
    units = n_shard * quarter
    aligned = -(-feats // 128) * 128
    in_wide = in_width(feats, n_shard)
    out_wide = feats // n_rep
    both_wide = -(-(in_wide + out_wide) // 128) * 128
    in_full = -(-in_wide // 128) * 128
    out_full = -(-out_wide // 128) * 128
    both_wide = -(-(in_wide + out_wide) // 128) * 128
    fold_wide = -(-(n_shard * in_wide + out_wide) // 128) * 128

    ends = jnp.cumsum(lengths[0]).astype(jnp.int32)
    (h_first,) = run(
        first_norm_kernel, [((tile, aligned), BF)], (tokens, slot.reshape(tile, 1), norm_gains, layer_biases)
    )

    (in_pack,) = run(
        pack_in_kernel, [((n_shard, row_part, both_wide), BF)], (spot, attn_in_weight, attn_out_weight), 1
    )
    ff_pack, up_bias_mine = run(
        functools.partial(pack_ff_kernel, n_shard),
        [((row_part, 2 * aligned), BF), ((1, units), F32)],
        (spot, up_weight, down_weight, up_bias.reshape(1, -1)), 1,
    )
    held = dict(
        in_own=exchange_shard(in_pack).reshape(feats, both_wide),
        dout=jnp.pad(cotangent, ((0, 0), (0, aligned - feats))),
        ff_pack=ff_pack,
    )

    held["w_all"] = gather_shard(ff_pack)

    def beside_gather(n, moving):
        names = []
        if n == 1:
            names = ["in_own", "dout"]
        elif n == 2:
            held["in_far"], held["dout_far"] = swap(held["in_own"], "x"), swap(held["dout"], "x")
            names = ["in_own", "in_far", "dout", "dout_far"]
        elif n == 3:
            held["in_a"] = jnp.stack([held["in_own"], held["in_far"]])
            held["in_b"] = swap(held["in_a"], "core")
            held["g_core"] = swap(jnp.stack([held["dout"], held["dout_far"]]), "core")
            names = ["in_a", "in_b", "dout", "dout_far", "g_core"]
        *moving, = together(*moving, *[held[name] for name in names])
        for name in reversed(names):
            held[name] = moving.pop()
        return moving

    h_parts = ring_gather(h_first, beside_gather)
    w_all, in_a, in_b = held["w_all"], held["in_a"], held["in_b"]
    dout, g_rep = held["dout"], (held["dout"], held["dout_far"], held["g_core"])
    (sp, kt, o_own, of, lse, q16, o16, lse16, w_own, slot_rows, slot_columns) = run(
        functools.partial(forward_kernel, n_shard),
        [
            ((total, 512), BF), ((n_shard, 128, tile), BF), ((n_shard, tile, 128), BF), ((total, 128), F32),
            ((n_shard, 2, tile), F32), ((tile, 128), BF), ((tile, 128), F32), ((1, tile), F32),
            ((aligned, 640), BF), ((n_shard, 1, tile), jnp.int32), ((total, 1), jnp.int32),
        ],
        (ends, spot, *h_parts, in_a, in_b, layer_biases, slot.reshape(1, tile)), 2,
        scratch=[((total, 640), BF), ((n_shard, 256, tile), BF), ((total, 128), BF), ((1, total), jnp.int32)],
        size=58, flops=30e9,
    )
    o_back = exchange_shard(o_own)
    h_second, middle, attended, w_out = run(
        middle_kernel,
        [((tile, aligned), BF), ((tile, feats), F32), ((tile, feats), BF), ((feats, feats), BF)],
        (spot, o_back, o16, in_a, in_b, tokens, norm_gains, layer_biases), 1, flops=2e9,
    )

    h_rep = gather_rep(h_second)
    whole, one, pair = (n_rep * tile, units), (tile, aligned), (2, tile, aligned)
    act, dpre, *dh_terms, up_bias_grad = run(
        feed_forward_kernel,
        [(whole, BF), (whole, BF), (one, F32), (one, F32), (pair, BF), ((1, units), F32)],
        (*h_rep, *g_rep, w_all, up_bias_mine), flops=10e9,
    )
    kept, joined, send = dh_terms
    across = swap(send, "core")
    joined, act, dpre = together((joined + across[1].astype(F32)).astype(BF), act, dpre)
    *mixed_terms, ff_grads = run(
        feed_grads_kernel,
        [(one, F32), (one, F32), (pair, BF), ((feats, 2 * aligned), BF)],
        (*h_rep, *g_rep, w_all, act, dpre),
        scratch=[((n_rep * tile, feats), BF)] * 2, size=58, flops=10e9,
    )
    far, ff_grads = together(swap(joined, "x"), ff_grads)
    ff_owned = sum_dp(scatter_shard(ff_grads))
    dh_terms = (kept, across[0], far)
    mixed_terms = scatter_rep(*mixed_terms)
    mixed = (
        middle
        + (mixed_terms[0] + mixed_terms[1].astype(F32) + mixed_terms[2].astype(F32))[:, :feats]
        + layer_biases[5]
    ).astype(BF)

    dmiddle, do_all, do16, *out_terms, sums = run(
        middle_back_kernel,
        [
            ((tile, feats), F32), ((n_shard, tile, mine), BF), ((tile, 128), BF),
            ((feats, out_full), F32), ((feats, out_full), F32), ((2, feats, out_full), BF), ((4, feats), F32),
        ],
        (spot, *dh_terms, middle, w_out, dout, attended, norm_gains), 1,
        scratch=[((feats, feats), F32)], flops=3e9,
    )

    out_terms = scatter_rep(*out_terms)
    do_own, *out_terms = together(exchange_shard(do_all).reshape(total, mine), *out_terms)
    dp, dq16, *dh_parts = run(
        backward_kernel,
        [((total, 512), BF), ((tile, 128), BF)] + [((tile, aligned), BF)] * n_shard,
        (
            ends, w_own, slot_rows, slot_columns, slot.reshape(1, tile),
            sp, kt, of, lse, do_own, q16, do16, o16, lse16,
        ),
        1,
        scratch=[((total, 128), BF), ((total, 256), F32), ((total, 128), F32), ((total, 512), BF)],
        size=58, flops=30e9,
    )
    in_kept, in_joined, in_send = run(
        functools.partial(in_grad_kernel, n_shard),
        [((feats, in_full), F32), ((feats, in_full), F32), ((2, feats, in_full), BF)],
        (spot, *h_parts, dp, dq16), 1, scratch=[((feats, 576), F32)], flops=3e9,
    )

    def beside_scatter(n, moving):
        if n == 2:
            held["across"] = swap(in_send, "core")
            far = swap((in_joined + held["across"][1].astype(F32)).astype(BF), "x")
            *moving, held["far"] = together(*moving, far)
        elif n == 3:
            (grad,) = run(
                functools.partial(join_kernel, in_wide, out_wide),
                [((feats, both_wide), BF)],
                (in_kept, held["across"][0], held["far"], *out_terms),
            )
            in_back = exchange_shard(grad.reshape(n_shard, row_part, both_wide))
            ff_far = swap(ff_owned, "x")
            *moving, held["in_back"], held["ff"], held["ff_far"] = together(*moving, in_back, ff_owned, ff_far)
        return moving

    dh_first = ring_scatter(dh_parts, beside_scatter)
    ff_pair = jnp.stack([held["ff"], held["ff_far"]])
    (in_back,) = run(functools.partial(fold_kernel, in_wide, out_wide), [((row_part, fold_wide), BF)], (held["in_back"],))
    in_back = gather_rep(sum_dp(in_back))

    tokens_grad, first_sums = run(
        last_kernel, [((tile, feats), F32), ((2, feats), F32)], (*dh_first, dmiddle, tokens, norm_gains)
    )

    up_out, down_out = run(
        functools.partial(owned_kernel, n_shard),
        [((row_part, up_weight.shape[1]), F32), ((ff_part, feats), F32)],
        (spot, held["ff"], held["ff_far"], swap(ff_pair, "core")), 1,
    )
    in_out, out_out = run(
        functools.partial(owned_in_kernel, n_shard),
        [((row_part, 3 * feats), F32), ((row_part, feats), F32)],
        (spot, *in_back), 1,
    )
    zeros = functools.partial(jnp.zeros, dtype=F32)
    dp_sums = jnp.sum(dp.astype(F32), axis=0)
    query_sums = lax.dynamic_update_slice(zeros(feats), dp_sums[:mine], (me * mine,))
    query_sums = query_sums + jnp.pad(jnp.sum(dq16[:, :HEAD].astype(F32), axis=0), (spare, 0))
    value_sums = lax.dynamic_update_slice(zeros(feats), dp_sums[2 * mine : 3 * mine], (me * mine,))
    value_sums = value_sums + jnp.pad(dp_sums[3 * mine + HEAD : 3 * mine + 2 * HEAD], (spare, 0))
    place = (jnp.arange(n_rep) == rep)[:, None]
    vectors = jnp.concatenate(
        [
            first_sums[0:1], jnp.stack([query_sums, value_sums]), sums[0:3], first_sums[1:2], sums[3:4],
            jnp.where(place, up_bias_grad, 0.0),
        ]
    )
    vectors = lax.dynamic_slice_in_dim(sum_all(vectors), me * row_part, row_part, 1)
    return (
        mixed, tokens_grad, in_out, out_out, up_out, down_out,
        vectors[6:8], vectors[0:6], vectors[8:].reshape(-1),
    )


def solution(mesh):
    replicas, n_shard = mesh.shape["replica"], mesh.shape["shard"]
    fine = Mesh(
        mesh.devices.reshape(replicas // 4, 2, 2, n_shard // 2, 2), ("dp", "x", "core", "z", "y")
    )
    rep = ("dp", "x", "core")
    both = rep + SHARD
    in_specs = (
        P(both, None), P(both), P(rep, None), P(SHARD, None), P(SHARD, None), P(SHARD, None), P(SHARD, None),
        P(), P(), P(), P(both, None),
    )
    out_specs = (
        P(both, None), P(both, None), P(SHARD, None), P(SHARD, None), P(SHARD, None), P(SHARD, None),
        P(None, SHARD), P(None, SHARD), P(SHARD),
    )
    return jax.shard_map(shards, mesh=fine, in_specs=in_specs, out_specs=out_specs, check_vma=False)
```

```python
import functools
import math

import jax
import jax.numpy as jnp
from jax import lax
from jax.experimental import pallas as pl
from jax.experimental.pallas import tpu as pltpu
from jax.sharding import Mesh, PartitionSpec as P

HEAD = 64
BF = jnp.bfloat16
F32 = jnp.float32
REP = ("x", "core")
SHARD = ("z", "y")
NEG = -1e30


def dot(left, right):
    return jnp.dot(left, right, preferred_element_type=F32)


def dot_nt(left, right):
    return lax.dot_general(left, right, (((1,), (1,)), ((), ())), preferred_element_type=F32)


def dot_tn(left, right):
    return lax.dot_general(left, right, (((0,), (0,)), ((), ())), preferred_element_type=F32)


def iota(shape, dim):
    return lax.broadcasted_iota(jnp.int32, shape, dim)


def doc_starts(places, ends_ref):
    starts = jnp.zeros_like(places)
    for n in range(ends_ref.shape[0]):
        starts = jnp.where(places >= ends_ref[n], ends_ref[n], starts)
    return starts


def first_block(block, tile, ends_ref):
    row = block * tile
    start = jnp.int32(0)
    for n in range(ends_ref.shape[0]):
        start = jnp.where(row >= ends_ref[n], ends_ref[n], start)
    return lax.div(start, jnp.int32(tile))


def rows(block, tile):
    return pl.ds(pl.multiple_of(block * tile, tile), tile)


def only_head(values, head):
    lanes = iota(values.shape, 1)
    keep = (lanes < HEAD) if head == 0 else (lanes >= HEAD)
    return jnp.where(keep, values, jnp.zeros_like(values))


def tail_slots(tail):
    lanes = iota(tail.shape, 1)
    spare = tail.shape[1] // 2
    weight = jnp.where(lanes == spare, 64.0, jnp.where(lanes == spare + 1, 1.0, 0.0))
    return tail.astype(F32) * weight


def forward_kernel(blocks, ends_ref, spot_ref, *refs):
    h_refs, refs = refs[:blocks], refs[blocks:]
    (
        wa_ref, wb_ref, bias_ref, own_ref,
        sp_ref, kt_ref, o_ref, of_ref, lse_ref, q16_ref, o16_ref, lse16_ref, w_ref, srow_ref, scol_ref,
        p_scr, vt_scr, ob_scr, row_scr,
    ) = refs
    tile = own_ref.shape[1]
    total = blocks * tile
    feats = wa_ref.shape[1]
    wide = in_width(feats, blocks)
    z, y, corner = spot_ref[0], spot_ref[1], spot_ref[2]
    zs = blocks // 2

    w_ref[...] = jnp.zeros_like(w_ref)
    for c in range(4):
        @pl.when(corner == c)
        def _(c=c):
            for n, (ref, at) in enumerate(((wa_ref, 0), (wa_ref, 1), (wb_ref, 0), (wb_ref, 1))):
                place = c ^ n
                w_ref[:feats, place * wide:(place + 1) * wide] = ref[at, :, :wide]

    me = z * 2 + y
    lanes = pl.ds(pl.multiple_of(me * 128, 128), 128)
    blank = jnp.zeros((1, 128), F32)
    last = bias_ref.shape[1] - HEAD
    bias = jnp.concatenate(
        [
            bias_ref[1:2, lanes], blank, bias_ref[2:3, lanes],
            blank[:, :HEAD], bias_ref[2:3, last:], bias_ref[1:2, last:], blank[:, :HEAD],
        ],
        axis=1,
    )
    for b in range(blocks):
        r = slice(b * tile, (b + 1) * tile)
        p_scr[r, :] = (dot(h_refs[b][...], w_ref[...]) + bias).astype(BF)
        tail = tail_slots(h_refs[b][:, h_refs[b].shape[1] - 128:])
        scol_ref[r, :] = jnp.sum(tail, axis=1, keepdims=True).astype(jnp.int32)
        row = jnp.sum(tail.T, axis=0, keepdims=True).astype(jnp.int32)
        row_scr[:, r] = row
        shard = lax.rem(z + zs - b // 2, zs) * 2 + lax.rem(y + b % 2, 2)
        srow_ref[shard] = row

    @pl.loop(0, blocks)
    def _(b):
        r = rows(b, tile)
        place = iota((tile, total), 0) + b * tile
        pick = jnp.where(row_scr[...] == place, 1.0, 0.0).astype(BF)
        sorted_f = dot(pick, p_scr[:, :512])
        sp_ref[r, :] = sorted_f.astype(BF)
        kt_ref[b] = sorted_f[:, 128:256].T.astype(BF)
        vt_scr[b, :128, :] = sorted_f[:, 256:384].T.astype(BF)
        vt_scr[b, 128:, :] = sorted_f[:, 384:512].T.astype(BF)

    q16 = p_scr[0:tile, 512:640]
    q16_ref[...] = q16

    own = own_ref[...]
    own_start = doc_starts(own, ends_ref)

    def step16(kb, state):
        m, l, acc = state
        kv = sp_ref[rows(kb, tile), 384:512]
        kpos = iota((tile, tile), 0) + kb * tile
        ok = (kpos <= own) & (kpos >= own_start)
        s = jnp.where(ok, dot_nt(kv, q16) * 0.125, NEG)
        mn = jnp.maximum(m, jnp.max(s, axis=0, keepdims=True))
        p = jnp.where(ok, jnp.exp(s - mn), 0.0)
        a = jnp.exp(m - mn)
        l = l * a + jnp.sum(p, axis=0, keepdims=True)
        acc = acc * a + dot(vt_scr[kb, 192:256, :], p.astype(BF))
        return mn, l, acc

    def query_block(qb, state16):
        state16 = step16(qb, state16)
        q = sp_ref[rows(qb, tile), 0:128]
        qs = [only_head(q, 0), only_head(q, 1)]
        qpos = iota((1, tile), 1) + qb * tile
        qstart = doc_starts(qpos, ends_ref)
        low = first_block(qb, tile, ends_ref)

        def step(n, state):
            kb = qb - n
            k = sp_ref[rows(kb, tile), 128:256]
            kpos = iota((tile, tile), 0) + kb * tile
            ok = (kpos <= qpos) & (kpos >= qstart)
            new = []
            for head in range(2):
                m, l, acc = state[head]
                s = jnp.where(ok, dot_nt(k, qs[head]) * 0.125, NEG)
                mn = jnp.maximum(m, jnp.max(s, axis=0, keepdims=True))
                p = jnp.exp(s - mn)
                a = jnp.exp(m - mn)
                l = l * a + jnp.sum(p, axis=0, keepdims=True)
                vt = vt_scr[kb, head * HEAD:(head + 1) * HEAD, :]
                acc = acc * a + dot(vt, p.astype(BF))
                new.append((mn, l, acc))
            return tuple(new)

        state = step(0, (start, start))
        state = lax.fori_loop(1, qb - low + 1, step, state)
        out = jnp.concatenate([state[0][2] / state[0][1], state[1][2] / state[1][1]], axis=0).T
        of_ref[rows(qb, tile), :] = out
        ob_scr[rows(qb, tile), :] = out.astype(BF)
        lse_ref[qb] = jnp.concatenate([s[0] + jnp.log(s[1]) for s in state], axis=0)
        return state16

    start = (jnp.full((1, tile), NEG, F32), jnp.zeros((1, tile), F32), jnp.zeros((HEAD, tile), F32))
    m, l, acc = lax.fori_loop(0, blocks, query_block, start)
    o16_ref[...] = jnp.concatenate([jnp.zeros_like(acc), acc / l], axis=0).T
    lse16_ref[...] = m + jnp.log(l)

    for b in range(blocks):
        pick = jnp.where(scol_ref[b * tile:(b + 1) * tile, :] == iota((tile, total), 1), 1.0, 0.0).astype(BF)
        shard = lax.rem(z + zs - b // 2, zs) * 2 + lax.rem(y + b % 2, 2)
        o_ref[shard] = dot(pick, ob_scr[...]).astype(BF)


def backward_kernel(
    ends_ref, w_ref, srow_ref, scol_ref, own_ref, sp_ref, kt_ref, of_ref, lse_ref,
    do_ref, q16_ref, do16_ref, o16_ref, lse16_ref,
    dp_ref, dq16_ref, *refs,
):
    total = sp_ref.shape[0]
    tile = own_ref.shape[1]
    blocks = total // tile
    dh_refs, (dos_scr, acc_scr, acc16_scr, dps_scr) = refs[:blocks], refs[blocks:]

    places = jnp.concatenate([srow_ref[b] for b in range(blocks)], axis=1)

    @pl.loop(0, blocks)
    def _(b):
        r = rows(b, tile)
        pick = jnp.where(places == iota((tile, total), 0) + b * tile, 1.0, 0.0).astype(BF)
        dos_scr[r, :] = dot(pick, do_ref[...]).astype(BF)
        acc_scr[r, :] = jnp.zeros((tile, 256), F32)

    own = own_ref[...]
    own_start = doc_starts(own, ends_ref)
    q16 = q16_ref[...]
    do16 = do16_ref[...]
    both = jnp.concatenate([q16, do16], axis=0)
    delta16 = jnp.sum((do16.astype(F32) * o16_ref[...]).T, axis=0, keepdims=True)
    lse16 = lse16_ref[...]

    def step16(kb, dq):
        kr = rows(kb, tile)
        kv = sp_ref[kr, 384:512]
        kpos = iota((tile, tile), 0) + kb * tile
        ok = (kpos <= own) & (kpos >= own_start)
        p = jnp.where(ok, jnp.exp(dot_nt(kv, q16) * 0.125 - lse16), 0.0)
        ds = (p * (dot_nt(kv, do16) - delta16)).astype(BF)
        acc16_scr[kr, :] = dot(jnp.concatenate([ds, p.astype(BF)], axis=1), both)
        return dq + dot_tn(ds, kv)

    def query_block(qb, dq16):
        dq16 = step16(qb, dq16)
        qr = rows(qb, tile)
        q = sp_ref[qr, 0:128]
        do = dos_scr[qr, :]
        qs = [only_head(q, 0), only_head(q, 1)]
        ds_ = [only_head(do, 0), only_head(do, 1)]
        q_two = jnp.concatenate(qs, axis=0)
        do_two = jnp.concatenate(ds_, axis=0)
        prod = (do.astype(F32) * of_ref[qr, :]).T
        delta = [jnp.sum(prod[:HEAD], axis=0, keepdims=True), jnp.sum(prod[HEAD:], axis=0, keepdims=True)]
        lse = lse_ref[qb]
        qpos = iota((1, tile), 1) + qb * tile
        qstart = doc_starts(qpos, ends_ref)
        low = first_block(qb, tile, ends_ref)

        def step(kb, dqt):
            kr = rows(kb, tile)
            k = sp_ref[kr, 128:256]
            v = sp_ref[kr, 256:384]
            kpos = iota((tile, tile), 0) + kb * tile
            ok = (kpos <= qpos) & (kpos >= qstart)
            ps, dss, new = [], [], []
            for head in range(2):
                s = dot_nt(k, qs[head]) * 0.125 - lse[head:head + 1]
                p = jnp.where(ok, jnp.exp(s), 0.0)
                dprob = dot_nt(v, ds_[head])
                ds = (p * (dprob - delta[head])).astype(BF)
                ps.append(p.astype(BF))
                dss.append(ds)
                new.append(dqt[head] + dot(kt_ref[kb, head * HEAD:(head + 1) * HEAD, :], ds))
            acc_scr[kr, 0:128] += dot(jnp.concatenate(dss, axis=1), q_two)
            acc_scr[kr, 128:256] += dot(jnp.concatenate(ps, axis=1), do_two)
            return tuple(new)

        zero = jnp.zeros((HEAD, tile), F32)
        dqt = lax.fori_loop(low, qb, step, step(qb, (zero, zero)))
        dps_scr[qr, 0:128] = (jnp.concatenate(dqt, axis=0).T * 0.125).astype(BF)
        return dq16

    dq16 = lax.fori_loop(0, blocks, query_block, jnp.zeros((tile, 128), F32))
    dq16 = (dq16 * 0.125).astype(BF)
    dq16_ref[...] = dq16

    @pl.loop(0, blocks)
    def _(b):
        r = rows(b, tile)
        dps_scr[r, 128:256] = (acc_scr[r, 0:128] * 0.125).astype(BF)
        dps_scr[r, 256:384] = acc_scr[r, 128:256].astype(BF)
        part = acc16_scr[r, :]
        dps_scr[r, 384:512] = jnp.where(iota(part.shape, 1) < HEAD, part * 0.125, part).astype(BF)

    for b in range(blocks):
        r = slice(b * tile, (b + 1) * tile)
        pick = jnp.where(scol_ref[r, :] == iota((tile, total), 1), 1.0, 0.0).astype(BF)
        dp = dot(pick, dps_scr[...]).astype(BF)
        dp_ref[r, :] = dp
        dh = dot_nt(dp, w_ref[:, :512])
        if b == 0:
            dh = dh + dot_nt(only_head(dq16, 0), w_ref[:, 512:640])
        dh_refs[b][...] = dh[:, :dh_refs[b].shape[1]].astype(BF)


def norm_stats(values):
    centre = values - jnp.mean(values, axis=-1, keepdims=True)
    spread = jnp.mean(centre * centre, axis=-1, keepdims=True)
    rate = lax.rsqrt(spread + 1e-05)
    return centre * rate, rate


def norm_back(grad, normed, rate, gain):
    scaled = grad * gain
    inner = jnp.mean(scaled * normed, axis=-1, keepdims=True)
    back = rate * (scaled - jnp.mean(scaled, axis=-1, keepdims=True) - normed * inner)
    return back, jnp.sum(grad * normed, axis=0, keepdims=True), jnp.sum(grad, axis=0, keepdims=True)


def put(ref, values):
    width = values.shape[1]
    ref[:, :width] = values
    ref[:, width:] = jnp.zeros((ref.shape[0], ref.shape[1] - width), ref.dtype)


def first_norm_kernel(tok_ref, slot_ref, gain_ref, bias_ref, h_ref):
    tile, feats = tok_ref.shape
    normed, _ = norm_stats(tok_ref[...].astype(F32))
    h_ref[:, :feats] = (normed * gain_ref[0:1] + bias_ref[0:1]).astype(BF)
    width = h_ref.shape[1] - feats
    slot = slot_ref[...]
    high = lax.shift_right_logical(slot, 6)
    lanes = iota((tile, width), 1)
    pair = jnp.where(lanes == 0, high, jnp.where(lanes == 1, slot - high * 64, 0))
    h_ref[:, feats:] = pair.astype(F32).astype(BF)


def slab(feats, n_shard, shard):
    mine = feats // HEAD // n_shard * HEAD
    spare = n_shard * mine
    left = feats - spare
    return [
        (shard * mine, mine), (feats + shard * mine, mine), (2 * feats + shard * mine, mine),
        (feats + spare, left), (2 * feats + spare, left), (spare, left),
    ]


def slab_part(feats, n_shard, shard, low, high):
    found, at = [], 0
    for start, width in slab(feats, n_shard, shard):
        first, end = max(at, low), min(at + width, high)
        if first < end:
            found.append((start + first - at, end - first, first - low))
        at = at + width
    return found


def in_width(feats, n_shard):
    return sum(width for _, width in slab(feats, n_shard, 0)) // 4


def pack_in_kernel(spot_ref, w_ref, out_w_ref, out_ref):
    feats = w_ref.shape[1] // 3
    n_shard = out_ref.shape[0]
    wide, out_wide = in_width(feats, n_shard), feats // 4
    for c in range(4):
        @pl.when(spot_ref[2] == c)
        def _(c=c):
            for s in range(n_shard):
                for column, width, place in slab_part(feats, n_shard, s, c * wide, (c + 1) * wide):
                    out_ref[s, :, place:place + width] = w_ref[:, column:column + width]
                out_ref[s, :, wide:wide + out_wide] = out_w_ref[:, c * out_wide:(c + 1) * out_wide]
                out_ref[s, :, wide + out_wide:] = jnp.zeros_like(out_ref[s, :, wide + out_wide:])


def pack_ff_kernel(n_shard, spot_ref, up_ref, down_ref, bias_ref, out_ref, own_bias_ref):
    feats = down_ref.shape[1]
    quarter = down_ref.shape[0] // 4
    aligned = -(-feats // 128) * 128
    out_ref[...] = jnp.zeros_like(out_ref)
    for c in range(4):
        r = (c % 2) * 2 + c // 2

        @pl.when(spot_ref[2] == c)
        def _(c=c, r=r):
            for s in range(n_shard):
                at = (s * 4 + r) * quarter
                out_ref[:, s * quarter:(s + 1) * quarter] = up_ref[:, at:at + quarter]
                own_bias_ref[:, s * quarter:(s + 1) * quarter] = bias_ref[:, at:at + quarter]
            out_ref[:, aligned:aligned + feats] = down_ref[r * quarter:(r + 1) * quarter, :]


def middle_kernel(
    spot_ref, o_ref, o16_ref, wa_ref, wb_ref, tok_ref, gain_ref, bias_ref,
    h_ref, middle_ref, attended_ref, w_ref,
):
    n_shard, tile, mine = o_ref.shape
    feats = tok_ref.shape[1]
    wide, first = feats // 4, in_width(feats, n_shard)
    for s in range(n_shard):
        attended_ref[:, s * mine:(s + 1) * mine] = o_ref[s]
    attended_ref[:, n_shard * mine:] = o16_ref[:, HEAD:].astype(BF)
    for c in range(4):
        @pl.when(spot_ref[2] == c)
        def _(c=c):
            for n, (ref, at) in enumerate(((wa_ref, 0), (wa_ref, 1), (wb_ref, 0), (wb_ref, 1))):
                place = c ^ n
                w_ref[:, place * wide:(place + 1) * wide] = ref[at, :, first:first + wide]
    middle = tok_ref[...].astype(F32) + (dot(attended_ref[...], w_ref[...]) + bias_ref[3:4])
    middle_ref[...] = middle
    normed, _ = norm_stats(middle)
    put(h_ref, (normed * gain_ref[1:2] + bias_ref[4:5]).astype(BF))


def by_corner(spot_ref, full_ref, wide, keep_a, keep_b, send_ref):
    for c in range(4):
        @pl.when(spot_ref[2] == c)
        def _(c=c):
            for n in range(4):
                p = c ^ n
                part = full_ref[:, p * wide:(p + 1) * wide]
                if n < 2:
                    put((keep_a, keep_b)[n], part)
                else:
                    put(send_ref.at[n - 2], part.astype(BF))


def middle_back_kernel(
    spot_ref, kept_ref, core_ref, far_ref, middle_ref, w_ref, cot_ref, attended_ref, gain_ref,
    dmiddle_ref, do_ref, do16_ref, keep_a, keep_b, send_ref, sums_ref, full_scr,
):
    n_shard, tile, mine = do_ref.shape
    feats = middle_ref.shape[1]
    dh = (kept_ref[...] + core_ref[...].astype(F32) + far_ref[...].astype(F32))[:, :feats]
    normed, rate = norm_stats(middle_ref[...])
    dout = cot_ref[:, :feats].astype(F32)
    back, gain_sum, bias_sum = norm_back(dh, normed, rate, gain_ref[1:2])
    dmiddle = dout + back
    dmiddle_ref[...] = dmiddle
    dbranch = dmiddle.astype(BF)
    dattended = dot_nt(dbranch, w_ref[...]).astype(BF)
    for s in range(n_shard):
        do_ref[s] = dattended[:, s * mine:(s + 1) * mine]
    last = dattended[:, n_shard * mine:]
    do16_ref[...] = jnp.concatenate([jnp.zeros_like(last), last], axis=1)
    full_scr[...] = dot_tn(attended_ref[...], dbranch)
    by_corner(spot_ref, full_scr, feats // 4, keep_a, keep_b, send_ref)
    sums_ref[0:1] = jnp.sum(dbranch.astype(F32), axis=0, keepdims=True)
    sums_ref[1:2] = bias_sum
    sums_ref[2:3] = jnp.sum(dout, axis=0, keepdims=True)
    sums_ref[3:4] = gain_sum


def last_kernel(kept_ref, y_ref, a_ref, b_ref, dmiddle_ref, tok_ref, gain_ref, out_ref, sums_ref):
    dh = kept_ref[...].astype(F32) + y_ref[...].astype(F32) + a_ref[...].astype(F32) + b_ref[...].astype(F32)
    dh = dh[:, :tok_ref.shape[1]]
    normed, rate = norm_stats(tok_ref[...].astype(F32))
    back, gain_sum, bias_sum = norm_back(dh, normed, rate, gain_ref[0:1])
    out_ref[...] = dmiddle_ref[...] + back
    sums_ref[0:1] = bias_sum
    sums_ref[1:2] = gain_sum


def feed_forward_kernel(
    h_a, h_b, h_c, g_a, g_b, g_c, w_ref, bias_ref,
    act_ref, dpre_ref, keep_a, keep_b, send_ref, sum_ref,
):
    tile, aligned = h_a.shape
    units, feats = act_ref.shape[1], w_ref.shape[0]
    total = jnp.zeros((1, units), F32)
    sources = ((h_a, g_a, None), (h_b, g_b, None), (h_c, g_c, 0), (h_c, g_c, 1))
    for n, (h_ref, g_ref, at) in enumerate(sources):
        h = h_ref[:, :feats] if at is None else h_ref[at, :, :feats]
        g = g_ref[:, :feats] if at is None else g_ref[at, :, :feats]
        r = slice(n * tile, (n + 1) * tile)
        pre = dot(h, w_ref[:, :units]) + bias_ref[...]
        dact = dot_nt(g, w_ref[:, aligned:aligned + feats])
        square = pre * pre
        root = 0.7978845608028654
        flat = jnp.tanh(root * pre * (1.0 + 0.044715 * square))
        half = 0.5 * (1.0 + flat)
        act_ref[r, :] = (pre * half).astype(BF)
        slope = half + 0.5 * pre * (1.0 - flat * flat) * root * (1.0 + 0.134145 * square)
        dpre = (dact * slope).astype(BF)
        dpre_ref[r, :] = dpre
        total = total + jnp.sum(dpre.astype(F32), axis=0, keepdims=True)
        dh = dot_nt(dpre, w_ref[:, :units])
        if n < 2:
            put((keep_a, keep_b)[n], dh)
        else:
            put(send_ref.at[n - 2], dh.astype(BF))
    sum_ref[...] = total


def feed_grads_kernel(
    h_a, h_b, h_c, g_a, g_b, g_c, w_ref, act_ref, dpre_ref,
    keep_a, keep_b, send_ref, grad_ref, h_scr, g_scr,
):
    tile, aligned = h_a.shape
    units, feats = act_ref.shape[1], w_ref.shape[0]
    down = w_ref[:, aligned:aligned + feats]
    sources = ((h_a, g_a, None), (h_b, g_b, None), (h_c, g_c, 0), (h_c, g_c, 1))
    for n, (h_ref, g_ref, at) in enumerate(sources):
        r = slice(n * tile, (n + 1) * tile)
        h_scr[r, :] = h_ref[:, :feats] if at is None else h_ref[at, :, :feats]
        g_scr[r, :] = g_ref[:, :feats] if at is None else g_ref[at, :, :feats]
    step = 256
    for at in range(0, units, step):
        c = slice(at, min(at + step, units))
        grad_ref[:, c] = dot_tn(h_scr[...], dpre_ref[:, c]).astype(BF)
    for at in range(0, feats, step):
        end = min(at + step, feats)
        part = dot_tn(act_ref[...], g_scr[:, at:end])
        grad_ref[:, aligned + at:aligned + end] = part.astype(BF)
    blank = jnp.zeros((grad_ref.shape[0], aligned - feats), BF)
    grad_ref[:, units:aligned] = blank
    grad_ref[:, aligned + feats:] = blank
    for n in range(4):
        mixed = dot(act_ref[n * tile:(n + 1) * tile, :], down)
        if n < 2:
            put((keep_a, keep_b)[n], mixed)
        else:
            put(send_ref.at[n - 2], mixed.astype(BF))


def in_grad_kernel(blocks, spot_ref, *refs):
    h_refs, (dp_ref, dq16_ref, keep_a, keep_b, send_ref, full_scr) = refs[:blocks], refs[blocks:]
    tile = dq16_ref.shape[0]
    feats = keep_a.shape[0]
    for at in range(0, 512, 256):
        acc = dot_tn(h_refs[0][:, :feats], dp_ref[:tile, at:at + 256])
        for b in range(1, blocks):
            acc = acc + dot_tn(h_refs[b][:, :feats], dp_ref[b * tile:(b + 1) * tile, at:at + 256])
        full_scr[:, at:at + 256] = acc
    full_scr[:, 512:576] = dot_tn(h_refs[0][:, :feats], dq16_ref[...])[:, :HEAD]
    by_corner(spot_ref, full_scr, in_width(feats, blocks), keep_a, keep_b, send_ref)


def join_kernel(wide, out_wide, a_ref, b_ref, c_ref, out_a_ref, out_b_ref, out_c_ref, to_ref):
    to_ref[...] = jnp.zeros_like(to_ref)
    part = a_ref[...] + b_ref[...].astype(F32) + c_ref[...].astype(F32)
    to_ref[:, :wide] = part[:, :wide].astype(BF)
    part = out_a_ref[...] + out_b_ref[...].astype(F32) + out_c_ref[...].astype(F32)
    to_ref[:, wide:wide + out_wide] = part[:, :out_wide].astype(BF)


def fold_kernel(wide, out_wide, in_ref, out_ref):
    n_shard = in_ref.shape[0]
    for s in range(n_shard):
        out_ref[:, s * wide:(s + 1) * wide] = in_ref[s, :, :wide]
    total = in_ref[0, :, wide:wide + out_wide].astype(F32)
    for s in range(1, n_shard):
        total = total + in_ref[s, :, wide:wide + out_wide].astype(F32)
    out_ref[:, n_shard * wide:n_shard * wide + out_wide] = total.astype(BF)
    out_ref[:, n_shard * wide + out_wide:] = jnp.zeros_like(out_ref[:, n_shard * wide + out_wide:])


def owned_kernel(n_shard, spot_ref, a_ref, b_ref, c_ref, up_ref, down_ref):
    quarter, feats = a_ref.shape[0], down_ref.shape[1]
    aligned = -(-feats // 128) * 128
    for c in range(4):
        @pl.when(spot_ref[2] == c)
        def _(c=c):
            for n, (ref, at) in enumerate(((a_ref, None), (b_ref, None), (c_ref, 0), (c_ref, 1))):
                place = c ^ n
                r = (place % 2) * 2 + place // 2
                part = ref[...] if at is None else ref[at]
                for s in range(n_shard):
                    to = (s * 4 + r) * quarter
                    up_ref[:, to:to + quarter] = part[:, s * quarter:(s + 1) * quarter].astype(F32)
                down_ref[r * quarter:(r + 1) * quarter, :] = part[:, aligned:aligned + feats].astype(F32)


def owned_in_kernel(n_shard, spot_ref, a_ref, b_ref, c_ref, out_ref, out_w_ref):
    feats = out_ref.shape[1] // 3
    wide, out_wide = in_width(feats, n_shard), feats // 4
    shared = 3 * (feats // HEAD // n_shard * HEAD)
    for c in range(4):
        @pl.when(spot_ref[2] == c)
        def _(c=c):
            for n, (ref, at) in enumerate(((a_ref, None), (b_ref, None), (c_ref, 0), (c_ref, 1))):
                place = c ^ n
                low = place * wide

                def block(s):
                    lanes = slice(s * wide, (s + 1) * wide)
                    return (ref[:, lanes] if at is None else ref[at, :, lanes]).astype(F32)

                lanes = slice(n_shard * wide, n_shard * wide + out_wide)
                part = ref[:, lanes] if at is None else ref[at, :, lanes]
                out_w_ref[:, place * out_wide:(place + 1) * out_wide] = part.astype(F32)
                for s in range(n_shard):
                    for column, width, to in slab_part(feats, n_shard, s, low, min(low + wide, shared)):
                        out_ref[:, column:column + width] = block(s)[:, to:to + width]
                if low + wide > shared:
                    total = block(0)
                    for s in range(1, n_shard):
                        total = total + block(s)
                    first = max(low, shared)
                    for column, width, to in slab_part(feats, n_shard, 0, first, low + wide):
                        to = to + first - low
                        out_ref[:, column:column + width] = total[:, to:to + width]


VM = pl.BlockSpec(memory_space=pltpu.VMEM)
SM = pl.BlockSpec(memory_space=pltpu.SMEM)


def run(kernel, outs, operands, scalars=0, scratch=(), size=58, flops=0.0):
    moved = sum(v.size * v.dtype.itemsize for v in operands)
    moved = moved + sum(math.prod(shape) * jnp.dtype(kind).itemsize for shape, kind in outs)
    return pl.pallas_call(
        kernel,
        out_shape=tuple(jax.ShapeDtypeStruct(shape, kind) for shape, kind in outs),
        in_specs=[SM] * scalars + [VM] * (len(operands) - scalars),
        out_specs=tuple([VM] * len(outs)),
        scratch_shapes=[pltpu.VMEM(shape, kind) for shape, kind in scratch],
        compiler_params=pltpu.CompilerParams(vmem_limit_bytes=size * 2**20),
        cost_estimate=pl.CostEstimate(flops=int(flops), bytes_accessed=int(moved), transcendentals=0),
    )(*operands)


def swap(values, axis):
    return lax.ppermute(values, axis, [(0, 1), (1, 0)])


def gather_rep(values):
    other = swap(values, "x")
    return values, other, swap(jnp.stack([values, other]), "core")


def scatter_rep(keep_a, keep_b, send):
    across = swap(send, "core")
    return keep_a, across[0], swap((keep_b + across[1].astype(F32)).astype(BF), "x")


def shift(values, step):
    size = lax.axis_size("z")
    return lax.ppermute(values, "z", [(n, (n + step) % size) for n in range(size)])


def together(*values):
    return lax.optimization_barrier(values)


def ring_gather(values, beside):
    size = lax.axis_size("z")
    column = [values] + [None] * (size - 1)
    other = [None] * size
    arrived, last = [(0, values)], {1: values, -1: values}
    for n in range(1, size // 2 + 2):
        places, moving = [], []
        for place, block in arrived:
            places.append((other, place))
            moving.append(swap(block, "y"))
        arrived = []
        if n <= size // 2:
            steps = (1, -1) if size - n > n else (1,)
            for step in steps:
                places.append((column, n if step == 1 else size - n))
                moving.append(shift(last[step], step))
        moving = beside(n, moving)
        for (target, place), block in zip(places, moving):
            target[place] = block
            if target is column:
                arrived.append((place, block))
                last[1 if place == n else -1] = block
    return [block for pair in zip(column, other) for block in pair]


def ring_scatter(parts, beside):
    size = lax.axis_size("z")
    kept, sent = parts[0::2], parts[1::2]
    half = size // 2
    joined, running = {}, {1: None, -1: None}
    wanted = [[half] + ([size - half + 1] if size - half + 1 < size else [])]
    wanted += [[n] + ([size - n + 1] if size - n + 1 < size else []) for n in range(half - 1, 0, -1)]
    wanted += [[0]]
    for index, now in enumerate(wanted + [[]]):
        moving = [swap(sent[n], "y") for n in now]
        steps = []
        if index > 0:
            n = half + 1 - index
            for step, place in ((-1, n), (1, size - n)):
                if n >= 1 and (step == -1 or size - n > n):
                    total = joined[place]
                    if running[step] is not None:
                        total = total + running[step].astype(F32)
                    steps.append(step)
                    moving.append(shift(total.astype(BF), step))
        if not moving:
            continue
        moving = beside(index + 1, moving)
        for n, block in zip(now, moving):
            joined[n] = block if n == 0 else kept[n].astype(F32) + block.astype(F32)
        for step, block in zip(steps, moving[len(now):]):
            running[step] = block
    return kept[0], joined[0], running[-1], running[1]


def sum_dp(values):
    if lax.axis_size("dp") > 1:
        return lax.psum(values, "dp")
    return values


def sum_all(values, beside):
    others = [shift(values, n) for n in range(1, lax.axis_size("z"))]
    for other in beside(1, others):
        values = values + other
    for n, axis in enumerate(("y", "core", "x")):
        (other,) = beside(n + 2, [swap(values, axis)])
        values = values + other
    return sum_dp(values)


def gather_shard(values):
    return lax.all_gather(values, SHARD, axis=0, tiled=True)


def scatter_shard(values):
    return lax.psum_scatter(values.astype(BF), SHARD, scatter_dimension=0, tiled=True)


def exchange_shard(values):
    return lax.all_to_all(values, SHARD, 0, 0, tiled=True)


def shards(
    tokens, slot, lengths, attn_in_weight, attn_out_weight, up_weight, down_weight,
    norm_gains, layer_biases, up_bias, cotangent,
):
    tile, feats = tokens.shape
    zs = lax.axis_size("z")
    n_shard = zs * 2
    total = n_shard * tile
    mine = feats // HEAD // n_shard * HEAD
    spare = n_shard * mine
    z, y = lax.axis_index("z"), lax.axis_index("y")
    me = z * 2 + y
    rep = lax.axis_index("x") * 2 + lax.axis_index("core")
    corner = lax.axis_index("core") * 2 + lax.axis_index("x")
    spot = jnp.stack([z, y, corner]).astype(jnp.int32)
    row_part = attn_in_weight.shape[0]
    ff_part = down_weight.shape[0]
    n_rep = 4
    quarter = ff_part // n_rep
    units = n_shard * quarter
    aligned = -(-feats // 128) * 128
    in_wide = in_width(feats, n_shard)
    out_wide = feats // n_rep
    both_wide = -(-(in_wide + out_wide) // 128) * 128
    in_full = -(-in_wide // 128) * 128
    out_full = -(-out_wide // 128) * 128
    both_wide = -(-(in_wide + out_wide) // 128) * 128
    fold_wide = -(-(n_shard * in_wide + out_wide) // 128) * 128

    ends = jnp.cumsum(lengths[0]).astype(jnp.int32)
    (h_first,) = run(
        first_norm_kernel, [((tile, aligned), BF)], (tokens, slot.reshape(tile, 1), norm_gains, layer_biases)
    )

    (in_pack,) = run(
        pack_in_kernel, [((n_shard, row_part, both_wide), BF)], (spot, attn_in_weight, attn_out_weight), 1
    )
    ff_pack, up_bias_mine = run(
        functools.partial(pack_ff_kernel, n_shard),
        [((row_part, 2 * aligned), BF), ((1, units), F32)],
        (spot, up_weight, down_weight, up_bias.reshape(1, -1)), 1,
    )
    held = dict(
        in_own=exchange_shard(in_pack).reshape(feats, both_wide),
        dout=jnp.pad(cotangent, ((0, 0), (0, aligned - feats))),
        ff_pack=ff_pack,
    )

    held["w_all"] = gather_shard(ff_pack)

    def beside_gather(n, moving):
        names = []
        if n == 1:
            held["dout_far"] = swap(held["dout"], "x")
            names = ["in_own", "dout", "dout_far"]
        elif n == 2:
            held["in_far"] = swap(held["in_own"], "x")
            names = ["in_own", "in_far", "dout", "dout_far"]
        elif n == 3:
            held["in_a"] = jnp.stack([held["in_own"], held["in_far"]])
            held["in_b"] = swap(held["in_a"], "core")
            held["g_core"] = swap(jnp.stack([held["dout"], held["dout_far"]]), "core")
            names = ["in_a", "in_b", "dout", "dout_far", "g_core"]
        *moving, = together(*moving, *[held[name] for name in names])
        for name in reversed(names):
            held[name] = moving.pop()
        return moving

    h_parts = ring_gather(h_first, beside_gather)
    w_all, in_a, in_b = held["w_all"], held["in_a"], held["in_b"]
    dout, g_rep = held["dout"], (held["dout"], held["dout_far"], held["g_core"])
    (sp, kt, o_own, of, lse, q16, o16, lse16, w_own, slot_rows, slot_columns) = run(
        functools.partial(forward_kernel, n_shard),
        [
            ((total, 512), BF), ((n_shard, 128, tile), BF), ((n_shard, tile, 128), BF), ((total, 128), F32),
            ((n_shard, 2, tile), F32), ((tile, 128), BF), ((tile, 128), F32), ((1, tile), F32),
            ((aligned, 640), BF), ((n_shard, 1, tile), jnp.int32), ((total, 1), jnp.int32),
        ],
        (ends, spot, *h_parts, in_a, in_b, layer_biases, slot.reshape(1, tile)), 2,
        scratch=[((total, 640), BF), ((n_shard, 256, tile), BF), ((total, 128), BF), ((1, total), jnp.int32)],
        size=58, flops=30e9,
    )
    o_back = exchange_shard(o_own)
    h_second, middle, attended, w_out = run(
        middle_kernel,
        [((tile, aligned), BF), ((tile, feats), F32), ((tile, feats), BF), ((feats, feats), BF)],
        (spot, o_back, o16, in_a, in_b, tokens, norm_gains, layer_biases), 1, flops=2e9,
    )

    h_rep = gather_rep(h_second)
    whole, one, pair = (n_rep * tile, units), (tile, aligned), (2, tile, aligned)
    act, dpre, *dh_terms, up_bias_grad = run(
        feed_forward_kernel,
        [(whole, BF), (whole, BF), (one, F32), (one, F32), (pair, BF), ((1, units), F32)],
        (*h_rep, *g_rep, w_all, up_bias_mine), flops=10e9,
    )
    kept, joined, send = dh_terms
    across = swap(send, "core")
    joined, act, dpre = together((joined + across[1].astype(F32)).astype(BF), act, dpre)
    *mixed_terms, ff_grads = run(
        feed_grads_kernel,
        [(one, F32), (one, F32), (pair, BF), ((feats, 2 * aligned), BF)],
        (*h_rep, *g_rep, w_all, act, dpre),
        scratch=[((n_rep * tile, feats), BF)] * 2, size=58, flops=10e9,
    )
    far, ff_grads = together(swap(joined, "x"), ff_grads)
    ff_owned = sum_dp(scatter_shard(ff_grads))
    dh_terms = (kept, across[0], far)
    dmiddle, do_all, do16, *out_terms, sums = run(
        middle_back_kernel,
        [
            ((tile, feats), F32), ((n_shard, tile, mine), BF), ((tile, 128), BF),
            ((feats, out_full), F32), ((feats, out_full), F32), ((2, feats, out_full), BF), ((4, feats), F32),
        ],
        (spot, *dh_terms, middle, w_out, dout, attended, norm_gains), 1,
        scratch=[((feats, feats), F32)], flops=3e9,
    )

    out_terms = scatter_rep(*out_terms)
    do_own, *out_terms = together(exchange_shard(do_all).reshape(total, mine), *out_terms)
    dp, dq16, *dh_parts = run(
        backward_kernel,
        [((total, 512), BF), ((tile, 128), BF)] + [((tile, aligned), BF)] * n_shard,
        (
            ends, w_own, slot_rows, slot_columns, slot.reshape(1, tile),
            sp, kt, of, lse, do_own, q16, do16, o16, lse16,
        ),
        1,
        scratch=[((total, 128), BF), ((total, 256), F32), ((total, 128), F32), ((total, 512), BF)],
        size=58, flops=30e9,
    )
    in_kept, in_joined, in_send = run(
        functools.partial(in_grad_kernel, n_shard),
        [((feats, in_full), F32), ((feats, in_full), F32), ((2, feats, in_full), BF)],
        (spot, *h_parts, dp, dq16), 1, scratch=[((feats, 576), F32)], flops=3e9,
    )

    def beside_scatter(n, moving):
        if n == 2:
            held["across"] = swap(in_send, "core")
            far = swap((in_joined + held["across"][1].astype(F32)).astype(BF), "x")
            *moving, held["far"] = together(*moving, far)
        elif n == 3:
            (grad,) = run(
                functools.partial(join_kernel, in_wide, out_wide),
                [((feats, both_wide), BF)],
                (in_kept, held["across"][0], held["far"], *out_terms),
            )
            in_back = exchange_shard(grad.reshape(n_shard, row_part, both_wide))
            ff_far = swap(ff_owned, "x")
            kept, joined, send = mixed_terms
            across = swap(send, "core")
            far = swap((joined + across[1].astype(F32)).astype(BF), "x")
            *moving, held["in_back"], held["ff"], held["ff_far"], far = together(
                *moving, in_back, ff_owned, ff_far, far
            )
            parts = kept + across[0].astype(F32) + far.astype(F32)
            held["mixed"] = (middle + parts[:, :feats] + layer_biases[5]).astype(BF)
        return moving

    dh_first = ring_scatter(dh_parts, beside_scatter)
    (in_back,) = run(
        functools.partial(fold_kernel, in_wide, out_wide), [((row_part, fold_wide), BF)], (held["in_back"],)
    )
    *dh_first, in_back = together(*dh_first, sum_dp(in_back))

    def beside_sum(n, moving):
        if n == 1:
            ff_core = swap(jnp.stack([held["ff"], held["ff_far"]]), "core")
            *moving, held["in_far"], held["ff_core"] = together(*moving, swap(in_back, "x"), ff_core)
        elif n == 2:
            in_core = swap(jnp.stack([in_back, held["in_far"]]), "core")
            up_out, down_out = run(
                functools.partial(owned_kernel, n_shard),
                [((row_part, up_weight.shape[1]), F32), ((ff_part, feats), F32)],
                (spot, held["ff"], held["ff_far"], held["ff_core"]), 1,
            )
            *moving, held["in_core"], held["up"], held["down"] = together(*moving, in_core, up_out, down_out)
        elif n == 4:
            in_out, out_out = run(
                functools.partial(owned_in_kernel, n_shard),
                [((row_part, 3 * feats), F32), ((row_part, feats), F32)],
                (spot, in_back, held["in_far"], held["in_core"]), 1,
            )
            *moving, held["in"], held["out"] = together(*moving, in_out, out_out)
        return moving

    tokens_grad, first_sums = run(
        last_kernel, [((tile, feats), F32), ((2, feats), F32)], (*dh_first, dmiddle, tokens, norm_gains)
    )

    zeros = functools.partial(jnp.zeros, dtype=F32)
    dp_sums = jnp.sum(dp.astype(F32), axis=0)
    query_sums = lax.dynamic_update_slice(zeros(feats), dp_sums[:mine], (me * mine,))
    query_sums = query_sums + jnp.pad(jnp.sum(dq16[:, :HEAD].astype(F32), axis=0), (spare, 0))
    value_sums = lax.dynamic_update_slice(zeros(feats), dp_sums[2 * mine : 3 * mine], (me * mine,))
    value_sums = value_sums + jnp.pad(dp_sums[3 * mine + HEAD : 3 * mine + 2 * HEAD], (spare, 0))
    place = (jnp.arange(n_rep) == rep)[:, None]
    vectors = jnp.concatenate(
        [
            first_sums[0:1], jnp.stack([query_sums, value_sums]), sums[0:3], first_sums[1:2], sums[3:4],
            jnp.where(place, up_bias_grad, 0.0),
        ]
    )
    vectors = lax.dynamic_slice_in_dim(sum_all(vectors, beside_sum), me * row_part, row_part, 1)

    return (
        held["mixed"], tokens_grad, held["in"], held["out"], held["up"], held["down"],
        vectors[6:8], vectors[0:6], vectors[8:].reshape(-1),
    )


def solution(mesh):
    replicas, n_shard = mesh.shape["replica"], mesh.shape["shard"]
    fine = Mesh(
        mesh.devices.reshape(replicas // 4, 2, 2, n_shard // 2, 2), ("dp", "x", "core", "z", "y")
    )
    rep = ("dp", "x", "core")
    both = rep + SHARD
    in_specs = (
        P(both, None), P(both), P(rep, None), P(SHARD, None), P(SHARD, None), P(SHARD, None), P(SHARD, None),
        P(), P(), P(), P(both, None),
    )
    out_specs = (
        P(both, None), P(both, None), P(SHARD, None), P(SHARD, None), P(SHARD, None), P(SHARD, None),
        P(None, SHARD), P(None, SHARD), P(SHARD),
    )
    return jax.shard_map(shards, mesh=fine, in_specs=in_specs, out_specs=out_specs, check_vma=False)
```

```python
import functools
import math

import jax
import jax.numpy as jnp
from jax import lax
from jax.experimental import pallas as pl
from jax.experimental.pallas import tpu as pltpu
from jax.sharding import Mesh, PartitionSpec as P

HEAD = 64
BF = jnp.bfloat16
F32 = jnp.float32
REP = ("x", "core")
SHARD = ("z", "y")
NEG = -1e30


def dot(left, right):
    return jnp.dot(left, right, preferred_element_type=F32)


def dot_nt(left, right):
    return lax.dot_general(left, right, (((1,), (1,)), ((), ())), preferred_element_type=F32)


def dot_tn(left, right):
    return lax.dot_general(left, right, (((0,), (0,)), ((), ())), preferred_element_type=F32)


def iota(shape, dim):
    return lax.broadcasted_iota(jnp.int32, shape, dim)


def doc_starts(places, ends_ref):
    starts = jnp.zeros_like(places)
    for n in range(ends_ref.shape[0]):
        starts = jnp.where(places >= ends_ref[n], ends_ref[n], starts)
    return starts


def first_block(block, tile, ends_ref):
    row = block * tile
    start = jnp.int32(0)
    for n in range(ends_ref.shape[0]):
        start = jnp.where(row >= ends_ref[n], ends_ref[n], start)
    return lax.div(start, jnp.int32(tile))


def rows(block, tile):
    return pl.ds(pl.multiple_of(block * tile, tile), tile)


def only_head(values, head):
    lanes = iota(values.shape, 1)
    keep = (lanes < HEAD) if head == 0 else (lanes >= HEAD)
    return jnp.where(keep, values, jnp.zeros_like(values))


def tail_slots(tail):
    lanes = iota(tail.shape, 1)
    spare = tail.shape[1] // 2
    weight = jnp.where(lanes == spare, 64.0, jnp.where(lanes == spare + 1, 1.0, 0.0))
    return tail.astype(F32) * weight


def forward_kernel(blocks, ends_ref, spot_ref, *refs):
    h_refs, refs = refs[:blocks], refs[blocks:]
    (
        wa_ref, wb_ref, bias_ref, own_ref,
        sp_ref, kt_ref, o_ref, of_ref, lse_ref, q16_ref, o16_ref, lse16_ref, w_ref, srow_ref, scol_ref,
        p_scr, vt_scr, ob_scr, row_scr,
    ) = refs
    tile = own_ref.shape[1]
    total = blocks * tile
    feats = wa_ref.shape[1]
    wide = in_width(feats, blocks)
    z, y, corner = spot_ref[0], spot_ref[1], spot_ref[2]
    zs = blocks // 2

    w_ref[...] = jnp.zeros_like(w_ref)
    for c in range(4):
        @pl.when(corner == c)
        def _(c=c):
            for n, (ref, at) in enumerate(((wa_ref, 0), (wa_ref, 1), (wb_ref, 0), (wb_ref, 1))):
                place = c ^ n
                w_ref[:feats, place * wide:(place + 1) * wide] = ref[at, :, :wide]

    me = z * 2 + y
    lanes = pl.ds(pl.multiple_of(me * 128, 128), 128)
    blank = jnp.zeros((1, 128), F32)
    last = bias_ref.shape[1] - HEAD
    bias = jnp.concatenate(
        [
            bias_ref[1:2, lanes], blank, bias_ref[2:3, lanes],
            blank[:, :HEAD], bias_ref[2:3, last:], bias_ref[1:2, last:], blank[:, :HEAD],
        ],
        axis=1,
    )
    for b in range(blocks):
        r = slice(b * tile, (b + 1) * tile)
        p_scr[r, :] = (dot(h_refs[b][...], w_ref[...]) + bias).astype(BF)
        tail = tail_slots(h_refs[b][:, h_refs[b].shape[1] - 128:])
        scol_ref[r, :] = jnp.sum(tail, axis=1, keepdims=True).astype(jnp.int32)
        row = jnp.sum(tail.T, axis=0, keepdims=True).astype(jnp.int32)
        row_scr[:, r] = row
        shard = lax.rem(z + zs - b // 2, zs) * 2 + lax.rem(y + b % 2, 2)
        srow_ref[shard] = row

    @pl.loop(0, blocks)
    def _(b):
        r = rows(b, tile)
        place = iota((tile, total), 0) + b * tile
        pick = jnp.where(row_scr[...] == place, 1.0, 0.0).astype(BF)
        sorted_f = dot(pick, p_scr[:, :512])
        sp_ref[r, :] = sorted_f.astype(BF)
        kt_ref[b] = sorted_f[:, 128:256].T.astype(BF)
        vt_scr[b, :128, :] = sorted_f[:, 256:384].T.astype(BF)
        vt_scr[b, 128:, :] = sorted_f[:, 384:512].T.astype(BF)

    q16 = p_scr[0:tile, 512:640]
    q16_ref[...] = q16

    own = own_ref[...]
    own_start = doc_starts(own, ends_ref)

    def step16(kb, state):
        m, l, acc = state
        kv = sp_ref[rows(kb, tile), 384:512]
        kpos = iota((tile, tile), 0) + kb * tile
        ok = (kpos <= own) & (kpos >= own_start)
        s = jnp.where(ok, dot_nt(kv, q16) * 0.125, NEG)
        mn = jnp.maximum(m, jnp.max(s, axis=0, keepdims=True))
        p = jnp.where(ok, jnp.exp(s - mn), 0.0)
        a = jnp.exp(m - mn)
        l = l * a + jnp.sum(p, axis=0, keepdims=True)
        acc = acc * a + dot(vt_scr[kb, 192:256, :], p.astype(BF))
        return mn, l, acc

    def query_block(qb, state16):
        state16 = step16(qb, state16)
        q = sp_ref[rows(qb, tile), 0:128]
        qs = [only_head(q, 0), only_head(q, 1)]
        qpos = iota((1, tile), 1) + qb * tile
        qstart = doc_starts(qpos, ends_ref)
        low = first_block(qb, tile, ends_ref)

        def step(n, state):
            kb = qb - n
            k = sp_ref[rows(kb, tile), 128:256]
            kpos = iota((tile, tile), 0) + kb * tile
            ok = (kpos <= qpos) & (kpos >= qstart)
            new = []
            for head in range(2):
                m, l, acc = state[head]
                s = jnp.where(ok, dot_nt(k, qs[head]) * 0.125, NEG)
                mn = jnp.maximum(m, jnp.max(s, axis=0, keepdims=True))
                p = jnp.exp(s - mn)
                a = jnp.exp(m - mn)
                l = l * a + jnp.sum(p, axis=0, keepdims=True)
                vt = vt_scr[kb, head * HEAD:(head + 1) * HEAD, :]
                acc = acc * a + dot(vt, p.astype(BF))
                new.append((mn, l, acc))
            return tuple(new)

        state = step(0, (start, start))
        state = lax.fori_loop(1, qb - low + 1, step, state)
        out = jnp.concatenate([state[0][2] / state[0][1], state[1][2] / state[1][1]], axis=0).T
        of_ref[rows(qb, tile), :] = out
        ob_scr[rows(qb, tile), :] = out.astype(BF)
        lse_ref[qb] = jnp.concatenate([s[0] + jnp.log(s[1]) for s in state], axis=0)
        return state16

    start = (jnp.full((1, tile), NEG, F32), jnp.zeros((1, tile), F32), jnp.zeros((HEAD, tile), F32))
    m, l, acc = lax.fori_loop(0, blocks, query_block, start)
    o16_ref[...] = jnp.concatenate([jnp.zeros_like(acc), acc / l], axis=0).T
    lse16_ref[...] = m + jnp.log(l)

    for b in range(blocks):
        pick = jnp.where(scol_ref[b * tile:(b + 1) * tile, :] == iota((tile, total), 1), 1.0, 0.0).astype(BF)
        shard = lax.rem(z + zs - b // 2, zs) * 2 + lax.rem(y + b % 2, 2)
        o_ref[shard] = dot(pick, ob_scr[...]).astype(BF)


def backward_kernel(
    ends_ref, w_ref, srow_ref, scol_ref, own_ref, sp_ref, kt_ref, of_ref, lse_ref,
    do_ref, q16_ref, do16_ref, o16_ref, lse16_ref,
    dp_ref, dq16_ref, *refs,
):
    total = sp_ref.shape[0]
    tile = own_ref.shape[1]
    blocks = total // tile
    dh_refs, (dos_scr, acc_scr, acc16_scr, dps_scr) = refs[:blocks], refs[blocks:]

    places = jnp.concatenate([srow_ref[b] for b in range(blocks)], axis=1)

    @pl.loop(0, blocks)
    def _(b):
        r = rows(b, tile)
        pick = jnp.where(places == iota((tile, total), 0) + b * tile, 1.0, 0.0).astype(BF)
        dos_scr[r, :] = dot(pick, do_ref[...]).astype(BF)
        acc_scr[r, :] = jnp.zeros((tile, 256), F32)

    own = own_ref[...]
    own_start = doc_starts(own, ends_ref)
    q16 = q16_ref[...]
    do16 = do16_ref[...]
    both = jnp.concatenate([q16, do16], axis=0)
    delta16 = jnp.sum((do16.astype(F32) * o16_ref[...]).T, axis=0, keepdims=True)
    lse16 = lse16_ref[...]

    def step16(kb, dq):
        kr = rows(kb, tile)
        kv = sp_ref[kr, 384:512]
        kpos = iota((tile, tile), 0) + kb * tile
        ok = (kpos <= own) & (kpos >= own_start)
        p = jnp.where(ok, jnp.exp(dot_nt(kv, q16) * 0.125 - lse16), 0.0)
        ds = (p * (dot_nt(kv, do16) - delta16)).astype(BF)
        acc16_scr[kr, :] = dot(jnp.concatenate([ds, p.astype(BF)], axis=1), both)
        return dq + dot_tn(ds, kv)

    def query_block(qb, dq16):
        dq16 = step16(qb, dq16)
        qr = rows(qb, tile)
        q = sp_ref[qr, 0:128]
        do = dos_scr[qr, :]
        qs = [only_head(q, 0), only_head(q, 1)]
        ds_ = [only_head(do, 0), only_head(do, 1)]
        q_two = jnp.concatenate(qs, axis=0)
        do_two = jnp.concatenate(ds_, axis=0)
        prod = (do.astype(F32) * of_ref[qr, :]).T
        delta = [jnp.sum(prod[:HEAD], axis=0, keepdims=True), jnp.sum(prod[HEAD:], axis=0, keepdims=True)]
        lse = lse_ref[qb]
        qpos = iota((1, tile), 1) + qb * tile
        qstart = doc_starts(qpos, ends_ref)
        low = first_block(qb, tile, ends_ref)

        def step(kb, dqt):
            kr = rows(kb, tile)
            k = sp_ref[kr, 128:256]
            v = sp_ref[kr, 256:384]
            kpos = iota((tile, tile), 0) + kb * tile
            ok = (kpos <= qpos) & (kpos >= qstart)
            ps, dss, new = [], [], []
            for head in range(2):
                s = dot_nt(k, qs[head]) * 0.125 - lse[head:head + 1]
                p = jnp.where(ok, jnp.exp(s), 0.0)
                dprob = dot_nt(v, ds_[head])
                ds = (p * (dprob - delta[head])).astype(BF)
                ps.append(p.astype(BF))
                dss.append(ds)
                new.append(dqt[head] + dot(kt_ref[kb, head * HEAD:(head + 1) * HEAD, :], ds))
            acc_scr[kr, 0:128] += dot(jnp.concatenate(dss, axis=1), q_two)
            acc_scr[kr, 128:256] += dot(jnp.concatenate(ps, axis=1), do_two)
            return tuple(new)

        zero = jnp.zeros((HEAD, tile), F32)
        dqt = lax.fori_loop(low, qb, step, step(qb, (zero, zero)))
        dps_scr[qr, 0:128] = (jnp.concatenate(dqt, axis=0).T * 0.125).astype(BF)
        return dq16

    dq16 = lax.fori_loop(0, blocks, query_block, jnp.zeros((tile, 128), F32))
    dq16 = (dq16 * 0.125).astype(BF)
    dq16_ref[...] = dq16

    @pl.loop(0, blocks)
    def _(b):
        r = rows(b, tile)
        dps_scr[r, 128:256] = (acc_scr[r, 0:128] * 0.125).astype(BF)
        dps_scr[r, 256:384] = acc_scr[r, 128:256].astype(BF)
        part = acc16_scr[r, :]
        dps_scr[r, 384:512] = jnp.where(iota(part.shape, 1) < HEAD, part * 0.125, part).astype(BF)

    for b in range(blocks):
        r = slice(b * tile, (b + 1) * tile)
        pick = jnp.where(scol_ref[r, :] == iota((tile, total), 1), 1.0, 0.0).astype(BF)
        dp = dot(pick, dps_scr[...]).astype(BF)
        dp_ref[r, :] = dp
        dh = dot_nt(dp, w_ref[:, :512])
        if b == 0:
            dh = dh + dot_nt(only_head(dq16, 0), w_ref[:, 512:640])
        dh_refs[b][...] = dh[:, :dh_refs[b].shape[1]].astype(BF)


def norm_stats(values):
    centre = values - jnp.mean(values, axis=-1, keepdims=True)
    spread = jnp.mean(centre * centre, axis=-1, keepdims=True)
    rate = lax.rsqrt(spread + 1e-05)
    return centre * rate, rate


def norm_back(grad, normed, rate, gain):
    scaled = grad * gain
    inner = jnp.mean(scaled * normed, axis=-1, keepdims=True)
    back = rate * (scaled - jnp.mean(scaled, axis=-1, keepdims=True) - normed * inner)
    return back, jnp.sum(grad * normed, axis=0, keepdims=True), jnp.sum(grad, axis=0, keepdims=True)


def put(ref, values):
    width = values.shape[1]
    ref[:, :width] = values
    ref[:, width:] = jnp.zeros((ref.shape[0], ref.shape[1] - width), ref.dtype)


def first_norm_kernel(tok_ref, slot_ref, gain_ref, bias_ref, h_ref):
    tile, feats = tok_ref.shape
    normed, _ = norm_stats(tok_ref[...].astype(F32))
    h_ref[:, :feats] = (normed * gain_ref[0:1] + bias_ref[0:1]).astype(BF)
    width = h_ref.shape[1] - feats
    slot = slot_ref[...]
    high = lax.shift_right_logical(slot, 6)
    lanes = iota((tile, width), 1)
    pair = jnp.where(lanes == 0, high, jnp.where(lanes == 1, slot - high * 64, 0))
    h_ref[:, feats:] = pair.astype(F32).astype(BF)


def slab(feats, n_shard, shard):
    mine = feats // HEAD // n_shard * HEAD
    spare = n_shard * mine
    left = feats - spare
    return [
        (shard * mine, mine), (feats + shard * mine, mine), (2 * feats + shard * mine, mine),
        (feats + spare, left), (2 * feats + spare, left), (spare, left),
    ]


def slab_part(feats, n_shard, shard, low, high):
    found, at = [], 0
    for start, width in slab(feats, n_shard, shard):
        first, end = max(at, low), min(at + width, high)
        if first < end:
            found.append((start + first - at, end - first, first - low))
        at = at + width
    return found


def in_width(feats, n_shard):
    return sum(width for _, width in slab(feats, n_shard, 0)) // 4


def pack_in_kernel(spot_ref, w_ref, out_w_ref, out_ref):
    feats = w_ref.shape[1] // 3
    n_shard = out_ref.shape[0]
    wide, out_wide = in_width(feats, n_shard), feats // 4
    for c in range(4):
        @pl.when(spot_ref[2] == c)
        def _(c=c):
            for s in range(n_shard):
                for column, width, place in slab_part(feats, n_shard, s, c * wide, (c + 1) * wide):
                    out_ref[s, :, place:place + width] = w_ref[:, column:column + width]
                out_ref[s, :, wide:wide + out_wide] = out_w_ref[:, c * out_wide:(c + 1) * out_wide]
                out_ref[s, :, wide + out_wide:] = jnp.zeros_like(out_ref[s, :, wide + out_wide:])


def pack_ff_kernel(n_shard, spot_ref, up_ref, down_ref, bias_ref, out_ref, own_bias_ref):
    feats = down_ref.shape[1]
    quarter = down_ref.shape[0] // 4
    aligned = -(-feats // 128) * 128
    out_ref[...] = jnp.zeros_like(out_ref)
    for c in range(4):
        r = (c % 2) * 2 + c // 2

        @pl.when(spot_ref[2] == c)
        def _(c=c, r=r):
            for s in range(n_shard):
                at = (s * 4 + r) * quarter
                out_ref[:, s * quarter:(s + 1) * quarter] = up_ref[:, at:at + quarter]
                own_bias_ref[:, s * quarter:(s + 1) * quarter] = bias_ref[:, at:at + quarter]
            out_ref[:, aligned:aligned + feats] = down_ref[r * quarter:(r + 1) * quarter, :]


def middle_kernel(
    spot_ref, o_ref, o16_ref, wa_ref, wb_ref, tok_ref, gain_ref, bias_ref,
    h_ref, middle_ref, attended_ref, w_ref,
):
    n_shard, tile, mine = o_ref.shape
    feats = tok_ref.shape[1]
    wide, first = feats // 4, in_width(feats, n_shard)
    for s in range(n_shard):
        attended_ref[:, s * mine:(s + 1) * mine] = o_ref[s]
    attended_ref[:, n_shard * mine:] = o16_ref[:, HEAD:].astype(BF)
    for c in range(4):
        @pl.when(spot_ref[2] == c)
        def _(c=c):
            for n, (ref, at) in enumerate(((wa_ref, 0), (wa_ref, 1), (wb_ref, 0), (wb_ref, 1))):
                place = c ^ n
                w_ref[:, place * wide:(place + 1) * wide] = ref[at, :, first:first + wide]
    middle = tok_ref[...].astype(F32) + (dot(attended_ref[...], w_ref[...]) + bias_ref[3:4])
    middle_ref[...] = middle
    normed, _ = norm_stats(middle)
    put(h_ref, (normed * gain_ref[1:2] + bias_ref[4:5]).astype(BF))


def by_corner(spot_ref, full_ref, wide, keep_a, keep_b, send_ref):
    for c in range(4):
        @pl.when(spot_ref[2] == c)
        def _(c=c):
            for n in range(4):
                p = c ^ n
                part = full_ref[:, p * wide:(p + 1) * wide]
                if n < 2:
                    put((keep_a, keep_b)[n], part)
                else:
                    put(send_ref.at[n - 2], part.astype(BF))


def middle_back_kernel(
    spot_ref, kept_ref, core_ref, far_ref, middle_ref, w_ref, cot_ref, attended_ref, gain_ref,
    dmiddle_ref, do_ref, do16_ref, keep_a, keep_b, send_ref, sums_ref, full_scr,
):
    n_shard, tile, mine = do_ref.shape
    feats = middle_ref.shape[1]
    dh = (kept_ref[...] + core_ref[...].astype(F32) + far_ref[...].astype(F32))[:, :feats]
    normed, rate = norm_stats(middle_ref[...])
    dout = cot_ref[:, :feats].astype(F32)
    back, gain_sum, bias_sum = norm_back(dh, normed, rate, gain_ref[1:2])
    dmiddle = dout + back
    dmiddle_ref[...] = dmiddle
    dbranch = dmiddle.astype(BF)
    dattended = dot_nt(dbranch, w_ref[...]).astype(BF)
    for s in range(n_shard):
        do_ref[s] = dattended[:, s * mine:(s + 1) * mine]
    last = dattended[:, n_shard * mine:]
    do16_ref[...] = jnp.concatenate([jnp.zeros_like(last), last], axis=1)
    full_scr[...] = dot_tn(attended_ref[...], dbranch)
    by_corner(spot_ref, full_scr, feats // 4, keep_a, keep_b, send_ref)
    sums_ref[0:1] = jnp.sum(dbranch.astype(F32), axis=0, keepdims=True)
    sums_ref[1:2] = bias_sum
    sums_ref[2:3] = jnp.sum(dout, axis=0, keepdims=True)
    sums_ref[3:4] = gain_sum


def last_kernel(kept_ref, y_ref, a_ref, b_ref, dmiddle_ref, tok_ref, gain_ref, out_ref, sums_ref):
    dh = kept_ref[...].astype(F32) + y_ref[...].astype(F32) + a_ref[...].astype(F32) + b_ref[...].astype(F32)
    dh = dh[:, :tok_ref.shape[1]]
    normed, rate = norm_stats(tok_ref[...].astype(F32))
    back, gain_sum, bias_sum = norm_back(dh, normed, rate, gain_ref[0:1])
    out_ref[...] = dmiddle_ref[...] + back
    sums_ref[0:1] = bias_sum
    sums_ref[1:2] = gain_sum


def feed_forward_kernel(
    h_a, h_b, h_c, h_d, g_a, g_b, g_c, w_ref, bias_ref,
    act_ref, dpre_ref, keep_a, keep_b, send_ref, sum_ref,
):
    tile, aligned = h_a.shape
    units, feats = act_ref.shape[1], w_ref.shape[0]
    total = jnp.zeros((1, units), F32)
    sources = ((h_a, g_a, None), (h_b, g_b, None), (h_c, g_c, 0), (h_d, g_c, 1))
    for n, (h_ref, g_ref, at) in enumerate(sources):
        h = h_ref[:, :feats]
        g = g_ref[:, :feats] if at is None else g_ref[at, :, :feats]
        r = slice(n * tile, (n + 1) * tile)
        pre = dot(h, w_ref[:, :units]) + bias_ref[...]
        dact = dot_nt(g, w_ref[:, aligned:aligned + feats])
        square = pre * pre
        root = 0.7978845608028654
        flat = jnp.tanh(root * pre * (1.0 + 0.044715 * square))
        half = 0.5 * (1.0 + flat)
        act_ref[r, :] = (pre * half).astype(BF)
        slope = half + 0.5 * pre * (1.0 - flat * flat) * root * (1.0 + 0.134145 * square)
        dpre = (dact * slope).astype(BF)
        dpre_ref[r, :] = dpre
        total = total + jnp.sum(dpre.astype(F32), axis=0, keepdims=True)
        dh = dot_nt(dpre, w_ref[:, :units])
        if n < 2:
            put((keep_a, keep_b)[n], dh)
        else:
            put(send_ref.at[n - 2], dh.astype(BF))
    sum_ref[...] = total


def feed_grads_kernel(
    h_a, h_b, h_c, h_d, g_a, g_b, g_c, w_ref, act_ref, dpre_ref,
    keep_a, keep_b, send_ref, grad_ref, h_scr, g_scr,
):
    tile, aligned = h_a.shape
    units, feats = act_ref.shape[1], w_ref.shape[0]
    down = w_ref[:, aligned:aligned + feats]
    sources = ((h_a, g_a, None), (h_b, g_b, None), (h_c, g_c, 0), (h_d, g_c, 1))
    for n, (h_ref, g_ref, at) in enumerate(sources):
        r = slice(n * tile, (n + 1) * tile)
        h_scr[r, :] = h_ref[:, :feats]
        g_scr[r, :] = g_ref[:, :feats] if at is None else g_ref[at, :, :feats]
    step = 256
    for at in range(0, units, step):
        c = slice(at, min(at + step, units))
        grad_ref[:, c] = dot_tn(h_scr[...], dpre_ref[:, c]).astype(BF)
    for at in range(0, feats, step):
        end = min(at + step, feats)
        part = dot_tn(act_ref[...], g_scr[:, at:end])
        grad_ref[:, aligned + at:aligned + end] = part.astype(BF)
    blank = jnp.zeros((grad_ref.shape[0], aligned - feats), BF)
    grad_ref[:, units:aligned] = blank
    grad_ref[:, aligned + feats:] = blank
    for n in range(4):
        mixed = dot(act_ref[n * tile:(n + 1) * tile, :], down)
        if n < 2:
            put((keep_a, keep_b)[n], mixed)
        else:
            put(send_ref.at[n - 2], mixed.astype(BF))


def in_grad_kernel(blocks, spot_ref, *refs):
    h_refs, (dp_ref, dq16_ref, keep_a, keep_b, send_ref, full_scr) = refs[:blocks], refs[blocks:]
    tile = dq16_ref.shape[0]
    feats = keep_a.shape[0]
    for at in range(0, 512, 256):
        acc = dot_tn(h_refs[0][:, :feats], dp_ref[:tile, at:at + 256])
        for b in range(1, blocks):
            acc = acc + dot_tn(h_refs[b][:, :feats], dp_ref[b * tile:(b + 1) * tile, at:at + 256])
        full_scr[:, at:at + 256] = acc
    full_scr[:, 512:576] = dot_tn(h_refs[0][:, :feats], dq16_ref[...])[:, :HEAD]
    by_corner(spot_ref, full_scr, in_width(feats, blocks), keep_a, keep_b, send_ref)


def join_kernel(wide, out_wide, a_ref, b_ref, c_ref, out_a_ref, out_b_ref, out_c_ref, to_ref):
    to_ref[...] = jnp.zeros_like(to_ref)
    part = a_ref[...] + b_ref[...].astype(F32) + c_ref[...].astype(F32)
    to_ref[:, :wide] = part[:, :wide].astype(BF)
    part = out_a_ref[...] + out_b_ref[...].astype(F32) + out_c_ref[...].astype(F32)
    to_ref[:, wide:wide + out_wide] = part[:, :out_wide].astype(BF)


def fold_kernel(wide, out_wide, in_ref, out_ref):
    n_shard = in_ref.shape[0]
    for s in range(n_shard):
        out_ref[:, s * wide:(s + 1) * wide] = in_ref[s, :, :wide]
    total = in_ref[0, :, wide:wide + out_wide].astype(F32)
    for s in range(1, n_shard):
        total = total + in_ref[s, :, wide:wide + out_wide].astype(F32)
    out_ref[:, n_shard * wide:n_shard * wide + out_wide] = total.astype(BF)
    out_ref[:, n_shard * wide + out_wide:] = jnp.zeros_like(out_ref[:, n_shard * wide + out_wide:])


def owned_kernel(n_shard, spot_ref, a_ref, b_ref, c_ref, up_ref, down_ref):
    quarter, feats = a_ref.shape[0], down_ref.shape[1]
    aligned = -(-feats // 128) * 128
    for c in range(4):
        @pl.when(spot_ref[2] == c)
        def _(c=c):
            for n, (ref, at) in enumerate(((a_ref, None), (b_ref, None), (c_ref, 0), (c_ref, 1))):
                place = c ^ n
                r = (place % 2) * 2 + place // 2
                part = ref[...] if at is None else ref[at]
                for s in range(n_shard):
                    to = (s * 4 + r) * quarter
                    up_ref[:, to:to + quarter] = part[:, s * quarter:(s + 1) * quarter].astype(F32)
                down_ref[r * quarter:(r + 1) * quarter, :] = part[:, aligned:aligned + feats].astype(F32)


def owned_in_kernel(n_shard, spot_ref, a_ref, b_ref, c_ref, out_ref, out_w_ref):
    feats = out_ref.shape[1] // 3
    wide, out_wide = in_width(feats, n_shard), feats // 4
    shared = 3 * (feats // HEAD // n_shard * HEAD)
    for c in range(4):
        @pl.when(spot_ref[2] == c)
        def _(c=c):
            for n, (ref, at) in enumerate(((a_ref, None), (b_ref, None), (c_ref, 0), (c_ref, 1))):
                place = c ^ n
                low = place * wide

                def block(s):
                    lanes = slice(s * wide, (s + 1) * wide)
                    return (ref[:, lanes] if at is None else ref[at, :, lanes]).astype(F32)

                lanes = slice(n_shard * wide, n_shard * wide + out_wide)
                part = ref[:, lanes] if at is None else ref[at, :, lanes]
                out_w_ref[:, place * out_wide:(place + 1) * out_wide] = part.astype(F32)
                for s in range(n_shard):
                    for column, width, to in slab_part(feats, n_shard, s, low, min(low + wide, shared)):
                        out_ref[:, column:column + width] = block(s)[:, to:to + width]
                if low + wide > shared:
                    total = block(0)
                    for s in range(1, n_shard):
                        total = total + block(s)
                    first = max(low, shared)
                    for column, width, to in slab_part(feats, n_shard, 0, first, low + wide):
                        to = to + first - low
                        out_ref[:, column:column + width] = total[:, to:to + width]


VM = pl.BlockSpec(memory_space=pltpu.VMEM)
SM = pl.BlockSpec(memory_space=pltpu.SMEM)


def run(kernel, outs, operands, scalars=0, scratch=(), size=58, flops=0.0):
    moved = sum(v.size * v.dtype.itemsize for v in operands)
    moved = moved + sum(math.prod(shape) * jnp.dtype(kind).itemsize for shape, kind in outs)
    return pl.pallas_call(
        kernel,
        out_shape=tuple(jax.ShapeDtypeStruct(shape, kind) for shape, kind in outs),
        in_specs=[SM] * scalars + [VM] * (len(operands) - scalars),
        out_specs=tuple([VM] * len(outs)),
        scratch_shapes=[pltpu.VMEM(shape, kind) for shape, kind in scratch],
        compiler_params=pltpu.CompilerParams(vmem_limit_bytes=size * 2**20),
        cost_estimate=pl.CostEstimate(flops=int(flops), bytes_accessed=int(moved), transcendentals=0),
    )(*operands)


def swap(values, axis):
    return lax.ppermute(values, axis, [(0, 1), (1, 0)])


def gather_rep(values):
    other = swap(values, "x")
    return values, other, swap(values, "core"), swap(other, "core")


def scatter_rep(keep_a, keep_b, send):
    across = swap(send, "core")
    return keep_a, across[0], swap((keep_b + across[1].astype(F32)).astype(BF), "x")


def shift(values, step):
    size = lax.axis_size("z")
    return lax.ppermute(values, "z", [(n, (n + step) % size) for n in range(size)])


def together(*values):
    return lax.optimization_barrier(values)


def ring_gather(values, beside):
    size = lax.axis_size("z")
    column = [values] + [None] * (size - 1)
    other = [None] * size
    arrived, last = [(0, values)], {1: values, -1: values}
    for n in range(1, size // 2 + 2):
        places, moving = [], []
        for place, block in arrived:
            places.append((other, place))
            moving.append(swap(block, "y"))
        arrived = []
        if n <= size // 2:
            steps = (1, -1) if size - n > n else (1,)
            for step in steps:
                places.append((column, n if step == 1 else size - n))
                moving.append(shift(last[step], step))
        moving = beside(n, moving)
        for (target, place), block in zip(places, moving):
            target[place] = block
            if target is column:
                arrived.append((place, block))
                last[1 if place == n else -1] = block
    return [block for pair in zip(column, other) for block in pair]


def ring_scatter(parts, beside):
    size = lax.axis_size("z")
    kept, sent = parts[0::2], parts[1::2]
    half = size // 2
    joined, running = {}, {1: None, -1: None}
    wanted = [[half] + ([size - half + 1] if size - half + 1 < size else [])]
    wanted += [[n] + ([size - n + 1] if size - n + 1 < size else []) for n in range(half - 1, 0, -1)]
    wanted += [[0]]
    for index, now in enumerate(wanted + [[]]):
        moving = [swap(sent[n], "y") for n in now]
        steps = []
        if index > 0:
            n = half + 1 - index
            for step, place in ((-1, n), (1, size - n)):
                if n >= 1 and (step == -1 or size - n > n):
                    total = joined[place]
                    if running[step] is not None:
                        total = total + running[step].astype(F32)
                    steps.append(step)
                    moving.append(shift(total.astype(BF), step))
        if not moving:
            continue
        moving = beside(index + 1, moving)
        for n, block in zip(now, moving):
            joined[n] = block if n == 0 else kept[n].astype(F32) + block.astype(F32)
        for step, block in zip(steps, moving[len(now):]):
            running[step] = block
    return kept[0], joined[0], running[-1], running[1]


def sum_dp(values):
    if lax.axis_size("dp") > 1:
        return lax.psum(values, "dp")
    return values


def sum_all(values, beside):
    others = [shift(values, n) for n in range(1, lax.axis_size("z"))]
    for other in beside(1, others):
        values = values + other
    for n, axis in enumerate(("y", "core", "x")):
        (other,) = beside(n + 2, [swap(values, axis)])
        values = values + other
    return sum_dp(values)


def gather_shard(values):
    return lax.all_gather(values, SHARD, axis=0, tiled=True)


def scatter_shard(values):
    return lax.psum_scatter(values.astype(BF), SHARD, scatter_dimension=0, tiled=True)


def exchange_shard(values):
    return lax.all_to_all(values, SHARD, 0, 0, tiled=True)


def shards(
    tokens, slot, lengths, attn_in_weight, attn_out_weight, up_weight, down_weight,
    norm_gains, layer_biases, up_bias, cotangent,
):
    tile, feats = tokens.shape
    zs = lax.axis_size("z")
    n_shard = zs * 2
    total = n_shard * tile
    mine = feats // HEAD // n_shard * HEAD
    spare = n_shard * mine
    z, y = lax.axis_index("z"), lax.axis_index("y")
    me = z * 2 + y
    rep = lax.axis_index("x") * 2 + lax.axis_index("core")
    corner = lax.axis_index("core") * 2 + lax.axis_index("x")
    spot = jnp.stack([z, y, corner]).astype(jnp.int32)
    row_part = attn_in_weight.shape[0]
    ff_part = down_weight.shape[0]
    n_rep = 4
    quarter = ff_part // n_rep
    units = n_shard * quarter
    aligned = -(-feats // 128) * 128
    in_wide = in_width(feats, n_shard)
    out_wide = feats // n_rep
    both_wide = -(-(in_wide + out_wide) // 128) * 128
    in_full = -(-in_wide // 128) * 128
    out_full = -(-out_wide // 128) * 128
    both_wide = -(-(in_wide + out_wide) // 128) * 128
    fold_wide = -(-(n_shard * in_wide + out_wide) // 128) * 128

    ends = jnp.cumsum(lengths[0]).astype(jnp.int32)
    (h_first,) = run(
        first_norm_kernel, [((tile, aligned), BF)], (tokens, slot.reshape(tile, 1), norm_gains, layer_biases)
    )

    (in_pack,) = run(
        pack_in_kernel, [((n_shard, row_part, both_wide), BF)], (spot, attn_in_weight, attn_out_weight), 1
    )
    ff_pack, up_bias_mine = run(
        functools.partial(pack_ff_kernel, n_shard),
        [((row_part, 2 * aligned), BF), ((1, units), F32)],
        (spot, up_weight, down_weight, up_bias.reshape(1, -1)), 1,
    )
    held = dict(
        in_own=exchange_shard(in_pack).reshape(feats, both_wide),
        dout=jnp.pad(cotangent, ((0, 0), (0, aligned - feats))),
        ff_pack=ff_pack,
    )

    held["w_all"] = gather_shard(ff_pack)

    def beside_gather(n, moving):
        names = []
        if n == 1:
            held["dout_far"] = swap(held["dout"], "x")
            names = ["in_own", "dout", "dout_far"]
        elif n == 2:
            held["in_far"] = swap(held["in_own"], "x")
            names = ["in_own", "in_far", "dout", "dout_far"]
        elif n == 3:
            held["in_a"] = jnp.stack([held["in_own"], held["in_far"]])
            held["in_b"] = swap(held["in_a"], "core")
            held["g_core"] = swap(jnp.stack([held["dout"], held["dout_far"]]), "core")
            names = ["in_a", "in_b", "dout", "dout_far", "g_core"]
        *moving, = together(*moving, *[held[name] for name in names])
        for name in reversed(names):
            held[name] = moving.pop()
        return moving

    h_parts = ring_gather(h_first, beside_gather)
    w_all, in_a, in_b = held["w_all"], held["in_a"], held["in_b"]
    dout, g_rep = held["dout"], (held["dout"], held["dout_far"], held["g_core"])
    (sp, kt, o_own, of, lse, q16, o16, lse16, w_own, slot_rows, slot_columns) = run(
        functools.partial(forward_kernel, n_shard),
        [
            ((total, 512), BF), ((n_shard, 128, tile), BF), ((n_shard, tile, 128), BF), ((total, 128), F32),
            ((n_shard, 2, tile), F32), ((tile, 128), BF), ((tile, 128), F32), ((1, tile), F32),
            ((aligned, 640), BF), ((n_shard, 1, tile), jnp.int32), ((total, 1), jnp.int32),
        ],
        (ends, spot, *h_parts, in_a, in_b, layer_biases, slot.reshape(1, tile)), 2,
        scratch=[((total, 640), BF), ((n_shard, 256, tile), BF), ((total, 128), BF), ((1, total), jnp.int32)],
        size=58, flops=30e9,
    )
    o_back = exchange_shard(o_own)
    h_second, middle, attended, w_out = run(
        middle_kernel,
        [((tile, aligned), BF), ((tile, feats), F32), ((tile, feats), BF), ((feats, feats), BF)],
        (spot, o_back, o16, in_a, in_b, tokens, norm_gains, layer_biases), 1, flops=2e9,
    )

    h_rep = gather_rep(h_second)
    whole, one, pair = (n_rep * tile, units), (tile, aligned), (2, tile, aligned)
    act, dpre, *dh_terms, up_bias_grad = run(
        feed_forward_kernel,
        [(whole, BF), (whole, BF), (one, F32), (one, F32), (pair, BF), ((1, units), F32)],
        (*h_rep, *g_rep, w_all, up_bias_mine), flops=10e9,
    )
    kept, joined, send = dh_terms
    across = swap(send, "core")
    joined, act, dpre = together((joined + across[1].astype(F32)).astype(BF), act, dpre)
    *mixed_terms, ff_grads = run(
        feed_grads_kernel,
        [(one, F32), (one, F32), (pair, BF), ((feats, 2 * aligned), BF)],
        (*h_rep, *g_rep, w_all, act, dpre),
        scratch=[((n_rep * tile, feats), BF)] * 2, size=58, flops=10e9,
    )
    far, ff_grads = together(swap(joined, "x"), ff_grads)
    ff_owned = sum_dp(scatter_shard(ff_grads))
    dh_terms = (kept, across[0], far)
    dmiddle, do_all, do16, *out_terms, sums = run(
        middle_back_kernel,
        [
            ((tile, feats), F32), ((n_shard, tile, mine), BF), ((tile, 128), BF),
            ((feats, out_full), F32), ((feats, out_full), F32), ((2, feats, out_full), BF), ((4, feats), F32),
        ],
        (spot, *dh_terms, middle, w_out, dout, attended, norm_gains), 1,
        scratch=[((feats, feats), F32)], flops=3e9,
    )

    out_terms = scatter_rep(*out_terms)
    do_own, *out_terms = together(exchange_shard(do_all).reshape(total, mine), *out_terms)
    dp, dq16, *dh_parts = run(
        backward_kernel,
        [((total, 512), BF), ((tile, 128), BF)] + [((tile, aligned), BF)] * n_shard,
        (
            ends, w_own, slot_rows, slot_columns, slot.reshape(1, tile),
            sp, kt, of, lse, do_own, q16, do16, o16, lse16,
        ),
        1,
        scratch=[((total, 128), BF), ((total, 256), F32), ((total, 128), F32), ((total, 512), BF)],
        size=58, flops=30e9,
    )
    in_kept, in_joined, in_send = run(
        functools.partial(in_grad_kernel, n_shard),
        [((feats, in_full), F32), ((feats, in_full), F32), ((2, feats, in_full), BF)],
        (spot, *h_parts, dp, dq16), 1, scratch=[((feats, 576), F32)], flops=3e9,
    )

    def beside_scatter(n, moving):
        if n == 2:
            held["across"] = swap(in_send, "core")
            far = swap((in_joined + held["across"][1].astype(F32)).astype(BF), "x")
            *moving, held["far"] = together(*moving, far)
        elif n == 3:
            (grad,) = run(
                functools.partial(join_kernel, in_wide, out_wide),
                [((feats, both_wide), BF)],
                (in_kept, held["across"][0], held["far"], *out_terms),
            )
            in_back = exchange_shard(grad.reshape(n_shard, row_part, both_wide))
            ff_far = swap(ff_owned, "x")
            kept, joined, send = mixed_terms
            across = swap(send, "core")
            far = swap((joined + across[1].astype(F32)).astype(BF), "x")
            *moving, held["in_back"], held["ff"], held["ff_far"], far = together(
                *moving, in_back, ff_owned, ff_far, far
            )
            parts = kept + across[0].astype(F32) + far.astype(F32)
            held["mixed"] = (middle + parts[:, :feats] + layer_biases[5]).astype(BF)
        return moving

    dh_first = ring_scatter(dh_parts, beside_scatter)
    (in_back,) = run(
        functools.partial(fold_kernel, in_wide, out_wide), [((row_part, fold_wide), BF)], (held["in_back"],)
    )
    *dh_first, in_back = together(*dh_first, sum_dp(in_back))

    def beside_sum(n, moving):
        if n == 1:
            ff_core = swap(jnp.stack([held["ff"], held["ff_far"]]), "core")
            *moving, held["in_far"], held["ff_core"] = together(*moving, swap(in_back, "x"), ff_core)
        elif n == 2:
            in_core = swap(jnp.stack([in_back, held["in_far"]]), "core")
            up_out, down_out = run(
                functools.partial(owned_kernel, n_shard),
                [((row_part, up_weight.shape[1]), F32), ((ff_part, feats), F32)],
                (spot, held["ff"], held["ff_far"], held["ff_core"]), 1,
            )
            *moving, held["in_core"], held["up"], held["down"] = together(*moving, in_core, up_out, down_out)
        elif n == 4:
            in_out, out_out = run(
                functools.partial(owned_in_kernel, n_shard),
                [((row_part, 3 * feats), F32), ((row_part, feats), F32)],
                (spot, in_back, held["in_far"], held["in_core"]), 1,
            )
            *moving, held["in"], held["out"] = together(*moving, in_out, out_out)
        return moving

    tokens_grad, first_sums = run(
        last_kernel, [((tile, feats), F32), ((2, feats), F32)], (*dh_first, dmiddle, tokens, norm_gains)
    )

    zeros = functools.partial(jnp.zeros, dtype=F32)
    dp_sums = jnp.sum(dp.astype(F32), axis=0)
    query_sums = lax.dynamic_update_slice(zeros(feats), dp_sums[:mine], (me * mine,))
    query_sums = query_sums + jnp.pad(jnp.sum(dq16[:, :HEAD].astype(F32), axis=0), (spare, 0))
    value_sums = lax.dynamic_update_slice(zeros(feats), dp_sums[2 * mine : 3 * mine], (me * mine,))
    value_sums = value_sums + jnp.pad(dp_sums[3 * mine + HEAD : 3 * mine + 2 * HEAD], (spare, 0))
    place = (jnp.arange(n_rep) == rep)[:, None]
    vectors = jnp.concatenate(
        [
            first_sums[0:1], jnp.stack([query_sums, value_sums]), sums[0:3], first_sums[1:2], sums[3:4],
            jnp.where(place, up_bias_grad, 0.0),
        ]
    )
    vectors = lax.dynamic_slice_in_dim(sum_all(vectors, beside_sum), me * row_part, row_part, 1)

    return (
        held["mixed"], tokens_grad, held["in"], held["out"], held["up"], held["down"],
        vectors[6:8], vectors[0:6], vectors[8:].reshape(-1),
    )


def solution(mesh):
    replicas, n_shard = mesh.shape["replica"], mesh.shape["shard"]
    fine = Mesh(
        mesh.devices.reshape(replicas // 4, 2, 2, n_shard // 2, 2), ("dp", "x", "core", "z", "y")
    )
    rep = ("dp", "x", "core")
    both = rep + SHARD
    in_specs = (
        P(both, None), P(both), P(rep, None), P(SHARD, None), P(SHARD, None), P(SHARD, None), P(SHARD, None),
        P(), P(), P(), P(both, None),
    )
    out_specs = (
        P(both, None), P(both, None), P(SHARD, None), P(SHARD, None), P(SHARD, None), P(SHARD, None),
        P(None, SHARD), P(None, SHARD), P(SHARD),
    )
    return jax.shard_map(shards, mesh=fine, in_specs=in_specs, out_specs=out_specs, check_vma=False)
```
